32 devices in a mesh: seq: 8 (over y, x, core), tensor: 4 (over z).
Axes of the slice: x: 2, y: 2, z: 4, core: 2. Of those that a mesh axis runs over, the one named last changes fastest.
Arguments:
- hidden: bfloat16 [4096, 4096], P('seq', 'tensor'), may hold values from -64 to 64
- depth: int32 [4096], P('seq'), may hold values from 1 to 4, as said below
- norm_gain: float32 [4096], replicated, may hold values from 0.1 to 1.9
- w_query: bfloat16 [4096, 2048], P(None, 'tensor'), may hold values from -1 to 1
- w_key: bfloat16 [4096, 2048], P(None, 'tensor'), may hold values from -12 to 12
- w_value: bfloat16 [4096, 2048], P(None, 'tensor'), may hold values from -0.09375 to 0.09375
- w_out: bfloat16 [2048, 4096], P('tensor'), may hold values from -0.125 to 0.125
Outputs:
- updated: bfloat16 [4096, 4096], P('seq', 'tensor')
The draws below stay inside these ranges and needn't reach their ends.
Inputs may be any that keep to these rules, and one draw needn't show every extreme that they name: A token takes part in recursion two when its depth is 2 or more; exactly half of the 4096 tokens take part, and the share of such tokens differs between blocks of 512 tokens.
All inputs are finite; a program needn't handle non-finite values.
Results may differ from the reference program's by a relative error of at most 0.006.
Values may be sent and summed in bfloat16 or wider, within the bound.
No kernel may reach another device: no remote copies, remote signals or barrier semaphores. Data moves between devices by JAX's collectives and lax.ppermute only.
A program may use at most 128 MiB of HBM per device.

```python
import math
import jax
import jax.numpy as jnp
from jax import lax

D = 4096
HEADS = 16
HEAD = 128
TOK_DEV = 512
TOKENS = 4096


def shared_base(key):
    return jnp.clip(jax.random.normal(key, (D, HEADS * HEAD), jnp.float32), -4.5, 4.5) * math.sqrt(3.0 / D)


def draw_w_query(key, part):
    return shared_base(key).astype(jnp.bfloat16)


def draw_w_key(key, part):
    key = jax.random.fold_in(key, 22)
    fresh = jnp.clip(jax.random.normal(key, (D, HEADS * HEAD), jnp.float32), -4.5, 4.5) * math.sqrt(3.0 / D)
    return fresh.astype(jnp.bfloat16)


def draw_hidden(key, part):
    key = jax.random.fold_in(key, 5)
    first, second = jax.random.split(key)
    column = 0.6 * 3.0 ** (jnp.arange(D, dtype=jnp.float32) / (D - 1))
    base = jnp.clip(jax.random.normal(first, (TOKENS, D), jnp.float32), -6.0, 6.0)
    rowscale = jnp.exp(jax.random.uniform(second, (TOKENS, 1), jnp.float32, -0.35, 0.35))
    return (base * column[None, :] * rowscale).astype(jnp.bfloat16)


def draw_depth(key, part):
    key = jax.random.fold_in(key, 11)
    first, second, third, fourth = jax.random.split(key, 4)
    blocks = TOKENS // TOK_DEV
    pairing = jax.random.permutation(first, blocks)
    low = TOK_DEV // 16
    chosen = jax.random.randint(second, (blocks // 2,), low, TOK_DEV - low + 1)
    counts = jnp.zeros((blocks,), jnp.int32)
    counts = counts.at[pairing[0::2]].set(chosen.astype(jnp.int32))
    counts = counts.at[pairing[1::2]].set((TOK_DEV - chosen).astype(jnp.int32))
    ranks = jax.vmap(lambda k: jax.random.permutation(k, TOK_DEV))(jax.random.split(third, blocks))
    taken = ranks < counts[:, None]
    deep = jax.random.randint(fourth, (blocks, TOK_DEV), 2, 5)
    return jnp.where(taken, deep, 1).reshape(TOKENS).astype(jnp.int32)


def level_of(own_key, extent, cuts, low, high):
    factor_of = 1.0
    for axis_at, shards_of in cuts:
        steps = jax.random.uniform(jax.random.fold_in(jax.random.fold_in(own_key, 6), axis_at), (shards_of,), jnp.float32, low / len(cuts), high / len(cuts))
        factor_of = factor_of * jnp.repeat(jnp.exp(steps), extent[axis_at] // shards_of).reshape((-1,) + (1,) * (len(extent) - 1 - axis_at))
    return factor_of


def noise(key, dims, spread, limit, cuts=(), held_as=jnp.bfloat16):
    array = jax.random.normal(key, dims, jnp.float32) * spread
    if len(cuts) > 0:
        array = level_of(key, dims, cuts, -0.22, 0.18) * array
    return jnp.clip(array, min=-limit, max=limit).astype(held_as)


def setup_inputs(seed: int = 0) -> dict:
    key_of = jax.random.split(jax.random.key(seed), 8)
    hidden = draw_hidden(jax.random.fold_in(key_of[7], 71), 0)
    depth = draw_depth(jax.random.fold_in(key_of[7], 71), 0)
    norm_gain = jnp.clip(1.0 + 0.18 * jax.random.normal(key_of[2], (D,), jnp.float32), 0.1, 1.9)
    w_query = draw_w_query(jax.random.fold_in(key_of[7], 71), 0)
    w_key = draw_w_key(jax.random.fold_in(key_of[7], 71), 0)
    w_value = noise(key_of[5], (D, HEADS * HEAD), D ** -0.5, 0.09375, ((1, 4),))
    w_out = noise(key_of[6], (HEADS * HEAD, D), (HEADS * HEAD) ** -0.5, 0.125, ((0, 4),))
    return {"hidden": hidden, "depth": depth, "norm_gain": norm_gain, "w_query": w_query, "w_key": w_key, "w_value": w_value, "w_out": w_out}


def reference(hidden, depth, norm_gain, w_query, w_key, w_value, w_out):
    heads = w_query.shape[1] // HEAD
    values32 = hidden.astype(jnp.float32)
    mean_sq = lax.optimization_barrier(jnp.mean(values32 * values32, axis=1, keepdims=True))
    normed = (values32 * lax.rsqrt(mean_sq + 1e-05) * norm_gain.astype(jnp.float32)).astype(jnp.bfloat16)
    queries = jnp.dot(normed, w_query, preferred_element_type=jnp.float32).astype(jnp.bfloat16)
    keys = jnp.dot(normed, w_key, preferred_element_type=jnp.float32).astype(jnp.bfloat16)
    values = jnp.dot(normed, w_value, preferred_element_type=jnp.float32).astype(jnp.bfloat16)
    places = jnp.arange(TOKENS, dtype=jnp.int32)
    active = depth >= 2
    key_place = jnp.where(active, places, TOKENS).astype(jnp.int32)
    key_full = keys.astype(jnp.float32).reshape(TOKENS, heads, HEAD)
    value_full = values.astype(jnp.float32).reshape(TOKENS, heads, HEAD)
    block = 256
    scale = 1.0 / math.sqrt(HEAD)
    query_blocks = queries.astype(jnp.float32).reshape(TOKENS // block, block, heads, HEAD)
    place_blocks = places.reshape(TOKENS // block, block)

    def one_block(args):
        query_part, query_place = args
        scores = jnp.einsum('qhd,khd->hqk', query_part, key_full) * scale
        allowed = key_place[None, None, :] <= query_place[None, :, None]
        scores = jnp.where(allowed, scores, -1e+30)
        best = lax.optimization_barrier(jnp.max(scores, axis=2, keepdims=True))
        weights = jnp.exp(scores - best)
        total = lax.optimization_barrier(jnp.sum(weights, axis=2))
        rounded = weights.astype(jnp.bfloat16).astype(jnp.float32)
        summed = jnp.einsum('hqk,khd->qhd', rounded, value_full)
        return summed / jnp.transpose(total)[:, :, None]
    attended = lax.map(one_block, (query_blocks, place_blocks))
    attended = attended.reshape(TOKENS, heads * HEAD).astype(jnp.bfloat16)
    projected = jnp.dot(attended, w_out, preferred_element_type=jnp.float32)
    renewed = (values32 + projected).astype(jnp.bfloat16)
    return jnp.where(active[:, None], renewed, hidden)
```

```python
import math
from functools import partial

import jax
import jax.numpy as jnp
from jax import lax
from jax.experimental import pallas as pl
from jax.experimental.pallas import tpu as pltpu
from jax.sharding import PartitionSpec as P

HEAD = 128
MASKED = -1e30
BACK = 2


def project_kernel(group, x_ref, gain_ref, wq_ref, wk_ref, wv_ref, out_ref, normed):
    @pl.when(pl.program_id(0) == 0)
    def _():
        values = x_ref[...].astype(jnp.float32)
        mean = jnp.mean(values * values, axis=1, keepdims=True)
        normed[...] = (values * lax.rsqrt(mean + 1e-05) * gain_ref[...]).astype(jnp.bfloat16)

    part_rows = out_ref.shape[1]
    heads = wq_ref.shape[1] // HEAD
    for which, weight in enumerate((wq_ref, wk_ref, wv_ref)):
        product = jnp.dot(normed[...], weight[...], preferred_element_type=jnp.float32)
        product = product.astype(jnp.bfloat16)
        for head in range(heads):
            for part in range(group):
                out_ref[head * group + part, :, which * HEAD : (which + 1) * HEAD] = product[
                    part * part_rows : (part + 1) * part_rows, head * HEAD : (head + 1) * HEAD
                ]


def project(x, gain, wq, wk, wv, seq_count, group):
    rows, features = x.shape
    width = wq.shape[1]
    block = min(256, width)
    per_step = block // HEAD * group
    part_rows = rows // group
    weight_spec = pl.BlockSpec((features, block), lambda j: (0, j))
    return pl.pallas_call(
        partial(project_kernel, group),
        grid=(width // block,),
        in_specs=[
            pl.BlockSpec((rows, features), lambda j: (0, 0)),
            pl.BlockSpec((1, features), lambda j: (0, 0)),
            weight_spec,
            weight_spec,
            weight_spec,
        ],
        out_specs=pl.BlockSpec((per_step, part_rows, 3 * HEAD), lambda j: (j, 0, 0)),
        out_shape=jax.ShapeDtypeStruct((seq_count, part_rows, 3 * HEAD), jnp.bfloat16),
        scratch_shapes=[pltpu.VMEM((rows, features), jnp.bfloat16)],
        compiler_params=pltpu.CompilerParams(vmem_limit_bytes=44 * 2**20),
        cost_estimate=pl.CostEstimate(
            flops=6 * rows * features * width,
            bytes_accessed=6 * features * width + 2 * rows * (features + 3 * width),
            transcendentals=0,
        ),
    )(x, gain, wq, wk, wv)


def attend_kernel(chunks, group, mine, part_ref, bias_ref, *refs):
    pieces = refs[: chunks * group]
    out_ref, keys, values = refs[chunks * group :]
    seq_count, part_rows, _ = pieces[0].shape
    rows = bias_ref.shape[1]
    chunk_rows = rows // chunks
    part = part_ref[0]

    def place(home, _):
        for chunk in range(chunks):
            for step in range(group):
                owner = lax.rem(part + step, group)
                at = pl.multiple_of(home * rows + chunk * chunk_rows + owner * part_rows, part_rows)
                piece = pieces[chunk * group + step]
                keys[pl.ds(at, part_rows), :] = piece[home, :, HEAD : 2 * HEAD]
                values[pl.ds(at, part_rows), :] = piece[home, :, 2 * HEAD :]
        return 0

    lax.fori_loop(0, seq_count, place, 0)
    scale = math.log2(math.e) / math.sqrt(HEAD)
    count = len(mine) * part_rows

    def one_home(home, _):
        queries = jnp.concatenate([pieces[c * group][home, :, :HEAD] for c in mine], axis=0)

        def fold(other, carry, diagonal):
            best, total, summed = carry
            at = pl.multiple_of(other * rows, rows)
            scores = lax.dot_general(
                queries,
                keys[pl.ds(at, rows), :],
                (((1,), (1,)), ((), ())),
                preferred_element_type=jnp.float32,
            )
            scores = scores * scale + bias_ref[pl.ds(other, 1), :]
            if diagonal:
                order = lax.broadcasted_iota(jnp.int32, (count, rows), 0)
                place_in = lax.broadcasted_iota(jnp.int32, (count, rows), 1)
                own = order % part_rows + part * part_rows
                for at_chunk, chunk in enumerate(mine):
                    own = jnp.where(order // part_rows == at_chunk, own + chunk * chunk_rows, own)
                scores = jnp.where(place_in <= own, scores, MASKED)
            newbest = jnp.maximum(best, jnp.max(scores, axis=1, keepdims=True))
            factor = jnp.exp2(best - newbest)
            weights = jnp.exp2(scores - newbest)
            total = total * factor + jnp.sum(weights, axis=1, keepdims=True)
            summed = summed * factor + jnp.dot(
                weights.astype(jnp.bfloat16),
                values[pl.ds(at, rows), :],
                preferred_element_type=jnp.float32,
            )
            return newbest, total, summed

        start = (
            jnp.full((count, 1), MASKED, jnp.float32),
            jnp.zeros((count, 1), jnp.float32),
            jnp.zeros((count, HEAD), jnp.float32),
        )
        carry = fold(home, start, True)
        carry = lax.fori_loop(0, home, lambda other, c: fold(other, c, False), carry)
        _, total, summed = carry
        out_ref[home] = (summed / total).astype(jnp.bfloat16)
        return 0

    lax.fori_loop(0, seq_count, one_home, 0)


def attend(part, bias, pieces, chunks, group, mine):
    seq_count, part_rows, _ = pieces[0].shape
    rows = bias.shape[1]
    count = len(mine) * part_rows
    vmem = pl.BlockSpec(memory_space=pltpu.VMEM)
    pairs = seq_count * (seq_count + 1) // 2
    return pl.pallas_call(
        partial(attend_kernel, chunks, group, mine),
        in_specs=[pl.BlockSpec(memory_space=pltpu.SMEM), vmem] + [vmem] * len(pieces),
        out_specs=vmem,
        out_shape=jax.ShapeDtypeStruct((seq_count, count, HEAD), jnp.bfloat16),
        scratch_shapes=[
            pltpu.VMEM((seq_count * rows, HEAD), jnp.bfloat16),
            pltpu.VMEM((seq_count * rows, HEAD), jnp.bfloat16),
        ],
        compiler_params=pltpu.CompilerParams(vmem_limit_bytes=56 * 2**20),
        cost_estimate=pl.CostEstimate(
            flops=4 * pairs * count * rows * HEAD,
            bytes_accessed=8 * seq_count * rows * HEAD,
            transcendentals=pairs * count * rows,
        ),
    )(part, bias, *pieces)


def output_kernel(chunks, group, *refs):
    attended_ref, weight_ref, hidden_ref, active_ref = refs[:4]
    out_ref, rows_in = refs[-2:]
    tensor_count, seq_count, count, _ = attended_ref.shape
    heads = seq_count // group
    part_rows = count // chunks
    chunk_rows = part_rows * group

    @pl.when(pl.program_id(0) == 0)
    def _():
        def place(tensor, _):
            for head in range(heads):
                at = pl.multiple_of((tensor * heads + head) * HEAD, HEAD)
                for part in range(group):
                    for chunk in range(chunks):
                        first = chunk * chunk_rows + part * part_rows
                        rows_in[first : first + part_rows, pl.ds(at, HEAD)] = attended_ref[
                            tensor, head * group + part, chunk * part_rows : (chunk + 1) * part_rows, :
                        ]
            return 0

        lax.fori_loop(0, tensor_count, place, 0)

    shares = jnp.dot(rows_in[...], weight_ref[...], preferred_element_type=jnp.float32)
    hidden = hidden_ref[...]
    renewed = (hidden.astype(jnp.float32) + shares).astype(jnp.bfloat16)
    out_ref[...] = jnp.where(active_ref[...] > 0, renewed, hidden)


def output(attended, weight, hidden, active, so_far, which, parts, chunks, group):
    rows, columns = hidden.shape
    here = rows // parts
    depth = weight.shape[0]
    block = min(256, columns)
    operands = [attended, weight, hidden, active]
    whole = lambda j: (0, 0, 0, 0)
    in_specs = [
        pl.BlockSpec(attended.shape, whole),
        pl.BlockSpec((depth, block), lambda j: (0, j)),
        pl.BlockSpec((here, block), lambda j: (which, j)),
        pl.BlockSpec((here, 1), lambda j: (which, 0)),
    ]
    aliases = {}
    if so_far is not None:
        operands.append(so_far)
        in_specs.append(pl.BlockSpec(memory_space=pl.ANY))
        aliases = {4: 0}
    return pl.pallas_call(
        partial(output_kernel, chunks, group),
        grid=(columns // block,),
        in_specs=in_specs,
        out_specs=pl.BlockSpec((here, block), lambda j: (which, j)),
        out_shape=jax.ShapeDtypeStruct((rows, columns), jnp.bfloat16),
        scratch_shapes=[pltpu.VMEM((here, depth), jnp.bfloat16)],
        input_output_aliases=aliases,
        compiler_params=pltpu.CompilerParams(vmem_limit_bytes=40 * 2**20),
        cost_estimate=pl.CostEstimate(
            flops=2 * here * depth * columns,
            bytes_accessed=2 * (here * depth + depth * columns + 2 * here * columns),
            transcendentals=0,
        ),
    )(*operands)


def output_weight(w_out, seq_count, tensor_count, columns):
    heads = w_out.shape[0] // HEAD
    cuts = seq_count // heads
    width = columns // cuts
    if width % HEAD:
        return lax.all_to_all(w_out, "tensor", split_axis=1, concat_axis=0, tiled=True)
    me = lax.axis_index("seq")
    by_owner = w_out.reshape(w_out.shape[0], tensor_count, columns)
    share = lax.dynamic_slice(
        by_owner, ((me // cuts) * HEAD, 0, (me % cuts) * width), (HEAD, tensor_count, width)
    )
    share = jnp.transpose(share, (1, 0, 2))
    share = lax.all_to_all(share, "tensor", split_axis=0, concat_axis=0)
    whole = lax.all_gather(share, "seq", axis=0)
    whole = whole.reshape(heads, cuts, tensor_count, HEAD, width)
    return jnp.transpose(whole, (2, 0, 3, 1, 4)).reshape(tensor_count * heads * HEAD, columns)


def shards(hidden, depth, norm_gain, w_query, w_key, w_value, w_out):
    rows, columns = hidden.shape
    seq_count = lax.axis_size("seq")
    tensor_count = lax.axis_size("tensor")
    heads = w_query.shape[1] // HEAD
    group = seq_count // heads
    chunks = min(4, rows // (16 * group))
    chunk_rows = rows // chunks
    back = min(BACK, chunks)
    part = (lax.axis_index("seq") % group).astype(jnp.int32).reshape(1)
    gain = norm_gain.reshape(1, -1)

    wholes = [
        lax.all_gather(hidden[c * chunk_rows : (c + 1) * chunk_rows], "tensor", axis=1, tiled=True)
        for c in range(chunks)
    ]
    depths = lax.all_gather(depth, "seq", axis=0)
    bias = jnp.where(depths >= 2, 0.0, MASKED).astype(jnp.float32)
    active = (depth >= 2).astype(jnp.int32).reshape(rows, 1)

    pieces = []
    for whole in wholes:
        sent = project(whole, gain, w_query, w_key, w_value, seq_count, group)
        got = lax.all_to_all(sent, "seq", split_axis=0, concat_axis=0)
        pieces.append(got)
        for step in range(1, group):
            ring = [
                (d, d - d % group + (d - step) % group) for d in range(seq_count)
            ]
            pieces.append(lax.ppermute(got, "seq", ring))

    weight = output_weight(w_out, seq_count, tensor_count, columns)
    updated = None
    each = chunks // back
    for which in range(back):
        mine = tuple(range(which * each, (which + 1) * each))
        out = attend(part, bias, pieces, chunks, group, mine)
        home = lax.all_to_all(out, "seq", split_axis=0, concat_axis=0)
        attended = lax.all_gather(home, "tensor", axis=0)
        updated = output(attended, weight, hidden, active, updated, which, back, each, group)
    return updated


def solution(mesh):
    return jax.shard_map(
        shards,
        mesh=mesh,
        in_specs=(
            P("seq", "tensor"),
            P("seq"),
            P(),
            P(None, "tensor"),
            P(None, "tensor"),
            P(None, "tensor"),
            P("tensor", None),
        ),
        out_specs=P("seq", "tensor"),
        check_vma=False,
    )
```

```python
import math
from functools import partial

import jax
import jax.numpy as jnp
from jax import lax
from jax.experimental import pallas as pl
from jax.experimental.pallas import tpu as pltpu
from jax.sharding import PartitionSpec as P

HEAD = 128
MASKED = -1e30
BACK = 2
LIMIT = 60 * 2**20


def sources(me, count):
    found = [(me, None)]
    for step in range(count - 1):
        found.append((me - 1 - step, me - 1 - step >= 0))
        found.append((me + 1 + step, me + 1 + step < count))
    return found


def line_gather(chunks, count):
    right = [(d, d + 1) for d in range(count - 1)]
    left = [(d + 1, d) for d in range(count - 1)]
    found = [[chunk] for chunk in chunks]
    last = [(chunk, chunk) for chunk in chunks]
    for step in range(count - 1):
        for at, (from_left, from_right) in enumerate(last):
            from_left = lax.ppermute(from_left, "tensor", right[step:])
            from_right = lax.ppermute(from_right, "tensor", left[: count - 1 - step])
            last[at] = (from_left, from_right)
            found[at] += [from_left, from_right]
    return found


def project_kernel(group, count, me_ref, gain_ref, wq_ref, wk_ref, wv_ref, *refs):
    pieces = refs[:-3]
    out_ref, raw, normed = refs[-3:]
    width = pieces[0].shape[1]

    @pl.when(pl.program_id(0) == 0)
    def _():
        for piece, (source, there) in zip(pieces, sources(me_ref[0], count)):
            def place(piece=piece, source=source):
                raw[:, pl.ds(pl.multiple_of(source * width, width), width)] = piece[...]

            if there is None:
                place()
            else:
                pl.when(there)(place)
        values = raw[...].astype(jnp.float32)
        mean = jnp.mean(values * values, axis=1, keepdims=True)
        normed[...] = (values * lax.rsqrt(mean + 1e-05) * gain_ref[...]).astype(jnp.bfloat16)

    part_rows = out_ref.shape[1]
    heads = wq_ref.shape[1] // HEAD
    for which, weight in enumerate((wq_ref, wk_ref, wv_ref)):
        product = jnp.dot(normed[...], weight[...], preferred_element_type=jnp.float32)
        product = product.astype(jnp.bfloat16)
        for head in range(heads):
            for part in range(group):
                out_ref[head * group + part, :, which * HEAD : (which + 1) * HEAD] = product[
                    part * part_rows : (part + 1) * part_rows, head * HEAD : (head + 1) * HEAD
                ]


def project(me, pieces, gain, wq, wk, wv, seq_count, group):
    rows, columns = pieces[0].shape
    features, width = wq.shape
    block = min(256, width)
    per_step = block // HEAD * group
    part_rows = rows // group
    weight_spec = pl.BlockSpec((features, block), lambda j: (0, j))
    return pl.pallas_call(
        partial(project_kernel, group, features // columns),
        grid=(width // block,),
        in_specs=[
            pl.BlockSpec(memory_space=pltpu.SMEM),
            pl.BlockSpec((1, features), lambda j: (0, 0)),
            weight_spec,
            weight_spec,
            weight_spec,
        ]
        + [pl.BlockSpec((rows, columns), lambda j: (0, 0))] * len(pieces),
        out_specs=pl.BlockSpec((per_step, part_rows, 3 * HEAD), lambda j: (j, 0, 0)),
        out_shape=jax.ShapeDtypeStruct((seq_count, part_rows, 3 * HEAD), jnp.bfloat16),
        scratch_shapes=[
            pltpu.VMEM((rows, features), jnp.bfloat16),
            pltpu.VMEM((rows, features), jnp.bfloat16),
        ],
        compiler_params=pltpu.CompilerParams(vmem_limit_bytes=LIMIT),
        cost_estimate=pl.CostEstimate(
            flops=6 * rows * features * width,
            bytes_accessed=6 * features * width + 2 * rows * (features + 3 * width),
            transcendentals=0,
        ),
    )(me, gain, wq, wk, wv, *pieces)


def attend_kernel(chunks, group, mine, part_ref, bias_ref, *refs):
    pieces = refs[: chunks * group]
    out_ref, keys, values = refs[chunks * group :]
    seq_count, part_rows, _ = pieces[0].shape
    rows = bias_ref.shape[1]
    chunk_rows = rows // chunks
    part = part_ref[0]

    def place(home, _):
        for chunk in range(chunks):
            for step in range(group):
                owner = lax.rem(part + step, group)
                at = pl.multiple_of(home * rows + chunk * chunk_rows + owner * part_rows, part_rows)
                piece = pieces[chunk * group + step]
                keys[pl.ds(at, part_rows), :] = piece[home, :, HEAD : 2 * HEAD]
                values[pl.ds(at, part_rows), :] = piece[home, :, 2 * HEAD :]
        return 0

    lax.fori_loop(0, seq_count, place, 0)
    scale = math.log2(math.e) / math.sqrt(HEAD)
    count = len(mine) * part_rows

    def own_places():
        order = lax.broadcasted_iota(jnp.int32, (count, rows), 0)
        own = order % part_rows + part * part_rows
        for at_chunk, chunk in enumerate(mine):
            own = jnp.where(order // part_rows == at_chunk, own + chunk * chunk_rows, own)
        return own

    if seq_count <= 8:
        later = lax.broadcasted_iota(jnp.int32, (count, rows), 1) > own_places()
        for home in range(seq_count):
            queries = jnp.concatenate([pieces[c * group][home, :, :HEAD] for c in mine], axis=0)
            blocks = []
            for other in range(home + 1):
                scores = lax.dot_general(
                    queries,
                    keys[other * rows : (other + 1) * rows, :],
                    (((1,), (1,)), ((), ())),
                    preferred_element_type=jnp.float32,
                )
                scores = scores * scale + bias_ref[other : other + 1, :]
                if other == home:
                    scores = jnp.where(later, MASKED, scores)
                blocks.append(scores)
            scores = jnp.concatenate(blocks, axis=1)
            best = jnp.max(scores, axis=1, keepdims=True)
            weights = jnp.exp2(scores - best)
            total = jnp.sum(weights, axis=1, keepdims=True)
            summed = jnp.dot(
                weights.astype(jnp.bfloat16),
                values[: (home + 1) * rows, :],
                preferred_element_type=jnp.float32,
            )
            out_ref[home] = (summed / total).astype(jnp.bfloat16)
        return

    def one_home(home, _):
        queries = jnp.concatenate([pieces[c * group][home, :, :HEAD] for c in mine], axis=0)

        def fold(other, carry, diagonal):
            best, total, summed = carry
            at = pl.multiple_of(other * rows, rows)
            scores = lax.dot_general(
                queries,
                keys[pl.ds(at, rows), :],
                (((1,), (1,)), ((), ())),
                preferred_element_type=jnp.float32,
            )
            scores = scores * scale + bias_ref[pl.ds(other, 1), :]
            if diagonal:
                place_in = lax.broadcasted_iota(jnp.int32, (count, rows), 1)
                scores = jnp.where(place_in <= own_places(), scores, MASKED)
            newbest = jnp.maximum(best, jnp.max(scores, axis=1, keepdims=True))
            factor = jnp.exp2(best - newbest)
            weights = jnp.exp2(scores - newbest)
            total = total * factor + jnp.sum(weights, axis=1, keepdims=True)
            summed = summed * factor + jnp.dot(
                weights.astype(jnp.bfloat16),
                values[pl.ds(at, rows), :],
                preferred_element_type=jnp.float32,
            )
            return newbest, total, summed

        start = (
            jnp.full((count, 1), MASKED, jnp.float32),
            jnp.zeros((count, 1), jnp.float32),
            jnp.zeros((count, HEAD), jnp.float32),
        )
        carry = fold(home, start, True)
        carry = lax.fori_loop(0, home, lambda other, c: fold(other, c, False), carry)
        _, total, summed = carry
        out_ref[home] = (summed / total).astype(jnp.bfloat16)
        return 0

    lax.fori_loop(0, seq_count, one_home, 0)


def attend(part, bias, pieces, chunks, group, mine):
    seq_count, part_rows, _ = pieces[0].shape
    rows = bias.shape[1]
    count = len(mine) * part_rows
    vmem = pl.BlockSpec(memory_space=pltpu.VMEM)
    pairs = seq_count * (seq_count + 1) // 2
    return pl.pallas_call(
        partial(attend_kernel, chunks, group, mine),
        in_specs=[pl.BlockSpec(memory_space=pltpu.SMEM), vmem] + [vmem] * len(pieces),
        out_specs=vmem,
        out_shape=jax.ShapeDtypeStruct((seq_count, count, HEAD), jnp.bfloat16),
        scratch_shapes=[
            pltpu.VMEM((seq_count * rows, HEAD), jnp.bfloat16),
            pltpu.VMEM((seq_count * rows, HEAD), jnp.bfloat16),
        ],
        compiler_params=pltpu.CompilerParams(vmem_limit_bytes=LIMIT),
        cost_estimate=pl.CostEstimate(
            flops=4 * pairs * count * rows * HEAD,
            bytes_accessed=8 * seq_count * rows * HEAD,
            transcendentals=pairs * count * rows,
        ),
    )(part, bias, *pieces)


def output_kernel(chunks, group, count, cuts, me_ref, at_ref, hidden_ref, active_ref, *refs):
    weights = refs[:cuts]
    pieces = refs[cuts : cuts + 2 * count - 1]
    out_ref, rows_in = refs[-2:]
    seq_count, piece_rows, _ = pieces[0].shape
    heads = seq_count // group
    part_rows = piece_rows // chunks
    chunk_rows = part_rows * group
    width = weights[0].shape[1]

    for piece, (source, there) in zip(pieces, sources(me_ref[0], count)):
        def place(piece=piece, source=source):
            for head in range(heads):
                at = pl.multiple_of(at_ref[source * heads + head] * HEAD, HEAD)
                for part in range(group):
                    for chunk in range(chunks):
                        first = chunk * chunk_rows + part * part_rows
                        rows_in[first : first + part_rows, pl.ds(at, HEAD)] = piece[
                            head * group + part, chunk * part_rows : (chunk + 1) * part_rows, :
                        ]

        if there is None:
            place()
        else:
            pl.when(there)(place)

    for cut, weight in enumerate(weights):
        columns = pl.ds(pl.multiple_of(me_ref[1 + cut] * width, width), width)
        shares = jnp.dot(rows_in[...], weight[...], preferred_element_type=jnp.float32)
        hidden = hidden_ref[:, columns]
        renewed = (hidden.astype(jnp.float32) + shares).astype(jnp.bfloat16)
        out_ref[:, columns] = jnp.where(active_ref[...] > 0, renewed, hidden)


def output(scalars, at, pieces, weights, hidden, active, so_far, which, parts, chunks, group):
    rows, columns = hidden.shape
    here = rows // parts
    depth = weights[0].shape[0]
    smem = pl.BlockSpec(memory_space=pltpu.SMEM)
    row_block = pl.BlockSpec((here, columns), lambda j: (which, 0))
    operands = [scalars, at, hidden, active, *weights, *pieces]
    in_specs = [smem, smem, row_block, pl.BlockSpec((here, 1), lambda j: (which, 0))]
    in_specs += [pl.BlockSpec(w.shape, lambda j: (0, 0)) for w in weights]
    in_specs += [pl.BlockSpec(p.shape, lambda j: (0, 0, 0)) for p in pieces]
    aliases = {}
    if so_far is not None:
        aliases = {len(operands): 0}
        operands.append(so_far)
        in_specs.append(pl.BlockSpec(memory_space=pl.ANY))
    return pl.pallas_call(
        partial(output_kernel, chunks, group, len(pieces) // 2 + 1, len(weights)),
        grid=(1,),
        in_specs=in_specs,
        out_specs=row_block,
        out_shape=jax.ShapeDtypeStruct((rows, columns), jnp.bfloat16),
        scratch_shapes=[pltpu.VMEM((here, depth), jnp.bfloat16)],
        input_output_aliases=aliases,
        compiler_params=pltpu.CompilerParams(vmem_limit_bytes=LIMIT),
        cost_estimate=pl.CostEstimate(
            flops=2 * here * depth * columns,
            bytes_accessed=2 * (here * depth + depth * columns + 2 * here * columns),
            transcendentals=0,
        ),
    )(*operands)


def output_weight(w_out, seq_count, tensor_count, columns, after):
    heads = w_out.shape[0] // HEAD
    cuts = seq_count // heads
    width = columns // cuts
    row = jnp.arange(tensor_count * heads, dtype=jnp.int32)
    if width % HEAD:
        weight = lax.all_to_all(w_out, "tensor", split_axis=1, concat_axis=0, tiled=True)
        return [weight], [jnp.int32(0)], row
    seq_me = lax.axis_index("seq").astype(jnp.int32)
    me = lax.axis_index("tensor").astype(jnp.int32)
    head, cut = seq_me // cuts, seq_me % cuts
    w_out, after = lax.optimization_barrier((w_out, after))

    def share(to):
        return lax.dynamic_slice(w_out, (head * HEAD, to * columns + cut * width), (HEAD, width))

    shares = [share(me)]
    for step in range(1, tensor_count):
        ring = [(d, (d + step) % tensor_count) for d in range(tensor_count)]
        shares.append(lax.ppermute(share((me + step) % tensor_count), "tensor", ring))
    held = jnp.concatenate(shares, axis=0)
    flip = seq_count // 2
    while flip >= cuts:
        pairs = [(d, d ^ flip) for d in range(seq_count)]
        held = jnp.concatenate([held, lax.ppermute(held, "seq", pairs)], axis=0)
        flip //= 2
    weights, which = [held], [cut]
    for step in range(1, cuts):
        ring = [(d, d - d % cuts + (d - step) % cuts) for d in range(seq_count)]
        weights.append(lax.ppermute(held, "seq", ring))
        which.append((cut + step) % cuts)
    tensor, of = row // heads, row % heads
    apart = of ^ head
    turned, bit, size = jnp.zeros_like(apart), 1, heads
    while bit < heads:
        turned = turned + jnp.where((apart & bit) > 0, heads // (2 * bit), 0)
        bit *= 2
    at = turned * tensor_count + (me - tensor) % tensor_count
    return weights, which, at


def shards(hidden, depth, norm_gain, w_query, w_key, w_value, w_out):
    rows, columns = hidden.shape
    seq_count = lax.axis_size("seq")
    tensor_count = lax.axis_size("tensor")
    heads = w_query.shape[1] // HEAD
    group = seq_count // heads
    chunks = min(4, rows // (16 * group))
    chunk_rows = rows // chunks
    back = min(BACK, chunks)
    part = (lax.axis_index("seq") % group).astype(jnp.int32).reshape(1)
    me = lax.axis_index("tensor").astype(jnp.int32)
    gain = norm_gain.reshape(1, -1)

    gathered = line_gather(
        [hidden[c * chunk_rows : (c + 1) * chunk_rows] for c in range(chunks)], tensor_count
    )
    depths = lax.all_gather(depth, "seq", axis=0)
    bias = jnp.where(depths >= 2, 0.0, MASKED).astype(jnp.float32)
    active = (depth >= 2).astype(jnp.int32).reshape(rows, 1)

    pieces = []
    for found in gathered:
        sent = project(me.reshape(1), found, gain, w_query, w_key, w_value, seq_count, group)
        got = lax.all_to_all(sent, "seq", split_axis=0, concat_axis=0)
        pieces.append(got)
        for step in range(1, group):
            ring = [(d, d - d % group + (d - step) % group) for d in range(seq_count)]
            pieces.append(lax.ppermute(got, "seq", ring))

    weights, cut_of, at = output_weight(w_out, seq_count, tensor_count, columns, gathered[-1][-1])
    scalars = jnp.stack([me, *cut_of])
    updated = None
    each = chunks // back
    for which in range(back):
        mine = tuple(range(which * each, (which + 1) * each))
        out = attend(part, bias, pieces, chunks, group, mine)
        home = lax.all_to_all(out, "seq", split_axis=0, concat_axis=0)
        (found,) = line_gather([home], tensor_count)
        updated = output(
            scalars, at, found, weights, hidden, active, updated, which, back, each, group
        )
    return updated


def solution(mesh):
    return jax.shard_map(
        shards,
        mesh=mesh,
        in_specs=(
            P("seq", "tensor"),
            P("seq"),
            P(),
            P(None, "tensor"),
            P(None, "tensor"),
            P(None, "tensor"),
            P("tensor", None),
        ),
        out_specs=P("seq", "tensor"),
        check_vma=False,
    )
```

```python
import math
from functools import partial

import jax
import jax.numpy as jnp
from jax import lax
from jax.experimental import pallas as pl
from jax.experimental.pallas import tpu as pltpu
from jax.sharding import PartitionSpec as P

HEAD = 128
MASKED = -1e30
BACK = 2
LIMIT = 60 * 2**20


def sources(me, count):
    found = [(me, None)]
    for step in range(count - 1):
        found.append((me - 1 - step, me - 1 - step >= 0))
        found.append((me + 1 + step, me + 1 + step < count))
    return found


def line_gather(chunks, count, also=None):
    right = [(d, d + 1) for d in range(count - 1)]
    left = [(d + 1, d) for d in range(count - 1)]
    found = []
    for first in range(0, len(chunks), 2):
        pair = []
        for chunk in chunks[first : first + 2]:
            if first:
                chunk, _ = lax.optimization_barrier((chunk, (found[len(found) - 2 + len(pair)], also)))
            pair.append([chunk])
        last = [(chunk[0], chunk[0]) for chunk in pair]
        for step in range(count - 1):
            for at, (from_left, from_right) in enumerate(last):
                from_left = lax.ppermute(from_left, "tensor", right[step:])
                from_right = lax.ppermute(from_right, "tensor", left[: count - 1 - step])
                last[at] = (from_left, from_right)
                pair[at] += [from_left, from_right]
        found += pair
    return found


def project_kernel(group, count, me_ref, gain_ref, wq_ref, wk_ref, wv_ref, *refs):
    pieces = refs[:-3]
    out_ref, normed, sums = refs[-3:]
    step = pl.program_id(0)
    rows, width = pieces[0].shape

    @pl.when(step == 0)
    def _():
        for piece, (source, there) in zip(pieces, sources(me_ref[0], count)):
            def place(piece=piece, source=source):
                normed[source] = piece[...]

            if there is None:
                place()
            else:
                pl.when(there)(place)
        square = jnp.zeros((rows, 1), jnp.float32)
        for source in range(count):
            values = normed[source].astype(jnp.float32)
            square = square + jnp.sum(values * values, axis=1, keepdims=True)
        row_scale = lax.rsqrt(square / (count * width) + 1e-05)
        for source in range(count):
            values = normed[source].astype(jnp.float32)
            normed[source] = (values * row_scale * gain_ref[source : source + 1, :]).astype(
                jnp.bfloat16
            )

    x = normed[step]
    for which, weight in enumerate((wq_ref, wk_ref, wv_ref)):
        product = jnp.dot(x, weight[...], preferred_element_type=jnp.float32)

        @pl.when(step == 0)
        def _():
            sums[which] = product

        @pl.when(step > 0)
        def _():
            sums[which] += product

    @pl.when(step == count - 1)
    def _():
        part_rows = out_ref.shape[1]
        for which in range(3):
            total = sums[which].astype(jnp.bfloat16)
            for head in range(wq_ref.shape[1] // HEAD):
                for part in range(group):
                    out_ref[head * group + part, :, which * HEAD : (which + 1) * HEAD] = total[
                        part * part_rows : (part + 1) * part_rows, head * HEAD : (head + 1) * HEAD
                    ]


def project(me, pieces, gain, wq, wk, wv, seq_count, group):
    rows, columns = pieces[0].shape
    features, width = wq.shape
    count = features // columns
    part_rows = rows // group
    weight_spec = pl.BlockSpec((columns, width), lambda j: (j, 0))
    return pl.pallas_call(
        partial(project_kernel, group, count),
        grid=(count,),
        in_specs=[
            pl.BlockSpec(memory_space=pltpu.SMEM),
            pl.BlockSpec((count, columns), lambda j: (0, 0)),
            weight_spec,
            weight_spec,
            weight_spec,
        ]
        + [pl.BlockSpec((rows, columns), lambda j: (0, 0))] * len(pieces),
        out_specs=pl.BlockSpec((seq_count, part_rows, 3 * HEAD), lambda j: (0, 0, 0)),
        out_shape=jax.ShapeDtypeStruct((seq_count, part_rows, 3 * HEAD), jnp.bfloat16),
        scratch_shapes=[
            pltpu.VMEM((count, rows, columns), jnp.bfloat16),
            pltpu.VMEM((3, rows, width), jnp.float32),
        ],
        compiler_params=pltpu.CompilerParams(vmem_limit_bytes=LIMIT),
        cost_estimate=pl.CostEstimate(
            flops=6 * rows * features * width,
            bytes_accessed=6 * features * width + 2 * rows * (features + 3 * width),
            transcendentals=0,
        ),
    )(me, gain, wq, wk, wv, *pieces)


def attend_kernel(chunks, group, back, part_ref, bias_ref, *refs):
    pieces = refs[: chunks * group]
    outs = refs[chunks * group : chunks * group + back]
    keys, values = refs[-2:]
    mine = range(chunks)
    seq_count, part_rows, _ = pieces[0].shape
    rows = bias_ref.shape[1]
    chunk_rows = rows // chunks
    part = part_ref[0]

    def place(home, _):
        for chunk in range(chunks):
            for step in range(group):
                owner = lax.rem(part + step, group)
                at = pl.multiple_of(home * rows + chunk * chunk_rows + owner * part_rows, part_rows)
                piece = pieces[chunk * group + step]
                keys[pl.ds(at, part_rows), :] = piece[home, :, HEAD : 2 * HEAD]
                values[pl.ds(at, part_rows), :] = piece[home, :, 2 * HEAD :]
        return 0

    lax.fori_loop(0, seq_count, place, 0)
    scale = math.log2(math.e) / math.sqrt(HEAD)
    count = len(mine) * part_rows

    def store(home, rows_out):
        each = count // back
        for at, out in enumerate(outs):
            out[home] = rows_out[at * each : (at + 1) * each]

    def own_places():
        order = lax.broadcasted_iota(jnp.int32, (count, rows), 0)
        own = order % part_rows + part * part_rows
        for at_chunk, chunk in enumerate(mine):
            own = jnp.where(order // part_rows == at_chunk, own + chunk * chunk_rows, own)
        return own

    if seq_count <= 8:
        later = lax.broadcasted_iota(jnp.int32, (count, rows), 1) > own_places()
        for home in range(seq_count):
            queries = jnp.concatenate([pieces[c * group][home, :, :HEAD] for c in mine], axis=0)
            blocks = []
            for other in range(home + 1):
                scores = lax.dot_general(
                    queries,
                    keys[other * rows : (other + 1) * rows, :],
                    (((1,), (1,)), ((), ())),
                    preferred_element_type=jnp.float32,
                )
                scores = scores * scale + bias_ref[other : other + 1, :]
                if other == home:
                    scores = jnp.where(later, MASKED, scores)
                blocks.append(scores)
            scores = jnp.concatenate(blocks, axis=1)
            best = jnp.max(scores, axis=1, keepdims=True)
            weights = jnp.exp2(scores - best)
            total = jnp.sum(weights, axis=1, keepdims=True)
            summed = jnp.dot(
                weights.astype(jnp.bfloat16),
                values[: (home + 1) * rows, :],
                preferred_element_type=jnp.float32,
            )
            store(home, (summed / total).astype(jnp.bfloat16))
        return

    def one_home(home, _):
        queries = jnp.concatenate([pieces[c * group][home, :, :HEAD] for c in mine], axis=0)

        def fold(other, carry, diagonal):
            best, total, summed = carry
            at = pl.multiple_of(other * rows, rows)
            scores = lax.dot_general(
                queries,
                keys[pl.ds(at, rows), :],
                (((1,), (1,)), ((), ())),
                preferred_element_type=jnp.float32,
            )
            scores = scores * scale + bias_ref[pl.ds(other, 1), :]
            if diagonal:
                place_in = lax.broadcasted_iota(jnp.int32, (count, rows), 1)
                scores = jnp.where(place_in <= own_places(), scores, MASKED)
            newbest = jnp.maximum(best, jnp.max(scores, axis=1, keepdims=True))
            factor = jnp.exp2(best - newbest)
            weights = jnp.exp2(scores - newbest)
            total = total * factor + jnp.sum(weights, axis=1, keepdims=True)
            summed = summed * factor + jnp.dot(
                weights.astype(jnp.bfloat16),
                values[pl.ds(at, rows), :],
                preferred_element_type=jnp.float32,
            )
            return newbest, total, summed

        start = (
            jnp.full((count, 1), MASKED, jnp.float32),
            jnp.zeros((count, 1), jnp.float32),
            jnp.zeros((count, HEAD), jnp.float32),
        )
        carry = fold(home, start, True)
        carry = lax.fori_loop(0, home, lambda other, c: fold(other, c, False), carry)
        _, total, summed = carry
        store(home, (summed / total).astype(jnp.bfloat16))
        return 0

    lax.fori_loop(0, seq_count, one_home, 0)


def attend(part, bias, pieces, chunks, group, back):
    seq_count, part_rows, _ = pieces[0].shape
    rows = bias.shape[1]
    count = chunks * part_rows
    vmem = pl.BlockSpec(memory_space=pltpu.VMEM)
    pairs = seq_count * (seq_count + 1) // 2
    return pl.pallas_call(
        partial(attend_kernel, chunks, group, back),
        in_specs=[pl.BlockSpec(memory_space=pltpu.SMEM), vmem] + [vmem] * len(pieces),
        out_specs=[vmem] * back,
        out_shape=[jax.ShapeDtypeStruct((seq_count, count // back, HEAD), jnp.bfloat16)] * back,
        scratch_shapes=[
            pltpu.VMEM((seq_count * rows, HEAD), jnp.bfloat16),
            pltpu.VMEM((seq_count * rows, HEAD), jnp.bfloat16),
        ],
        compiler_params=pltpu.CompilerParams(vmem_limit_bytes=LIMIT),
        cost_estimate=pl.CostEstimate(
            flops=4 * pairs * count * rows * HEAD,
            bytes_accessed=8 * seq_count * rows * HEAD,
            transcendentals=pairs * count * rows,
        ),
    )(part, bias, *pieces)


def output_kernel(chunks, group, count, cuts, halves, me_ref, at_ref, hidden_ref, active_ref, *refs):
    weights = refs[:cuts]
    pieces = refs[cuts:-4]
    out_ref, rows_in, held, arrived = refs[-4:]
    copies = [
        pltpu.make_async_copy(weight, held.at[cut], arrived.at[cut])
        for cut, weight in enumerate(weights)
    ]
    for copy in copies:
        copy.start()
    seq_count, piece_rows, _ = pieces[0].shape
    heads = seq_count // group
    per_half = chunks // halves
    part_rows = piece_rows // per_half
    chunk_rows = part_rows * group
    width = weights[0].shape[1]
    found = sources(me_ref[0], count)

    for number, piece in enumerate(pieces):
        half, (source, there) = number // len(found), found[number % len(found)]

        def place(half=half, piece=piece, source=source):
            for head in range(heads):
                at = pl.multiple_of(at_ref[source * heads + head] * HEAD, HEAD)
                for part in range(group):
                    for chunk in range(per_half):
                        first = (half * per_half + chunk) * chunk_rows + part * part_rows
                        rows_in[first : first + part_rows, pl.ds(at, HEAD)] = piece[
                            head * group + part, chunk * part_rows : (chunk + 1) * part_rows, :
                        ]

        if there is None:
            place()
        else:
            pl.when(there)(place)

    for cut in range(cuts):
        copies[cut].wait()
        columns = pl.ds(pl.multiple_of(me_ref[1 + cut] * width, width), width)
        shares = jnp.dot(rows_in[...], held[cut], preferred_element_type=jnp.float32)
        hidden = hidden_ref[:, columns]
        renewed = (hidden.astype(jnp.float32) + shares).astype(jnp.bfloat16)
        out_ref[:, columns] = jnp.where(active_ref[...] > 0, renewed, hidden)


def output(scalars, at, pieces, weights, hidden, active, chunks, group, halves):
    rows, columns = hidden.shape
    depth, width = weights[0].shape
    smem = pl.BlockSpec(memory_space=pltpu.SMEM)
    vmem = pl.BlockSpec(memory_space=pltpu.VMEM)
    cuts = len(weights)
    count = (len(pieces) // halves + 1) // 2
    return pl.pallas_call(
        partial(output_kernel, chunks, group, count, cuts, halves),
        in_specs=[smem, smem, vmem, vmem]
        + [pl.BlockSpec(memory_space=pl.ANY)] * cuts
        + [vmem] * len(pieces),
        out_specs=vmem,
        out_shape=jax.ShapeDtypeStruct((rows, columns), jnp.bfloat16),
        scratch_shapes=[
            pltpu.VMEM((rows, depth), jnp.bfloat16),
            pltpu.VMEM((cuts, depth, width), jnp.bfloat16),
            pltpu.SemaphoreType.DMA((cuts,)),
        ],
        compiler_params=pltpu.CompilerParams(vmem_limit_bytes=LIMIT),
        cost_estimate=pl.CostEstimate(
            flops=2 * rows * depth * columns,
            bytes_accessed=2 * (rows * depth + depth * columns + 2 * rows * columns),
            transcendentals=0,
        ),
    )(scalars, at, hidden, active, *weights, *pieces)


def output_weight(w_out, seq_count, tensor_count, columns, after):
    heads = w_out.shape[0] // HEAD
    cuts = seq_count // heads
    width = columns // cuts
    row = jnp.arange(tensor_count * heads, dtype=jnp.int32)
    if width % HEAD:
        weight = lax.all_to_all(w_out, "tensor", split_axis=1, concat_axis=0, tiled=True)
        return [weight], [jnp.int32(0)], row
    seq_me = lax.axis_index("seq").astype(jnp.int32)
    me = lax.axis_index("tensor").astype(jnp.int32)
    head, cut = seq_me // cuts, seq_me % cuts

    def share(to):
        return lax.dynamic_slice(w_out, (head * HEAD, to * columns + cut * width), (HEAD, width))

    shares = [share((me + step) % tensor_count) for step in range(tensor_count)]
    shares, _ = lax.optimization_barrier((shares, after))
    for step in range(1, tensor_count):
        ring = [(d, (d + step) % tensor_count) for d in range(tensor_count)]
        shares[step] = lax.ppermute(shares[step], "tensor", ring)
    flips = []
    while cuts << len(flips) < seq_count:
        flips.append(cuts << len(flips))
    halves = 2 if width % (2 * HEAD) == 0 else 1
    each = width // halves
    weights, which = [], []
    for half in range(halves):
        held = {0: jnp.concatenate([s[:, half * each : (half + 1) * each] for s in shares], axis=0)}
        for flip in flips if half == 0 else flips[::-1]:
            pairs = [(d, d ^ flip) for d in range(seq_count)]
            sent = list(held)
            got = lax.ppermute(jnp.concatenate([held[k] for k in sent], axis=0), "seq", pairs)
            for k, block in zip(sent, jnp.split(got, len(sent))):
                held[k ^ flip] = block
        weights.append(jnp.concatenate([held[k] for k in sorted(held)], axis=0))
        which.append(cut * halves + half)
    for step in range(1, cuts):
        ring = [(d, d - d % cuts + (d - step) % cuts) for d in range(seq_count)]
        for half in range(halves):
            weights.append(lax.ppermute(weights[half], "seq", ring))
            which.append((cut + step) % cuts * halves + half)
    tensor, of = row // heads, row % heads
    at = (of ^ head) * tensor_count + (me - tensor) % tensor_count
    return weights, which, at


def shards(hidden, depth, norm_gain, w_query, w_key, w_value, w_out):
    rows, columns = hidden.shape
    seq_count = lax.axis_size("seq")
    tensor_count = lax.axis_size("tensor")
    heads = w_query.shape[1] // HEAD
    group = seq_count // heads
    chunks = min(4, rows // (16 * group))
    chunk_rows = rows // chunks
    back = min(BACK, chunks)
    part = (lax.axis_index("seq") % group).astype(jnp.int32).reshape(1)
    me = lax.axis_index("tensor").astype(jnp.int32)
    gain = norm_gain.reshape(tensor_count, columns)
    depths = lax.all_gather(depth, "seq", axis=0)
    bias = jnp.where(depths >= 2, 0.0, MASKED).astype(jnp.float32)
    active = (depth >= 2).astype(jnp.int32).reshape(rows, 1)

    gathered = line_gather(
        [hidden[c * chunk_rows : (c + 1) * chunk_rows] for c in range(chunks)], tensor_count, bias
    )
    pieces = []
    for found in gathered:
        sent = project(me.reshape(1), found, gain, w_query, w_key, w_value, seq_count, group)
        got = lax.all_to_all(sent, "seq", split_axis=0, concat_axis=0)
        pieces.append(got)
        for step in range(1, group):
            ring = [(d, d - d % group + (d - step) % group) for d in range(seq_count)]
            pieces.append(lax.ppermute(got, "seq", ring))

    weights, cut_of, at = output_weight(w_out, seq_count, tensor_count, columns, sent)
    scalars = jnp.stack([me, *cut_of])
    outs = attend(part, bias, pieces, chunks, group, back)
    homes = [lax.all_to_all(out, "seq", split_axis=0, concat_axis=0) for out in outs]
    found = sum(line_gather(homes, tensor_count), [])
    return output(scalars, at, found, weights, hidden, active, chunks, group, back)


def solution(mesh):
    return jax.shard_map(
        shards,
        mesh=mesh,
        in_specs=(
            P("seq", "tensor"),
            P("seq"),
            P(),
            P(None, "tensor"),
            P(None, "tensor"),
            P(None, "tensor"),
            P("tensor", None),
        ),
        out_specs=P("seq", "tensor"),
        check_vma=False,
    )
```

```python
import math
from functools import partial

import jax
import jax.numpy as jnp
from jax import lax
from jax.experimental import pallas as pl
from jax.experimental.pallas import tpu as pltpu
from jax.sharding import PartitionSpec as P

HEAD = 128
MASKED = -1e30
ASIDE = 2.0**100
LIMIT = 60 * 2**20


def sources(me, count):
    found = [(me, None)]
    for step in range(count - 1):
        found.append((me - 1 - step, me - 1 - step >= 0))
        found.append((me + 1 + step, me + 1 + step < count))
    return found


def line_gather(chunks, count, between=None):
    right = [(d, d + 1) for d in range(count - 1)]
    left = [(d + 1, d) for d in range(count - 1)]
    found, made = [], None
    for first in range(0, len(chunks), 2):
        pair = []
        for chunk in chunks[first : first + 2]:
            if first:
                chunk, _ = lax.optimization_barrier((chunk, found[first - 2 + len(pair)]))
            pair.append([chunk])
        last = [(chunk[0], chunk[0]) for chunk in pair]
        for step in range(count - 1):
            for at in range(len(pair)):
                if step == 1 and at == 0 and made is not None:
                    last[at], _ = lax.optimization_barrier((last[at], made))
                from_left = lax.ppermute(last[at][0], "tensor", right[step:])
                from_right = lax.ppermute(last[at][1], "tensor", left[: count - 1 - step])
                last[at] = (from_left, from_right)
                pair[at] += [from_left, from_right]
        found += pair
        if between is not None and first + 2 < len(chunks):
            made = between(pair)
    return found


def project_kernel(group, count, me_ref, gain_ref, active_ref, *refs):
    matrices = refs[:3]
    pieces = refs[3:-4]
    out_ref, normed, held, arrived = refs[-4:]
    block = held.shape[3]
    blocks = matrices[0].shape[1] // block
    copies = [
        pltpu.make_async_copy(
            matrix.at[:, at * block : (at + 1) * block], held.at[at, which], arrived.at[at, which]
        )
        for at in range(blocks)
        for which, matrix in enumerate(matrices)
    ]
    for copy in copies:
        copy.start()
    found = sources(me_ref[0], count)
    chunk_rows, width = pieces[0].shape
    chunks = len(pieces) // len(found)
    rows = chunks * chunk_rows

    for number, piece in enumerate(pieces):
        first, (source, there) = number // len(found) * chunk_rows, found[number % len(found)]

        def place(first=first, piece=piece, source=source):
            normed[source, first : first + chunk_rows, :] = piece[...]

        if there is None:
            place()
        else:
            pl.when(there)(place)

    square = jnp.zeros((rows, 1), jnp.float32)
    for source in range(count):
        values = normed[source].astype(jnp.float32)
        square = square + jnp.sum(values * values, axis=1, keepdims=True)
    row_scale = lax.rsqrt(square / (count * width) + 1e-05)
    x = jnp.concatenate(
        [
            (normed[source].astype(jnp.float32) * row_scale * gain_ref[source : source + 1, :]).astype(
                jnp.bfloat16
            )
            for source in range(count)
        ],
        axis=1,
    )
    part_rows = chunk_rows // group
    for at in range(blocks):
        for which in range(3):
            copies[at * 3 + which].wait()
            total = jnp.dot(x, held[at, which], preferred_element_type=jnp.float32)
            if which == 0:
                total = jnp.where(active_ref[...] > 0, total, ASIDE)
            total = total.astype(jnp.bfloat16)
            for inner in range(block // HEAD):
                head = at * (block // HEAD) + inner
                for part in range(group):
                    for chunk in range(chunks):
                        first = chunk * chunk_rows + part * part_rows
                        out_ref[
                            head * group + part,
                            chunk * part_rows : (chunk + 1) * part_rows,
                            which * HEAD : (which + 1) * HEAD,
                        ] = total[first : first + part_rows, inner * HEAD : (inner + 1) * HEAD]


def project(me, pieces, active, gain, wq, wk, wv, seq_count, group):
    columns = pieces[0].shape[1]
    rows = active.shape[0]
    features, width = wq.shape
    count = features // columns
    block = min(256, width)
    vmem = pl.BlockSpec(memory_space=pltpu.VMEM)
    return pl.pallas_call(
        partial(project_kernel, group, count),
        in_specs=[pl.BlockSpec(memory_space=pltpu.SMEM), vmem, vmem]
        + [pl.BlockSpec(memory_space=pl.ANY)] * 3
        + [vmem] * len(pieces),
        out_specs=vmem,
        out_shape=jax.ShapeDtypeStruct((seq_count, rows // group, 3 * HEAD), jnp.bfloat16),
        scratch_shapes=[
            pltpu.VMEM((count, rows, columns), jnp.bfloat16),
            pltpu.VMEM((width // block, 3, features, block), jnp.bfloat16),
            pltpu.SemaphoreType.DMA((width // block, 3)),
        ],
        compiler_params=pltpu.CompilerParams(vmem_limit_bytes=LIMIT),
        cost_estimate=pl.CostEstimate(
            flops=6 * rows * features * width,
            bytes_accessed=6 * features * width + 2 * rows * (features + 3 * width),
            transcendentals=0,
        ),
    )(me, gain, active, wq, wk, wv, *pieces)


def attend_kernel(chunks, group, rows, part_ref, *refs):
    pieces = refs[:-3]
    out_ref, keys, values = refs[-3:]
    seq_count = pieces[0].shape[0]
    chunk_rows = rows // chunks
    part_rows = chunk_rows // group
    part = part_ref[0]

    def place(home, _):
        chunk = 0
        for number in range(0, len(pieces), group):
            inside = pieces[number].shape[1] // part_rows
            for step in range(group):
                owner = lax.rem(part + step, group)
                piece = pieces[number + step]
                for at_chunk in range(inside):
                    at = home * rows + (chunk + at_chunk) * chunk_rows + owner * part_rows
                    to = pl.ds(pl.multiple_of(at, part_rows), part_rows)
                    of = slice(at_chunk * part_rows, (at_chunk + 1) * part_rows)
                    aside = piece[home, of, :HEAD].astype(jnp.float32) >= ASIDE
                    keys[to, :HEAD] = piece[home, of, HEAD : 2 * HEAD]
                    keys[to, HEAD:] = jnp.where(aside, MASKED, 0.0).astype(jnp.bfloat16)
                    values[to, :] = piece[home, of, 2 * HEAD :]
            chunk += inside
        return 0

    lax.fori_loop(0, seq_count, place, 0)
    scale = math.log2(math.e) / math.sqrt(HEAD)
    count = chunks * part_rows
    first_lane = lax.broadcasted_iota(jnp.int32, (count, HEAD), 1) == 0
    mask_lane = jnp.where(first_lane, 1.0, 0.0).astype(jnp.bfloat16)
    order = lax.broadcasted_iota(jnp.int32, (count, rows), 0)
    own = order // part_rows * chunk_rows + part * part_rows + order % part_rows
    later = lax.broadcasted_iota(jnp.int32, (count, rows), 1) > own

    def queries_of(home):
        queries = jnp.concatenate(
            [pieces[number][home, :, :HEAD] for number in range(0, len(pieces), group)], axis=0
        )
        return jnp.concatenate([queries, mask_lane], axis=1)

    def scores_of(queries, at):
        return scale * lax.dot_general(
            queries,
            keys[at, :],
            (((1,), (1,)), ((), ())),
            preferred_element_type=jnp.float32,
        )

    if seq_count <= 8:
        for home in range(seq_count):
            queries = queries_of(home)
            blocks = []
            for other in range(home + 1):
                scores = scores_of(queries, slice(other * rows, (other + 1) * rows))
                if other == home:
                    scores = jnp.where(later, MASKED, scores)
                blocks.append(scores)
            scores = jnp.concatenate(blocks, axis=1)
            best = jnp.max(scores, axis=1, keepdims=True)
            weights = jnp.exp2(scores - best)
            total = jnp.sum(weights, axis=1, keepdims=True)
            summed = jnp.dot(
                weights.astype(jnp.bfloat16),
                values[: (home + 1) * rows, :],
                preferred_element_type=jnp.float32,
            )
            out_ref[home] = (summed / total).astype(jnp.bfloat16)
        return

    def one_home(home, _):
        queries = queries_of(home)

        def fold(other, carry, diagonal):
            best, total, summed = carry
            at = pl.ds(pl.multiple_of(other * rows, rows), rows)
            scores = scores_of(queries, at)
            if diagonal:
                scores = jnp.where(later, MASKED, scores)
            newbest = jnp.maximum(best, jnp.max(scores, axis=1, keepdims=True))
            factor = jnp.exp2(best - newbest)
            weights = jnp.exp2(scores - newbest)
            total = total * factor + jnp.sum(weights, axis=1, keepdims=True)
            summed = summed * factor + jnp.dot(
                weights.astype(jnp.bfloat16), values[at, :], preferred_element_type=jnp.float32
            )
            return newbest, total, summed

        start = (
            jnp.full((count, 1), MASKED, jnp.float32),
            jnp.zeros((count, 1), jnp.float32),
            jnp.zeros((count, HEAD), jnp.float32),
        )
        carry = fold(home, start, True)
        carry = lax.fori_loop(0, home, lambda other, c: fold(other, c, False), carry)
        _, total, summed = carry
        out_ref[home] = (summed / total).astype(jnp.bfloat16)
        return 0

    lax.fori_loop(0, seq_count, one_home, 0)


def attend(part, pieces, chunks, group, rows):
    seq_count = pieces[0].shape[0]
    count = rows // group
    vmem = pl.BlockSpec(memory_space=pltpu.VMEM)
    pairs = seq_count * (seq_count + 1) // 2
    return pl.pallas_call(
        partial(attend_kernel, chunks, group, rows),
        in_specs=[pl.BlockSpec(memory_space=pltpu.SMEM)] + [vmem] * len(pieces),
        out_specs=vmem,
        out_shape=jax.ShapeDtypeStruct((seq_count, count, HEAD), jnp.bfloat16),
        scratch_shapes=[
            pltpu.VMEM((seq_count * rows, 2 * HEAD), jnp.bfloat16),
            pltpu.VMEM((seq_count * rows, HEAD), jnp.bfloat16),
        ],
        compiler_params=pltpu.CompilerParams(vmem_limit_bytes=LIMIT),
        cost_estimate=pl.CostEstimate(
            flops=6 * pairs * count * rows * HEAD,
            bytes_accessed=8 * seq_count * rows * HEAD,
            transcendentals=pairs * count * rows,
        ),
    )(part, *pieces)


def output_kernel(chunks, group, count, cuts, halves, me_ref, at_ref, hidden_ref, active_ref, *refs):
    weights = refs[:cuts]
    pieces = refs[cuts:-4]
    out_ref, rows_in, held, arrived = refs[-4:]
    copies = [
        pltpu.make_async_copy(weight, held.at[cut], arrived.at[cut])
        for cut, weight in enumerate(weights)
    ]
    for copy in copies:
        copy.start()
    sent, piece_rows, _ = pieces[0].shape
    heads = sent // group
    part_rows = piece_rows // chunks
    chunk_rows = part_rows * group
    width = weights[0].shape[1]
    found = sources(me_ref[0], count)

    for number, piece in enumerate(pieces):
        half, (source, there) = number // len(found), found[number % len(found)]

        def place(half=half, piece=piece, source=source):
            for head in range(heads):
                at = pl.multiple_of(at_ref[(source * halves + half) * heads + head] * HEAD, HEAD)
                for part in range(group):
                    for chunk in range(chunks):
                        first = chunk * chunk_rows + part * part_rows
                        rows_in[first : first + part_rows, pl.ds(at, HEAD)] = piece[
                            head * group + part, chunk * part_rows : (chunk + 1) * part_rows, :
                        ]

        if there is None:
            place()
        else:
            pl.when(there)(place)

    for cut in range(cuts):
        copies[cut].wait()
        columns = pl.ds(pl.multiple_of(me_ref[1 + cut] * width, width), width)
        shares = jnp.dot(rows_in[...], held[cut], preferred_element_type=jnp.float32)
        hidden = hidden_ref[:, columns]
        renewed = (hidden.astype(jnp.float32) + shares).astype(jnp.bfloat16)
        out_ref[:, columns] = jnp.where(active_ref[...] > 0, renewed, hidden)


def output(scalars, at, pieces, weights, hidden, active, chunks, group, halves):
    rows, columns = hidden.shape
    depth, width = weights[0].shape
    smem = pl.BlockSpec(memory_space=pltpu.SMEM)
    vmem = pl.BlockSpec(memory_space=pltpu.VMEM)
    cuts = len(weights)
    count = (len(pieces) // halves + 1) // 2
    return pl.pallas_call(
        partial(output_kernel, chunks, group, count, cuts, halves),
        in_specs=[smem, smem, vmem, vmem]
        + [pl.BlockSpec(memory_space=pl.ANY)] * cuts
        + [vmem] * len(pieces),
        out_specs=vmem,
        out_shape=jax.ShapeDtypeStruct((rows, columns), jnp.bfloat16),
        scratch_shapes=[
            pltpu.VMEM((rows, depth), jnp.bfloat16),
            pltpu.VMEM((cuts, depth, width), jnp.bfloat16),
            pltpu.SemaphoreType.DMA((cuts,)),
        ],
        compiler_params=pltpu.CompilerParams(vmem_limit_bytes=LIMIT),
        cost_estimate=pl.CostEstimate(
            flops=2 * rows * depth * columns,
            bytes_accessed=2 * (rows * depth + depth * columns + 2 * rows * columns),
            transcendentals=0,
        ),
    )(scalars, at, hidden, active, *weights, *pieces)


def share_kernel(columns, place_ref, w_ref, *refs):
    shares, arrived = refs[:-1], refs[-1]
    copies = []
    for step, share in enumerate(shares):
        to = lax.rem(place_ref[2] + step, len(shares))
        for half in range(share.shape[0]):
            each = share.shape[2]
            first = pl.multiple_of(to * columns + place_ref[1] + half * each, each)
            rows = pl.ds(pl.multiple_of(place_ref[0], HEAD), HEAD)
            copies.append(
                pltpu.make_async_copy(
                    w_ref.at[rows, pl.ds(first, each)], share.at[half], arrived.at[step, half]
                )
            )
    for copy in copies:
        copy.start()
    for copy in copies:
        copy.wait()


def shares_of(w_out, place, count, halves, each):
    columns = w_out.shape[1] // count
    return pl.pallas_call(
        partial(share_kernel, columns),
        in_specs=[pl.BlockSpec(memory_space=pltpu.SMEM), pl.BlockSpec(memory_space=pl.ANY)],
        out_specs=[pl.BlockSpec(memory_space=pl.ANY)] * count,
        out_shape=[jax.ShapeDtypeStruct((halves, HEAD, each), w_out.dtype)] * count,
        scratch_shapes=[pltpu.SemaphoreType.DMA((count, halves))],
        compiler_params=pltpu.CompilerParams(vmem_limit_bytes=LIMIT),
    )(place, w_out)


def output_weight(w_out, seq_count, tensor_count, columns, after, last):
    heads = w_out.shape[0] // HEAD
    cuts = seq_count // heads
    width = columns // cuts
    row = jnp.arange(tensor_count * heads, dtype=jnp.int32)
    if width % HEAD:
        weight = lax.all_to_all(w_out, "tensor", split_axis=1, concat_axis=0, tiled=True)
        return [weight], [jnp.int32(0)], row
    seq_me = lax.axis_index("seq").astype(jnp.int32)
    me = lax.axis_index("tensor").astype(jnp.int32)
    head, cut = seq_me // cuts, seq_me % cuts

    halves = 2 if width % (2 * HEAD) == 0 else 1
    each = width // halves
    shares = shares_of(
        w_out, jnp.stack([head * HEAD, cut * width, me]), tensor_count, halves, each
    )
    shares, _ = lax.optimization_barrier((list(shares), after))
    for step in range(1, tensor_count):
        ring = [(d, (d + step) % tensor_count) for d in range(tensor_count)]
        shares[step] = lax.ppermute(shares[step], "tensor", ring)
    flips = []
    while cuts << len(flips) < seq_count:
        flips.append(cuts << len(flips))
    shares, _ = lax.optimization_barrier((shares, last))
    weights, which = [], []
    for half in range(halves):
        held = {0: jnp.concatenate([share[half] for share in shares], axis=0)}
        for flip in flips if half == 0 else flips[::-1]:
            pairs = [(d, d ^ flip) for d in range(seq_count)]
            sent = list(held)
            got = lax.ppermute(jnp.concatenate([held[k] for k in sent], axis=0), "seq", pairs)
            for k, block in zip(sent, jnp.split(got, len(sent))):
                held[k ^ flip] = block
        weights.append(jnp.concatenate([held[k] for k in sorted(held)], axis=0))
        which.append(cut * halves + half)
    for step in range(1, cuts):
        ring = [(d, d - d % cuts + (d - step) % cuts) for d in range(seq_count)]
        for half in range(halves):
            weights.append(lax.ppermute(weights[half], "seq", ring))
            which.append((cut + step) % cuts * halves + half)
    tensor, of = row // heads, row % heads
    at = (of ^ head) * tensor_count + (me - tensor) % tensor_count
    return weights, which, at


def shards(hidden, depth, norm_gain, w_query, w_key, w_value, w_out):
    rows, columns = hidden.shape
    seq_count = lax.axis_size("seq")
    tensor_count = lax.axis_size("tensor")
    heads = w_query.shape[1] // HEAD
    group = seq_count // heads
    chunks = min(4, rows // (16 * group))
    chunk_rows = rows // chunks
    part = (lax.axis_index("seq") % group).astype(jnp.int32).reshape(1)
    me = lax.axis_index("tensor").astype(jnp.int32)
    gain = norm_gain.reshape(tensor_count, columns)
    active = (depth >= 2).astype(jnp.int32).reshape(rows, 1)
    made = []

    def work(found):
        first = sum(count for count, _ in made)
        here = active[first * chunk_rows : (first + len(found)) * chunk_rows]
        sent = project(
            me.reshape(1), sum(found, []), here, gain, w_query, w_key, w_value, seq_count, group
        )
        made.append((len(found), sent))
        return sent

    gathered = line_gather(
        [hidden[c * chunk_rows : (c + 1) * chunk_rows] for c in range(chunks)], tensor_count, work
    )
    for found in gathered[sum(count for count, _ in made) :]:
        work([found])
    pieces = []
    for _, sent in made:
        got = lax.all_to_all(sent, "seq", split_axis=0, concat_axis=0)
        pieces.append(got)
        for step in range(1, group):
            ring = [(d, d - d % group + (d - step) % group) for d in range(seq_count)]
            pieces.append(lax.ppermute(got, "seq", ring))

    out = attend(part, pieces, chunks, group, rows)
    weights, cut_of, at = output_weight(w_out, seq_count, tensor_count, columns, made[-1][1], out)
    scalars = jnp.stack([me, *cut_of])
    home = lax.all_to_all(out, "seq", split_axis=0, concat_axis=0)
    found = sum(line_gather([home[: seq_count // 2], home[seq_count // 2 :]], tensor_count), [])
    return output(scalars, at, found, weights, hidden, active, chunks, group, 2)


def solution(mesh):
    return jax.shard_map(
        shards,
        mesh=mesh,
        in_specs=(
            P("seq", "tensor"),
            P("seq"),
            P(),
            P(None, "tensor"),
            P(None, "tensor"),
            P(None, "tensor"),
            P("tensor", None),
        ),
        out_specs=P("seq", "tensor"),
        check_vma=False,
    )
```

```python
import math
from functools import partial

import jax
import jax.numpy as jnp
from jax import lax
from jax.experimental import pallas as pl
from jax.experimental.pallas import tpu as pltpu
from jax.sharding import PartitionSpec as P

HEAD = 128
MASKED = -1e30
ASIDE = 2.0**100
LIMIT = 60 * 2**20


def sources(me, count):
    found = [(me, None)]
    for step in range(count - 1):
        found.append((me - 1 - step, me - 1 - step >= 0))
        found.append((me + 1 + step, me + 1 + step < count))
    return found


def when(there, act):
    if there is None:
        act()
    else:
        pl.when(there)(act)


def line_gather(chunks, count, between=None):
    right = [(d, d + 1) for d in range(count - 1)]
    left = [(d + 1, d) for d in range(count - 1)]
    found, made = [], None
    for first in range(0, len(chunks), 2):
        pair = []
        for chunk in chunks[first : first + 2]:
            if first:
                chunk, _ = lax.optimization_barrier((chunk, found[first - 2]))
            pair.append([chunk])
        last = [(chunk[0], chunk[0]) for chunk in pair]
        for step in range(count - 1):
            for at in range(len(pair)):
                if step == 1 and at == 0 and made is not None:
                    last[at], _ = lax.optimization_barrier((last[at], made))
                from_left = lax.ppermute(last[at][0], "tensor", right[step:])
                from_right = lax.ppermute(last[at][1], "tensor", left[: count - 1 - step])
                last[at] = (from_left, from_right)
                pair[at] += [from_left, from_right]
        found += pair
        if between is not None and first + 2 < len(chunks):
            made = between(pair)
    return found


def project_kernel(group, count, me_ref, gain_ref, active_ref, *refs):
    matrices = refs[:3]
    pieces = refs[3:-5]
    out_ref, normed, held, piece_in, weight_in = refs[-5:]
    found = sources(me_ref[0], count)
    chunk_rows, width = pieces[0].shape
    chunks = len(pieces) // len(found)
    rows = chunks * chunk_rows

    def copy_of(number):
        chunk, (source, there) = number // len(found), found[number % len(found)]
        to = normed.at[source, chunk * chunk_rows : (chunk + 1) * chunk_rows, :]
        return there, lambda: pltpu.make_async_copy(
            pieces[number], to, piece_in.at[chunk, source]
        )

    for number in range(len(pieces)):
        there, copy = copy_of(number)
        when(there, lambda: copy().start())
    copies = [
        [
            pltpu.make_async_copy(
                matrix.at[step * width : (step + 1) * width, :],
                held.at[step, which],
                weight_in.at[step, which],
            )
            for which, matrix in enumerate(matrices)
        ]
        for step in range(count)
    ]
    for step in range(count):
        for copy in copies[step]:
            copy.start()
    for number in range(len(pieces)):
        there, copy = copy_of(number)
        when(there, lambda: copy().wait())

    square = jnp.zeros((rows, 1), jnp.float32)
    for source in range(count):
        values = normed[source].astype(jnp.float32)
        square = square + jnp.sum(values * values, axis=1, keepdims=True)
    row_scale = lax.rsqrt(square / (count * width) + 1e-05)
    for source in range(count):
        values = normed[source].astype(jnp.float32) * row_scale * gain_ref[source : source + 1, :]
        normed[source] = values.astype(jnp.bfloat16)
    part_rows = chunk_rows // group
    totals = [None] * 3
    for step in range(count):
        for which in range(3):
            copies[step][which].wait()
            product = jnp.dot(normed[step], held[step, which], preferred_element_type=jnp.float32)
            totals[which] = product if step == 0 else totals[which] + product
    for which, total in enumerate(totals):
        if which == 0:
            total = jnp.where(active_ref[...] > 0, total, ASIDE)
        total = total.astype(jnp.bfloat16)
        for head in range(total.shape[1] // HEAD):
            for part in range(group):
                for chunk in range(chunks):
                    first = chunk * chunk_rows + part * part_rows
                    out_ref[
                        head * group + part,
                        chunk * part_rows : (chunk + 1) * part_rows,
                        which * HEAD : (which + 1) * HEAD,
                    ] = total[first : first + part_rows, head * HEAD : (head + 1) * HEAD]


def project(me, pieces, active, gain, wq, wk, wv, seq_count, group):
    columns = pieces[0].shape[1]
    rows = active.shape[0]
    features, width = wq.shape
    count = features // columns
    vmem = pl.BlockSpec(memory_space=pltpu.VMEM)
    return pl.pallas_call(
        partial(project_kernel, group, count),
        in_specs=[pl.BlockSpec(memory_space=pltpu.SMEM), vmem, vmem]
        + [pl.BlockSpec(memory_space=pl.ANY)] * (3 + len(pieces)),
        out_specs=vmem,
        out_shape=jax.ShapeDtypeStruct((seq_count, rows // group, 3 * HEAD), jnp.bfloat16),
        scratch_shapes=[
            pltpu.VMEM((count, rows, columns), jnp.bfloat16),
            pltpu.VMEM((count, 3, columns, width), jnp.bfloat16),
            pltpu.SemaphoreType.DMA((rows // pieces[0].shape[0], count)),
            pltpu.SemaphoreType.DMA((count, 3)),
        ],
        compiler_params=pltpu.CompilerParams(vmem_limit_bytes=LIMIT),
        cost_estimate=pl.CostEstimate(
            flops=6 * rows * features * width,
            bytes_accessed=6 * features * width + 2 * rows * (features + 3 * width),
            transcendentals=0,
        ),
    )(me, gain, active, wq, wk, wv, *pieces)


def attend_kernel(chunks, group, rows, part_ref, *refs):
    pieces = refs[:-3]
    out_ref, keys, values = refs[-3:]
    seq_count = pieces[0].shape[0]
    chunk_rows = rows // chunks
    part_rows = chunk_rows // group
    part = part_ref[0]

    def place(home, _):
        chunk = 0
        for number in range(0, len(pieces), group):
            inside = pieces[number].shape[1] // part_rows
            for step in range(group):
                owner = lax.rem(part + step, group)
                piece = pieces[number + step]
                for at_chunk in range(inside):
                    at = home * rows + (chunk + at_chunk) * chunk_rows + owner * part_rows
                    to = pl.ds(pl.multiple_of(at, part_rows), part_rows)
                    of = slice(at_chunk * part_rows, (at_chunk + 1) * part_rows)
                    aside = piece[home, of, :HEAD].astype(jnp.float32) >= ASIDE
                    keys[to, :HEAD] = piece[home, of, HEAD : 2 * HEAD]
                    keys[to, HEAD:] = jnp.where(aside, MASKED, 0.0).astype(jnp.bfloat16)
                    values[to, :] = piece[home, of, 2 * HEAD :]
            chunk += inside
        return 0

    lax.fori_loop(0, seq_count, place, 0)
    scale = math.log2(math.e) / math.sqrt(HEAD)
    count = chunks * part_rows
    first_lane = lax.broadcasted_iota(jnp.int32, (count, HEAD), 1) == 0
    mask_lane = jnp.where(first_lane, 1.0, 0.0).astype(jnp.bfloat16)
    order = lax.broadcasted_iota(jnp.int32, (count, rows), 0)
    own = order // part_rows * chunk_rows + part * part_rows + order % part_rows
    later = lax.broadcasted_iota(jnp.int32, (count, rows), 1) > own

    def queries_of(home):
        queries = jnp.concatenate(
            [pieces[number][home, :, :HEAD] for number in range(0, len(pieces), group)], axis=0
        )
        return jnp.concatenate([queries, mask_lane], axis=1)

    def scores_of(queries, at):
        return scale * lax.dot_general(
            queries,
            keys[at, :],
            (((1,), (1,)), ((), ())),
            preferred_element_type=jnp.float32,
        )

    if seq_count <= 8:
        for home in range(seq_count):
            queries = queries_of(home)
            blocks = []
            for other in range(home + 1):
                scores = scores_of(queries, slice(other * rows, (other + 1) * rows))
                if other == home:
                    scores = jnp.where(later, MASKED, scores)
                blocks.append(scores)
            scores = jnp.concatenate(blocks, axis=1)
            best = jnp.max(scores, axis=1, keepdims=True)
            weights = jnp.exp2(scores - best)
            total = jnp.sum(weights, axis=1, keepdims=True)
            summed = jnp.dot(
                weights.astype(jnp.bfloat16),
                values[: (home + 1) * rows, :],
                preferred_element_type=jnp.float32,
            )
            out_ref[home] = (summed / total).astype(jnp.bfloat16)
        return

    def one_home(home, _):
        queries = queries_of(home)

        def fold(other, carry, diagonal):
            best, total, summed = carry
            at = pl.ds(pl.multiple_of(other * rows, rows), rows)
            scores = scores_of(queries, at)
            if diagonal:
                scores = jnp.where(later, MASKED, scores)
            newbest = jnp.maximum(best, jnp.max(scores, axis=1, keepdims=True))
            factor = jnp.exp2(best - newbest)
            weights = jnp.exp2(scores - newbest)
            total = total * factor + jnp.sum(weights, axis=1, keepdims=True)
            summed = summed * factor + jnp.dot(
                weights.astype(jnp.bfloat16), values[at, :], preferred_element_type=jnp.float32
            )
            return newbest, total, summed

        start = (
            jnp.full((count, 1), MASKED, jnp.float32),
            jnp.zeros((count, 1), jnp.float32),
            jnp.zeros((count, HEAD), jnp.float32),
        )
        carry = fold(home, start, True)
        carry = lax.fori_loop(0, home, lambda other, c: fold(other, c, False), carry)
        _, total, summed = carry
        out_ref[home] = (summed / total).astype(jnp.bfloat16)
        return 0

    lax.fori_loop(0, seq_count, one_home, 0)


def attend(part, pieces, chunks, group, rows):
    seq_count = pieces[0].shape[0]
    count = rows // group
    vmem = pl.BlockSpec(memory_space=pltpu.VMEM)
    pairs = seq_count * (seq_count + 1) // 2
    return pl.pallas_call(
        partial(attend_kernel, chunks, group, rows),
        in_specs=[pl.BlockSpec(memory_space=pltpu.SMEM)] + [vmem] * len(pieces),
        out_specs=vmem,
        out_shape=jax.ShapeDtypeStruct((seq_count, count, HEAD), jnp.bfloat16),
        scratch_shapes=[
            pltpu.VMEM((seq_count * rows, 2 * HEAD), jnp.bfloat16),
            pltpu.VMEM((seq_count * rows, HEAD), jnp.bfloat16),
        ],
        compiler_params=pltpu.CompilerParams(vmem_limit_bytes=LIMIT),
        cost_estimate=pl.CostEstimate(
            flops=6 * pairs * count * rows * HEAD,
            bytes_accessed=8 * seq_count * rows * HEAD,
            transcendentals=pairs * count * rows,
        ),
    )(part, *pieces)


def output_kernel(group, count, cuts, halves, me_ref, at_ref, active_ref, hidden_ref, *refs):
    weights = refs[:cuts]
    pieces = refs[cuts:-7]
    out_ref, rows_in, held, own, piece_in, weight_in, own_in = refs[-7:]
    heads = pieces[0].shape[0] // group
    found = sources(me_ref[0], count)
    own_copy = pltpu.make_async_copy(hidden_ref, own, own_in)
    weight_copies = [
        pltpu.make_async_copy(weight, held.at[cut], weight_in.at[cut])
        for cut, weight in enumerate(weights)
    ]

    def copies_of(number):
        half, (source, there) = number // len(found), found[number % len(found)]

        def each(act):
            for head in range(heads):
                at = pl.multiple_of(at_ref[(source * halves + half) * heads + head] * HEAD, HEAD)
                for part in range(group):
                    act(
                        pltpu.make_async_copy(
                            pieces[number].at[head * group + part],
                            rows_in.at[:, part, :, pl.ds(at, HEAD)],
                            piece_in.at[half, source, head, part],
                        )
                    )

        return there, each

    for number in range(len(pieces)):
        there, each = copies_of(number)
        when(there, lambda: each(lambda copy: copy.start()))
    weight_copies[0].start()
    own_copy.start()
    for copy in weight_copies[1:]:
        copy.start()
    for number in range(len(pieces)):
        there, each = copies_of(number)
        when(there, lambda: each(lambda copy: copy.wait()))

    rows, width = own.shape[0], held.shape[2]
    x = rows_in[...].reshape(rows, -1)
    for cut in range(cuts):
        weight_copies[cut].wait()
        columns = pl.ds(pl.multiple_of(me_ref[1 + cut] * width, width), width)
        shares = jnp.dot(x, held[cut], preferred_element_type=jnp.float32)
        if cut == 0:
            own_copy.wait()
        hidden = own[:, columns]
        renewed = (hidden.astype(jnp.float32) + shares).astype(jnp.bfloat16)
        out_ref[:, columns] = jnp.where(active_ref[...] > 0, renewed, hidden)


def output(scalars, at, pieces, weights, hidden, active, chunks, group, halves):
    rows, columns = hidden.shape
    depth, width = weights[0].shape
    cuts = len(weights)
    count = (len(pieces) // halves + 1) // 2
    part_rows = rows // chunks // group
    pieces = [piece.reshape(-1, chunks, part_rows, HEAD) for piece in pieces]
    smem = pl.BlockSpec(memory_space=pltpu.SMEM)
    vmem = pl.BlockSpec(memory_space=pltpu.VMEM)
    return pl.pallas_call(
        partial(output_kernel, group, count, cuts, halves),
        in_specs=[smem, smem, vmem]
        + [pl.BlockSpec(memory_space=pl.ANY)] * (1 + cuts + len(pieces)),
        out_specs=vmem,
        out_shape=jax.ShapeDtypeStruct((rows, columns), jnp.bfloat16),
        scratch_shapes=[
            pltpu.VMEM((chunks, group, part_rows, depth), jnp.bfloat16),
            pltpu.VMEM((cuts, depth, width), jnp.bfloat16),
            pltpu.VMEM((rows, columns), jnp.bfloat16),
            pltpu.SemaphoreType.DMA((halves, count, pieces[0].shape[0] // group, group)),
            pltpu.SemaphoreType.DMA((cuts,)),
            pltpu.SemaphoreType.DMA,
        ],
        compiler_params=pltpu.CompilerParams(vmem_limit_bytes=LIMIT),
        cost_estimate=pl.CostEstimate(
            flops=2 * rows * depth * columns,
            bytes_accessed=2 * (rows * depth + depth * columns + 2 * rows * columns),
            transcendentals=0,
        ),
    )(scalars, at, active, hidden, *weights, *pieces)


def share_kernel(place_ref, w_ref, *shares):
    for step, share in enumerate(shares):

        @pl.when(pl.program_id(0) == step)
        def _():
            each = share.shape[2]
            for half in range(share.shape[0]):
                share[half] = w_ref[:, half * each : (half + 1) * each]


def shares_of(w_out, place, count, halves, each):
    width = halves * each
    cuts = w_out.shape[1] // count // width
    return pl.pallas_call(
        share_kernel,
        grid_spec=pltpu.PrefetchScalarGridSpec(
            num_scalar_prefetch=1,
            grid=(count,),
            in_specs=[
                pl.BlockSpec(
                    (HEAD, width),
                    lambda j, place: (place[0], lax.rem(place[2] + j, count) * cuts + place[1]),
                )
            ],
            out_specs=[pl.BlockSpec((halves, HEAD, each), lambda j, place: (0, 0, 0))] * count,
        ),
        out_shape=[jax.ShapeDtypeStruct((halves, HEAD, each), w_out.dtype)] * count,
        compiler_params=pltpu.CompilerParams(vmem_limit_bytes=LIMIT),
    )(place, w_out)


def weight_cuts(w_out, seq_count, columns):
    heads = w_out.shape[0] // HEAD
    cuts = seq_count // heads
    width = columns // cuts
    halves = 2 if width % (2 * HEAD) == 0 else 1
    return heads, cuts, halves, width // halves


def weight_shares(w_out, seq_count, tensor_count, columns):
    heads, cuts, halves, each = weight_cuts(w_out, seq_count, columns)
    if each % HEAD:
        return None
    seq_me = lax.axis_index("seq").astype(jnp.int32)
    me = lax.axis_index("tensor").astype(jnp.int32)
    place = jnp.stack([seq_me // cuts, seq_me % cuts, me])
    return list(shares_of(w_out, place, tensor_count, halves, each))


def send_shares(shares, tensor_count, after):
    if shares is None:
        return None
    shares, _ = lax.optimization_barrier((list(shares), after))
    for step in range(1, tensor_count):
        ring = [(d, (d + step) % tensor_count) for d in range(tensor_count)]
        shares[step] = lax.ppermute(shares[step], "tensor", ring)
    return shares


def output_weight(w_out, shares, seq_count, tensor_count, columns, after):
    heads, cuts, halves, each = weight_cuts(w_out, seq_count, columns)
    row = jnp.arange(tensor_count * heads, dtype=jnp.int32)
    if shares is None:
        weight = lax.all_to_all(w_out, "tensor", split_axis=1, concat_axis=0, tiled=True)
        return [weight], [jnp.int32(0)], row
    seq_me = lax.axis_index("seq").astype(jnp.int32)
    me = lax.axis_index("tensor").astype(jnp.int32)
    head, cut = seq_me // cuts, seq_me % cuts
    flips = []
    while cuts << len(flips) < seq_count:
        flips.append(cuts << len(flips))
    shares, _ = lax.optimization_barrier((shares, after))
    weights, which = [], []
    for half in range(halves):
        held = {0: jnp.concatenate([share[half] for share in shares], axis=0)}
        for flip in flips if half == 0 else flips[::-1]:
            pairs = [(d, d ^ flip) for d in range(seq_count)]
            sent = list(held)
            got = lax.ppermute(jnp.concatenate([held[k] for k in sent], axis=0), "seq", pairs)
            for k, block in zip(sent, jnp.split(got, len(sent))):
                held[k ^ flip] = block
        weights.append(jnp.concatenate([held[k] for k in sorted(held)], axis=0))
        which.append(cut * halves + half)
    for step in range(1, cuts):
        ring = [(d, d - d % cuts + (d - step) % cuts) for d in range(seq_count)]
        for half in range(halves):
            weights.append(lax.ppermute(weights[half], "seq", ring))
            which.append((cut + step) % cuts * halves + half)
    tensor, of = row // heads, row % heads
    at = (of ^ head) * tensor_count + (me - tensor) % tensor_count
    return weights, which, at


def shards(hidden, depth, norm_gain, w_query, w_key, w_value, w_out):
    rows, columns = hidden.shape
    seq_count = lax.axis_size("seq")
    tensor_count = lax.axis_size("tensor")
    heads = w_query.shape[1] // HEAD
    group = seq_count // heads
    chunks = min(4, rows // (16 * group))
    chunk_rows = rows // chunks
    part = (lax.axis_index("seq") % group).astype(jnp.int32).reshape(1)
    me = lax.axis_index("tensor").astype(jnp.int32)
    gain = norm_gain.reshape(tensor_count, columns)
    active = (depth >= 2).astype(jnp.int32).reshape(rows, 1)
    made = []
    shares = weight_shares(w_out, seq_count, tensor_count, columns)

    def work(found):
        first = sum(count for count, _ in made)
        here = active[first * chunk_rows : (first + len(found)) * chunk_rows]
        sent = project(
            me.reshape(1), sum(found, []), here, gain, w_query, w_key, w_value, seq_count, group
        )
        made.append((len(found), sent))
        return sent, shares

    gathered = line_gather(
        [hidden[c * chunk_rows : (c + 1) * chunk_rows] for c in range(chunks)], tensor_count, work
    )
    rest = gathered[sum(count for count, _ in made) :]
    sending = send_shares(shares, tensor_count, rest[-1])
    work(rest)
    pieces = []
    for _, sent in made:
        got = lax.all_to_all(sent, "seq", split_axis=0, concat_axis=0)
        pieces.append(got)
        for step in range(1, group):
            ring = [(d, d - d % group + (d - step) % group) for d in range(seq_count)]
            pieces.append(lax.ppermute(got, "seq", ring))

    pieces[-1], sending = lax.optimization_barrier((pieces[-1], sending))
    out = attend(part, pieces, chunks, group, rows)
    home = lax.all_to_all(out, "seq", split_axis=0, concat_axis=0)
    found = line_gather([home[: seq_count // 2], home[seq_count // 2 :]], tensor_count)
    weights, cut_of, at = output_weight(
        w_out, sending, seq_count, tensor_count, columns, [pieces[1:3] for pieces in found]
    )
    scalars = jnp.stack([me, *cut_of])
    return output(scalars, at, sum(found, []), weights, hidden, active, chunks, group, 2)


def solution(mesh):
    return jax.shard_map(
        shards,
        mesh=mesh,
        in_specs=(
            P("seq", "tensor"),
            P("seq"),
            P(),
            P(None, "tensor"),
            P(None, "tensor"),
            P(None, "tensor"),
            P("tensor", None),
        ),
        out_specs=P("seq", "tensor"),
        check_vma=False,
    )
```

```python
import math
from functools import partial

import jax
import jax.numpy as jnp
from jax import lax
from jax.experimental import pallas as pl
from jax.experimental.pallas import tpu as pltpu
from jax.sharding import PartitionSpec as P

HEAD = 128
MASKED = -1e30
ASIDE = 2.0**100
LIMIT = 60 * 2**20


def sources(me, count):
    found = [(me, None)]
    for step in range(count - 1):
        found.append((me - 1 - step, me - 1 - step >= 0))
        found.append((me + 1 + step, me + 1 + step < count))
    return found


def when(there, act):
    if there is None:
        act()
    else:
        pl.when(there)(act)


def line_gather(chunks, count, join=None):
    right = [(d, d + 1) for d in range(count - 1)]
    left = [(d + 1, d) for d in range(count - 1)]
    found = []
    for first in range(0, len(chunks), 2):
        pair = []
        for chunk in chunks[first : first + 2]:
            if first:
                chunk, _ = lax.optimization_barrier((chunk, found[first - 2]))
            pair.append([chunk])
        last = [(chunk[0], chunk[0]) for chunk in pair]
        for step in range(count - 1):
            if join is not None:
                last = join(first, step, last, found)
            for at in range(len(pair)):
                from_left = lax.ppermute(last[at][0], "tensor", right[step:])
                from_right = lax.ppermute(last[at][1], "tensor", left[: count - 1 - step])
                last[at] = (from_left, from_right)
                pair[at] += [from_left, from_right]
        found += pair
    return found


def project_kernel(group, count, me_ref, gain_ref, active_ref, *refs):
    matrices = refs[:3]
    pieces = refs[3:-5]
    out_ref, normed, held, piece_in, weight_in = refs[-5:]
    found = sources(me_ref[0], count)
    chunk_rows, width = pieces[0].shape
    chunks = len(pieces) // len(found)
    rows = chunks * chunk_rows

    def copy_of(number):
        chunk, (source, there) = number // len(found), found[number % len(found)]
        to = normed.at[source, chunk * chunk_rows : (chunk + 1) * chunk_rows, :]
        return there, lambda: pltpu.make_async_copy(
            pieces[number], to, piece_in.at[chunk, source]
        )

    for number in range(len(pieces)):
        there, copy = copy_of(number)
        when(there, lambda: copy().start())
    copies = [
        [
            pltpu.make_async_copy(
                matrix.at[step * width : (step + 1) * width, :],
                held.at[step, which],
                weight_in.at[step, which],
            )
            for which, matrix in enumerate(matrices)
        ]
        for step in range(count)
    ]
    for step in range(count):
        for copy in copies[step]:
            copy.start()
    for number in range(len(pieces)):
        there, copy = copy_of(number)
        when(there, lambda: copy().wait())

    square = jnp.zeros((rows, 1), jnp.float32)
    for source in range(count):
        values = normed[source].astype(jnp.float32)
        square = square + jnp.sum(values * values, axis=1, keepdims=True)
    row_scale = lax.rsqrt(square / (count * width) + 1e-05)
    for source in range(count):
        values = normed[source].astype(jnp.float32) * row_scale * gain_ref[source : source + 1, :]
        normed[source] = values.astype(jnp.bfloat16)
    part_rows = chunk_rows // group
    totals = [None] * 3
    for step in range(count):
        for which in range(3):
            copies[step][which].wait()
            product = jnp.dot(normed[step], held[step, which], preferred_element_type=jnp.float32)
            totals[which] = product if step == 0 else totals[which] + product
    for which, total in enumerate(totals):
        if which == 0:
            total = jnp.where(active_ref[...] > 0, total, ASIDE)
        total = total.astype(jnp.bfloat16)
        for head in range(total.shape[1] // HEAD):
            for part in range(group):
                for chunk in range(chunks):
                    first = chunk * chunk_rows + part * part_rows
                    out_ref[
                        head * group + part,
                        chunk * part_rows : (chunk + 1) * part_rows,
                        which * HEAD : (which + 1) * HEAD,
                    ] = total[first : first + part_rows, head * HEAD : (head + 1) * HEAD]


def project(me, pieces, active, gain, wq, wk, wv, seq_count, group):
    columns = pieces[0].shape[1]
    rows = active.shape[0]
    features, width = wq.shape
    count = features // columns
    vmem = pl.BlockSpec(memory_space=pltpu.VMEM)
    return pl.pallas_call(
        partial(project_kernel, group, count),
        in_specs=[pl.BlockSpec(memory_space=pltpu.SMEM), vmem, vmem]
        + [pl.BlockSpec(memory_space=pl.ANY)] * (3 + len(pieces)),
        out_specs=vmem,
        out_shape=jax.ShapeDtypeStruct((seq_count, rows // group, 3 * HEAD), jnp.bfloat16),
        scratch_shapes=[
            pltpu.VMEM((count, rows, columns), jnp.bfloat16),
            pltpu.VMEM((count, 3, columns, width), jnp.bfloat16),
            pltpu.SemaphoreType.DMA((rows // pieces[0].shape[0], count)),
            pltpu.SemaphoreType.DMA((count, 3)),
        ],
        compiler_params=pltpu.CompilerParams(vmem_limit_bytes=LIMIT),
        cost_estimate=pl.CostEstimate(
            flops=6 * rows * features * width,
            bytes_accessed=6 * features * width + 2 * rows * (features + 3 * width),
            transcendentals=0,
        ),
    )(me, gain, active, wq, wk, wv, *pieces)


def attend_kernel(chunks, group, rows, part_ref, *refs):
    pieces = refs[:-3]
    out_ref, keys, values = refs[-3:]
    seq_count = pieces[0].shape[0]
    chunk_rows = rows // chunks
    part_rows = chunk_rows // group
    part = part_ref[0]

    def place(home, _):
        chunk = 0
        for number in range(0, len(pieces), group):
            inside = pieces[number].shape[1] // part_rows
            for step in range(group):
                owner = lax.rem(part + step, group)
                piece = pieces[number + step]
                for at_chunk in range(inside):
                    at = home * rows + (chunk + at_chunk) * chunk_rows + owner * part_rows
                    to = pl.ds(pl.multiple_of(at, part_rows), part_rows)
                    of = slice(at_chunk * part_rows, (at_chunk + 1) * part_rows)
                    aside = piece[home, of, :HEAD].astype(jnp.float32) >= ASIDE
                    keys[to, :HEAD] = piece[home, of, HEAD : 2 * HEAD]
                    keys[to, HEAD:] = jnp.where(aside, MASKED, 0.0).astype(jnp.bfloat16)
                    values[to, :] = piece[home, of, 2 * HEAD :]
            chunk += inside
        return 0

    lax.fori_loop(0, seq_count, place, 0)
    scale = math.log2(math.e) / math.sqrt(HEAD)
    count = chunks * part_rows
    first_lane = lax.broadcasted_iota(jnp.int32, (count, HEAD), 1) == 0
    mask_lane = jnp.where(first_lane, 1.0, 0.0).astype(jnp.bfloat16)
    order = lax.broadcasted_iota(jnp.int32, (count, rows), 0)
    own = order // part_rows * chunk_rows + part * part_rows + order % part_rows
    later = lax.broadcasted_iota(jnp.int32, (count, rows), 1) > own

    def queries_of(home):
        queries = jnp.concatenate(
            [pieces[number][home, :, :HEAD] for number in range(0, len(pieces), group)], axis=0
        )
        return jnp.concatenate([queries, mask_lane], axis=1)

    def scores_of(queries, at):
        return scale * lax.dot_general(
            queries,
            keys[at, :],
            (((1,), (1,)), ((), ())),
            preferred_element_type=jnp.float32,
        )

    if seq_count <= 8:
        for home in range(seq_count):
            queries = queries_of(home)
            blocks = []
            for other in range(home + 1):
                scores = scores_of(queries, slice(other * rows, (other + 1) * rows))
                if other == home:
                    scores = jnp.where(later, MASKED, scores)
                blocks.append(scores)
            scores = jnp.concatenate(blocks, axis=1)
            best = jnp.max(scores, axis=1, keepdims=True)
            weights = jnp.exp2(scores - best)
            total = jnp.sum(weights, axis=1, keepdims=True)
            summed = jnp.dot(
                weights.astype(jnp.bfloat16),
                values[: (home + 1) * rows, :],
                preferred_element_type=jnp.float32,
            )
            out_ref[home] = (summed / total).astype(jnp.bfloat16)
        return

    def one_home(home, _):
        queries = queries_of(home)

        def fold(other, carry, diagonal):
            best, total, summed = carry
            at = pl.ds(pl.multiple_of(other * rows, rows), rows)
            scores = scores_of(queries, at)
            if diagonal:
                scores = jnp.where(later, MASKED, scores)
            newbest = jnp.maximum(best, jnp.max(scores, axis=1, keepdims=True))
            factor = jnp.exp2(best - newbest)
            weights = jnp.exp2(scores - newbest)
            total = total * factor + jnp.sum(weights, axis=1, keepdims=True)
            summed = summed * factor + jnp.dot(
                weights.astype(jnp.bfloat16), values[at, :], preferred_element_type=jnp.float32
            )
            return newbest, total, summed

        start = (
            jnp.full((count, 1), MASKED, jnp.float32),
            jnp.zeros((count, 1), jnp.float32),
            jnp.zeros((count, HEAD), jnp.float32),
        )
        carry = fold(home, start, True)
        carry = lax.fori_loop(0, home, lambda other, c: fold(other, c, False), carry)
        _, total, summed = carry
        out_ref[home] = (summed / total).astype(jnp.bfloat16)
        return 0

    lax.fori_loop(0, seq_count, one_home, 0)


def attend(part, pieces, chunks, group, rows):
    seq_count = pieces[0].shape[0]
    count = rows // group
    vmem = pl.BlockSpec(memory_space=pltpu.VMEM)
    pairs = seq_count * (seq_count + 1) // 2
    return pl.pallas_call(
        partial(attend_kernel, chunks, group, rows),
        in_specs=[pl.BlockSpec(memory_space=pltpu.SMEM)] + [vmem] * len(pieces),
        out_specs=vmem,
        out_shape=jax.ShapeDtypeStruct((seq_count, count, HEAD), jnp.bfloat16),
        scratch_shapes=[
            pltpu.VMEM((seq_count * rows, 2 * HEAD), jnp.bfloat16),
            pltpu.VMEM((seq_count * rows, HEAD), jnp.bfloat16),
        ],
        compiler_params=pltpu.CompilerParams(vmem_limit_bytes=LIMIT),
        cost_estimate=pl.CostEstimate(
            flops=6 * pairs * count * rows * HEAD,
            bytes_accessed=8 * seq_count * rows * HEAD,
            transcendentals=pairs * count * rows,
        ),
    )(part, *pieces)


def output_kernel(group, count, cuts, halves, me_ref, at_ref, active_ref, hidden_ref, *refs):
    weights = refs[:cuts]
    pieces = refs[cuts:-7]
    out_ref, rows_in, held, own, piece_in, weight_in, own_in = refs[-7:]
    heads = pieces[0].shape[0] // group
    found = sources(me_ref[0], count)
    own_copy = pltpu.make_async_copy(hidden_ref, own, own_in)
    weight_copies = [
        pltpu.make_async_copy(weight, held.at[cut], weight_in.at[cut])
        for cut, weight in enumerate(weights)
    ]

    def copies_of(number):
        half, (source, there) = number // len(found), found[number % len(found)]

        def each(act):
            for head in range(heads):
                at = pl.multiple_of(at_ref[(source * halves + half) * heads + head] * HEAD, HEAD)
                for part in range(group):
                    act(
                        pltpu.make_async_copy(
                            pieces[number].at[head * group + part],
                            rows_in.at[:, part, :, pl.ds(at, HEAD)],
                            piece_in.at[half, source, head, part],
                        )
                    )

        return there, each

    for number in range(len(pieces)):
        there, each = copies_of(number)
        when(there, lambda: each(lambda copy: copy.start()))
    weight_copies[0].start()
    own_copy.start()
    for copy in weight_copies[1:]:
        copy.start()
    for number in range(len(pieces)):
        there, each = copies_of(number)
        when(there, lambda: each(lambda copy: copy.wait()))

    rows, width = own.shape[0], held.shape[2]
    x = rows_in[...].reshape(rows, -1)
    for cut in range(cuts):
        weight_copies[cut].wait()
        columns = pl.ds(pl.multiple_of(me_ref[1 + cut] * width, width), width)
        shares = jnp.dot(x, held[cut], preferred_element_type=jnp.float32)
        if cut == 0:
            own_copy.wait()
        hidden = own[:, columns]
        renewed = (hidden.astype(jnp.float32) + shares).astype(jnp.bfloat16)
        out_ref[:, columns] = jnp.where(active_ref[...] > 0, renewed, hidden)


def output(scalars, at, pieces, weights, hidden, active, chunks, group, halves):
    rows, columns = hidden.shape
    depth, width = weights[0].shape
    cuts = len(weights)
    count = (len(pieces) // halves + 1) // 2
    part_rows = rows // chunks // group
    pieces = [piece.reshape(-1, chunks, part_rows, HEAD) for piece in pieces]
    smem = pl.BlockSpec(memory_space=pltpu.SMEM)
    vmem = pl.BlockSpec(memory_space=pltpu.VMEM)
    return pl.pallas_call(
        partial(output_kernel, group, count, cuts, halves),
        in_specs=[smem, smem, vmem]
        + [pl.BlockSpec(memory_space=pl.ANY)] * (1 + cuts + len(pieces)),
        out_specs=vmem,
        out_shape=jax.ShapeDtypeStruct((rows, columns), jnp.bfloat16),
        scratch_shapes=[
            pltpu.VMEM((chunks, group, part_rows, depth), jnp.bfloat16),
            pltpu.VMEM((cuts, depth, width), jnp.bfloat16),
            pltpu.VMEM((rows, columns), jnp.bfloat16),
            pltpu.SemaphoreType.DMA((halves, count, pieces[0].shape[0] // group, group)),
            pltpu.SemaphoreType.DMA((cuts,)),
            pltpu.SemaphoreType.DMA,
        ],
        compiler_params=pltpu.CompilerParams(vmem_limit_bytes=LIMIT),
        cost_estimate=pl.CostEstimate(
            flops=2 * rows * depth * columns,
            bytes_accessed=2 * (rows * depth + depth * columns + 2 * rows * columns),
            transcendentals=0,
        ),
    )(scalars, at, active, hidden, *weights, *pieces)


def share_kernel(place_ref, w_ref, *shares):
    for step, share in enumerate(shares):

        @pl.when(pl.program_id(0) == step)
        def _():
            each = share.shape[2]
            for half in range(share.shape[0]):
                share[half] = w_ref[:, half * each : (half + 1) * each]


def shares_of(w_out, place, count, halves, each):
    width = halves * each
    cuts = w_out.shape[1] // count // width
    return pl.pallas_call(
        share_kernel,
        grid_spec=pltpu.PrefetchScalarGridSpec(
            num_scalar_prefetch=1,
            grid=(count,),
            in_specs=[
                pl.BlockSpec(
                    (HEAD, width),
                    lambda j, place: (place[0], lax.rem(place[2] + j, count) * cuts + place[1]),
                )
            ],
            out_specs=[pl.BlockSpec((halves, HEAD, each), lambda j, place: (0, 0, 0))] * count,
        ),
        out_shape=[jax.ShapeDtypeStruct((halves, HEAD, each), w_out.dtype)] * count,
        compiler_params=pltpu.CompilerParams(vmem_limit_bytes=LIMIT),
    )(place, w_out)


def weight_cuts(w_out, seq_count, columns):
    heads = w_out.shape[0] // HEAD
    cuts = seq_count // heads
    width = columns // cuts
    halves = 2 if width % (2 * HEAD) == 0 else 1
    return heads, cuts, halves, width // halves


def weight_shares(w_out, seq_count, tensor_count, columns):
    heads, cuts, halves, each = weight_cuts(w_out, seq_count, columns)
    if each % HEAD:
        return None
    seq_me = lax.axis_index("seq").astype(jnp.int32)
    me = lax.axis_index("tensor").astype(jnp.int32)
    place = jnp.stack([seq_me // cuts, seq_me % cuts, me])
    return list(shares_of(w_out, place, tensor_count, halves, each))


def send_shares(shares, tensor_count, after):
    if shares is None:
        return None
    shares, _ = lax.optimization_barrier((list(shares), after))
    for step in range(1, tensor_count):
        ring = [(d, (d + step) % tensor_count) for d in range(tensor_count)]
        shares[step] = lax.ppermute(shares[step], "tensor", ring)
    return shares


def swap(held, flips):
    grown = []
    for blocks, flip in zip(held, flips):
        pairs = [(d, d ^ flip) for d in range(lax.axis_size("seq"))]
        sent = list(blocks)
        whole = [blocks[k] for k in sent]
        got = lax.ppermute(
            jnp.concatenate(whole, axis=0) if len(whole) > 1 else whole[0], "seq", pairs
        )
        grown.append(dict(blocks))
        for k, block in zip(sent, jnp.split(got, len(sent))):
            grown[-1][k ^ flip] = block
    return grown


def output_order(w_out, seq_count, tensor_count, columns):
    heads, cuts, halves, each = weight_cuts(w_out, seq_count, columns)
    row = jnp.arange(tensor_count * heads, dtype=jnp.int32)
    if each % HEAD:
        return [jnp.int32(0)], row
    seq_me = lax.axis_index("seq").astype(jnp.int32)
    me = lax.axis_index("tensor").astype(jnp.int32)
    which = [
        (seq_me % cuts + step) % cuts * halves + half for step in range(cuts) for half in range(halves)
    ]
    tensor, of = row // heads, row % heads
    return which, (of ^ (seq_me // cuts)) * tensor_count + (me - tensor) % tensor_count


def shards(hidden, depth, norm_gain, w_query, w_key, w_value, w_out):
    rows, columns = hidden.shape
    seq_count = lax.axis_size("seq")
    tensor_count = lax.axis_size("tensor")
    heads = w_query.shape[1] // HEAD
    group = seq_count // heads
    chunks = min(4, rows // (16 * group))
    chunk_rows = rows // chunks
    part = (lax.axis_index("seq") % group).astype(jnp.int32).reshape(1)
    me = lax.axis_index("tensor").astype(jnp.int32)
    gain = norm_gain.reshape(tensor_count, columns)
    active = (depth >= 2).astype(jnp.int32).reshape(rows, 1)
    made = []
    shares = weight_shares(w_out, seq_count, tensor_count, columns)

    def work(found):
        first = chunks - len(found) if made else 0
        here = active[first * chunk_rows : (first + len(found)) * chunk_rows]
        return project(
            me.reshape(1), sum(found, []), here, gain, w_query, w_key, w_value, seq_count, group
        )

    def to_heads(sent):
        return lax.all_to_all(sent, "seq", split_axis=0, concat_axis=0)

    def to_parts(got):
        rings = [
            [(d, d - d % group + (d - step) % group) for d in range(seq_count)]
            for step in range(1, group)
        ]
        return [got] + [lax.ppermute(got, "seq", ring) for ring in rings]

    def first_pair(first, step, last, found):
        if first == 2 and step == 1:
            last, sent, _ = lax.optimization_barrier((last, work(found[:2]), shares))
            made.append(to_heads(sent))
        if first == 2 and step == 2:
            got, last = lax.optimization_barrier((made.pop(), last))
            made.extend(to_parts(got))
        return last

    gathered = line_gather(
        [hidden[c * chunk_rows : (c + 1) * chunk_rows] for c in range(chunks)],
        tensor_count,
        first_pair,
    )
    rest = gathered[-2:]
    sending = send_shares(shares, tensor_count, rest[-1])
    sent = work(rest)
    sent, sending, made = lax.optimization_barrier((sent, sending, made))
    pieces = list(made) + to_parts(to_heads(sent))

    heads, cuts, halves, _ = weight_cuts(w_out, seq_count, columns)
    held, flips = [], []
    if sending is not None:
        held = [
            {0: jnp.concatenate([share[half] for share in sending], axis=0)}
            for half in range(halves)
        ]
        while cuts << len(flips) < seq_count:
            flips.append(cuts << len(flips))
        held = swap(held, [flips[0], flips[-1]])
    out = attend(part, pieces, chunks, group, rows)
    out, held = lax.optimization_barrier((out, held))
    home = lax.all_to_all(out, "seq", split_axis=0, concat_axis=0)
    home, held = lax.optimization_barrier((home, held))

    def spread(first, step, last, found):
        nonlocal held
        if held and 0 < step < len(flips):
            last, held = lax.optimization_barrier(
                (last, swap(held, [flips[step], flips[-1 - step]]))
            )
        return last

    found = line_gather([home[: seq_count // 2], home[seq_count // 2 :]], tensor_count, spread)
    weights = [jnp.concatenate([blocks[k] for k in sorted(blocks)], axis=0) for blocks in held]
    for turn in range(1, cuts):
        ring = [(d, d - d % cuts + (d - turn) % cuts) for d in range(seq_count)]
        weights += [lax.ppermute(weights[half], "seq", ring) for half in range(len(held))]
    if not held:
        weights = [lax.all_to_all(w_out, "tensor", split_axis=1, concat_axis=0, tiled=True)]
    cut_of, at = output_order(w_out, seq_count, tensor_count, columns)
    scalars = jnp.stack([me, *cut_of])
    return output(scalars, at, sum(found, []), weights, hidden, active, chunks, group, 2)


def solution(mesh):
    return jax.shard_map(
        shards,
        mesh=mesh,
        in_specs=(
            P("seq", "tensor"),
            P("seq"),
            P(),
            P(None, "tensor"),
            P(None, "tensor"),
            P(None, "tensor"),
            P("tensor", None),
        ),
        out_specs=P("seq", "tensor"),
        check_vma=False,
    )
```

```python
import math
from functools import partial

import jax
import jax.numpy as jnp
from jax import lax
from jax.experimental import pallas as pl
from jax.experimental.pallas import tpu as pltpu
from jax.sharding import PartitionSpec as P

HEAD = 128
MASKED = -1e30
ASIDE = 2.0**100
LIMIT = 63 * 2**20


def sources(me, count):
    found = [(me, None)]
    for step in range(count - 1):
        found.append((me - 1 - step, me - 1 - step >= 0))
        found.append((me + 1 + step, me + 1 + step < count))
    return found


def when(there, act):
    if there is None:
        act()
    else:
        pl.when(there)(act)


def line_gather(chunks, count, join=None):
    right = [(d, d + 1) for d in range(count - 1)]
    left = [(d + 1, d) for d in range(count - 1)]
    found = []
    for first in range(0, len(chunks), 2):
        pair = []
        for chunk in chunks[first : first + 2]:
            if first:
                chunk, _ = lax.optimization_barrier((chunk, found[first - 2]))
            pair.append([chunk])
        last = [(chunk[0], chunk[0]) for chunk in pair]
        for step in range(count - 1):
            if join is not None:
                last = join(first, step, last, found)
            for at in range(len(pair)):
                from_left = lax.ppermute(last[at][0], "tensor", right[step:])
                from_right = lax.ppermute(last[at][1], "tensor", left[: count - 1 - step])
                last[at] = (from_left, from_right)
                pair[at] += [from_left, from_right]
        found += pair
    return found


def project_kernel(group, count, me_ref, gain_ref, active_ref, *refs):
    matrices = refs[:3]
    pieces = refs[3:-5]
    out_ref, normed, held, piece_in, weight_in = refs[-5:]
    found = sources(me_ref[0], count)
    chunk_rows, width = pieces[0].shape
    chunks = len(pieces) // len(found)
    rows = chunks * chunk_rows

    def copy_of(number):
        chunk, (source, there) = number // len(found), found[number % len(found)]
        to = normed.at[source, chunk * chunk_rows : (chunk + 1) * chunk_rows, :]
        return there, lambda: pltpu.make_async_copy(
            pieces[number], to, piece_in.at[chunk, source]
        )

    for number in range(len(pieces)):
        there, copy = copy_of(number)
        when(there, lambda: copy().start())
    copies = [
        [
            pltpu.make_async_copy(
                matrix.at[step * width : (step + 1) * width, :],
                held.at[step, which],
                weight_in.at[step, which],
            )
            for which, matrix in enumerate(matrices)
        ]
        for step in range(count)
    ]
    for step in range(count):
        for copy in copies[step]:
            copy.start()
    for number in range(len(pieces)):
        there, copy = copy_of(number)
        when(there, lambda: copy().wait())

    square = jnp.zeros((rows, 1), jnp.float32)
    for source in range(count):
        values = normed[source].astype(jnp.float32)
        square = square + jnp.sum(values * values, axis=1, keepdims=True)
    row_scale = lax.rsqrt(square / (count * width) + 1e-05)
    for source in range(count):
        values = normed[source].astype(jnp.float32) * row_scale * gain_ref[source : source + 1, :]
        normed[source] = values.astype(jnp.bfloat16)
    part_rows = chunk_rows // group
    totals = [None] * 3
    for step in range(count):
        for which in range(3):
            copies[step][which].wait()
            product = jnp.dot(normed[step], held[step, which], preferred_element_type=jnp.float32)
            totals[which] = product if step == 0 else totals[which] + product
    for which, total in enumerate(totals):
        if which == 0:
            total = jnp.where(active_ref[...] > 0, total, ASIDE)
        total = total.astype(jnp.bfloat16)
        for head in range(total.shape[1] // HEAD):
            for part in range(group):
                for chunk in range(chunks):
                    first = chunk * chunk_rows + part * part_rows
                    out_ref[
                        head * group + part,
                        chunk * part_rows : (chunk + 1) * part_rows,
                        which * HEAD : (which + 1) * HEAD,
                    ] = total[first : first + part_rows, head * HEAD : (head + 1) * HEAD]


def project(me, pieces, active, gain, wq, wk, wv, seq_count, group):
    columns = pieces[0].shape[1]
    rows = active.shape[0]
    features, width = wq.shape
    count = features // columns
    vmem = pl.BlockSpec(memory_space=pltpu.VMEM)
    return pl.pallas_call(
        partial(project_kernel, group, count),
        in_specs=[pl.BlockSpec(memory_space=pltpu.SMEM), vmem, vmem]
        + [pl.BlockSpec(memory_space=pl.ANY)] * (3 + len(pieces)),
        out_specs=vmem,
        out_shape=jax.ShapeDtypeStruct((seq_count, rows // group, 3 * HEAD), jnp.bfloat16),
        scratch_shapes=[
            pltpu.VMEM((count, rows, columns), jnp.bfloat16),
            pltpu.VMEM((count, 3, columns, width), jnp.bfloat16),
            pltpu.SemaphoreType.DMA((rows // pieces[0].shape[0], count)),
            pltpu.SemaphoreType.DMA((count, 3)),
        ],
        compiler_params=pltpu.CompilerParams(vmem_limit_bytes=LIMIT),
        cost_estimate=pl.CostEstimate(
            flops=6 * rows * features * width,
            bytes_accessed=6 * features * width + 2 * rows * (features + 3 * width),
            transcendentals=0,
        ),
    )(me, gain, active, wq, wk, wv, *pieces)


def attend_kernel(chunks, group, rows, part_ref, *refs):
    pieces = refs[:-3]
    out_ref, keys, values = refs[-3:]
    seq_count = pieces[0].shape[0]
    chunk_rows = rows // chunks
    part_rows = chunk_rows // group
    part = part_ref[0]

    def place(home, _):
        chunk = 0
        for number in range(0, len(pieces), group):
            inside = pieces[number].shape[1] // part_rows
            for step in range(group):
                owner = lax.rem(part + step, group)
                piece = pieces[number + step]
                for at_chunk in range(inside):
                    at = home * rows + (chunk + at_chunk) * chunk_rows + owner * part_rows
                    to = pl.ds(pl.multiple_of(at, part_rows), part_rows)
                    of = slice(at_chunk * part_rows, (at_chunk + 1) * part_rows)
                    aside = piece[home, of, :HEAD].astype(jnp.float32) >= ASIDE
                    keys[to, :HEAD] = piece[home, of, HEAD : 2 * HEAD]
                    keys[to, HEAD:] = jnp.where(aside, MASKED, 0.0).astype(jnp.bfloat16)
                    values[to, :] = piece[home, of, 2 * HEAD :]
            chunk += inside
        return 0

    lax.fori_loop(0, seq_count, place, 0)
    scale = math.log2(math.e) / math.sqrt(HEAD)
    count = chunks * part_rows
    first_lane = lax.broadcasted_iota(jnp.int32, (count, HEAD), 1) == 0
    mask_lane = jnp.where(first_lane, 1.0, 0.0).astype(jnp.bfloat16)
    order = lax.broadcasted_iota(jnp.int32, (count, rows), 0)
    own = order // part_rows * chunk_rows + part * part_rows + order % part_rows
    later = lax.broadcasted_iota(jnp.int32, (count, rows), 1) > own

    def queries_of(home):
        queries = jnp.concatenate(
            [pieces[number][home, :, :HEAD] for number in range(0, len(pieces), group)], axis=0
        )
        return jnp.concatenate([queries, mask_lane], axis=1)

    def scores_of(queries, at):
        return scale * lax.dot_general(
            queries,
            keys[at, :],
            (((1,), (1,)), ((), ())),
            preferred_element_type=jnp.float32,
        )

    if seq_count <= 8:
        for home in range(seq_count):
            queries = queries_of(home)
            blocks = []
            for other in range(home + 1):
                scores = scores_of(queries, slice(other * rows, (other + 1) * rows))
                if other == home:
                    scores = jnp.where(later, MASKED, scores)
                blocks.append(scores)
            scores = jnp.concatenate(blocks, axis=1)
            best = jnp.max(scores, axis=1, keepdims=True)
            weights = jnp.exp2(scores - best)
            total = jnp.sum(weights, axis=1, keepdims=True)
            summed = jnp.dot(
                weights.astype(jnp.bfloat16),
                values[: (home + 1) * rows, :],
                preferred_element_type=jnp.float32,
            )
            out_ref[home] = (summed / total).astype(jnp.bfloat16)
        return

    def one_home(home, _):
        queries = queries_of(home)

        def fold(other, carry, diagonal):
            best, total, summed = carry
            at = pl.ds(pl.multiple_of(other * rows, rows), rows)
            scores = scores_of(queries, at)
            if diagonal:
                scores = jnp.where(later, MASKED, scores)
            newbest = jnp.maximum(best, jnp.max(scores, axis=1, keepdims=True))
            factor = jnp.exp2(best - newbest)
            weights = jnp.exp2(scores - newbest)
            total = total * factor + jnp.sum(weights, axis=1, keepdims=True)
            summed = summed * factor + jnp.dot(
                weights.astype(jnp.bfloat16), values[at, :], preferred_element_type=jnp.float32
            )
            return newbest, total, summed

        start = (
            jnp.full((count, 1), MASKED, jnp.float32),
            jnp.zeros((count, 1), jnp.float32),
            jnp.zeros((count, HEAD), jnp.float32),
        )
        carry = fold(home, start, True)
        carry = lax.fori_loop(0, home, lambda other, c: fold(other, c, False), carry)
        _, total, summed = carry
        out_ref[home] = (summed / total).astype(jnp.bfloat16)
        return 0

    lax.fori_loop(0, seq_count, one_home, 0)


def attend(part, pieces, chunks, group, rows):
    seq_count = pieces[0].shape[0]
    count = rows // group
    vmem = pl.BlockSpec(memory_space=pltpu.VMEM)
    pairs = seq_count * (seq_count + 1) // 2
    return pl.pallas_call(
        partial(attend_kernel, chunks, group, rows),
        in_specs=[pl.BlockSpec(memory_space=pltpu.SMEM)] + [vmem] * len(pieces),
        out_specs=vmem,
        out_shape=jax.ShapeDtypeStruct((seq_count, count, HEAD), jnp.bfloat16),
        scratch_shapes=[
            pltpu.VMEM((seq_count * rows, 2 * HEAD), jnp.bfloat16),
            pltpu.VMEM((seq_count * rows, HEAD), jnp.bfloat16),
        ],
        compiler_params=pltpu.CompilerParams(vmem_limit_bytes=LIMIT),
        cost_estimate=pl.CostEstimate(
            flops=6 * pairs * count * rows * HEAD,
            bytes_accessed=8 * seq_count * rows * HEAD,
            transcendentals=pairs * count * rows,
        ),
    )(part, *pieces)


def output_kernel(group, count, cuts, halves, me_ref, at_ref, active_ref, hidden_ref, *refs):
    weights = refs[:cuts]
    pieces = refs[cuts:-7]
    out_ref, rows_in, held, own, piece_in, weight_in, own_in = refs[-7:]
    heads = pieces[0].shape[0] // group
    found = sources(me_ref[0], count)
    own_copy = pltpu.make_async_copy(hidden_ref, own, own_in)
    weight_copies = [
        pltpu.make_async_copy(weight, held.at[cut], weight_in.at[cut])
        for cut, weight in enumerate(weights)
    ]

    def copies_of(number):
        half, (source, there) = number // len(found), found[number % len(found)]

        def each(act):
            for head in range(heads):
                at = pl.multiple_of(at_ref[(source * halves + half) * heads + head] * HEAD, HEAD)
                for part in range(group):
                    act(
                        pltpu.make_async_copy(
                            pieces[number].at[head * group + part],
                            rows_in.at[:, part, :, pl.ds(at, HEAD)],
                            piece_in.at[half, source, head, part],
                        )
                    )

        return there, each

    for number in range(len(pieces)):
        there, each = copies_of(number)
        when(there, lambda: each(lambda copy: copy.start()))
    weight_copies[0].start()
    own_copy.start()
    for copy in weight_copies[1:]:
        copy.start()
    for number in range(len(pieces)):
        there, each = copies_of(number)
        when(there, lambda: each(lambda copy: copy.wait()))

    rows, width = own.shape[0], held.shape[2]
    x = rows_in[...].reshape(rows, -1)
    for cut in range(cuts):
        weight_copies[cut].wait()
        columns = pl.ds(pl.multiple_of(me_ref[1 + cut] * width, width), width)
        shares = jnp.dot(x, held[cut], preferred_element_type=jnp.float32)
        if cut == 0:
            own_copy.wait()
        hidden = own[:, columns]
        renewed = (hidden.astype(jnp.float32) + shares).astype(jnp.bfloat16)
        out_ref[:, columns] = jnp.where(active_ref[...] > 0, renewed, hidden)


def output(scalars, at, pieces, weights, hidden, active, chunks, group, halves):
    rows, columns = hidden.shape
    depth, width = weights[0].shape
    cuts = len(weights)
    count = (len(pieces) // halves + 1) // 2
    part_rows = rows // chunks // group
    pieces = [piece.reshape(-1, chunks, part_rows, HEAD) for piece in pieces]
    smem = pl.BlockSpec(memory_space=pltpu.SMEM)
    vmem = pl.BlockSpec(memory_space=pltpu.VMEM)
    return pl.pallas_call(
        partial(output_kernel, group, count, cuts, halves),
        in_specs=[smem, smem, vmem]
        + [pl.BlockSpec(memory_space=pl.ANY)] * (1 + cuts + len(pieces)),
        out_specs=vmem,
        out_shape=jax.ShapeDtypeStruct((rows, columns), jnp.bfloat16),
        scratch_shapes=[
            pltpu.VMEM((chunks, group, part_rows, depth), jnp.bfloat16),
            pltpu.VMEM((cuts, depth, width), jnp.bfloat16),
            pltpu.VMEM((rows, columns), jnp.bfloat16),
            pltpu.SemaphoreType.DMA((halves, count, pieces[0].shape[0] // group, group)),
            pltpu.SemaphoreType.DMA((cuts,)),
            pltpu.SemaphoreType.DMA,
        ],
        compiler_params=pltpu.CompilerParams(vmem_limit_bytes=LIMIT),
        cost_estimate=pl.CostEstimate(
            flops=2 * rows * depth * columns,
            bytes_accessed=2 * (rows * depth + depth * columns + 2 * rows * columns),
            transcendentals=0,
        ),
    )(scalars, at, active, hidden, *weights, *pieces)


def share_kernel(place_ref, w_ref, *shares):
    for step, share in enumerate(shares):

        @pl.when(pl.program_id(0) == step)
        def _():
            each = share.shape[2]
            for half in range(share.shape[0]):
                share[half] = w_ref[:, half * each : (half + 1) * each]


def shares_of(w_out, place, count, halves, each):
    width = halves * each
    cuts = w_out.shape[1] // count // width
    return pl.pallas_call(
        share_kernel,
        grid_spec=pltpu.PrefetchScalarGridSpec(
            num_scalar_prefetch=1,
            grid=(count,),
            in_specs=[
                pl.BlockSpec(
                    (HEAD, width),
                    lambda j, place: (place[0], lax.rem(place[2] + j, count) * cuts + place[1]),
                )
            ],
            out_specs=[pl.BlockSpec((halves, HEAD, each), lambda j, place: (0, 0, 0))] * count,
        ),
        out_shape=[jax.ShapeDtypeStruct((halves, HEAD, each), w_out.dtype)] * count,
        compiler_params=pltpu.CompilerParams(vmem_limit_bytes=LIMIT),
    )(place, w_out)


def weight_cuts(w_out, seq_count, columns):
    heads = w_out.shape[0] // HEAD
    cuts = seq_count // heads
    width = columns // cuts
    halves = 2 if width % (2 * HEAD) == 0 else 1
    return heads, cuts, halves, width // halves


def weight_shares(w_out, seq_count, tensor_count, columns):
    heads, cuts, halves, each = weight_cuts(w_out, seq_count, columns)
    if each % HEAD:
        return None
    seq_me = lax.axis_index("seq").astype(jnp.int32)
    me = lax.axis_index("tensor").astype(jnp.int32)
    place = jnp.stack([seq_me // cuts, seq_me % cuts, me])
    return list(shares_of(w_out, place, tensor_count, halves, each))


def send_shares(shares, tensor_count, after):
    if shares is None:
        return None
    shares, _ = lax.optimization_barrier((list(shares), after))
    for step in range(1, tensor_count):
        ring = [(d, (d + step) % tensor_count) for d in range(tensor_count)]
        shares[step] = lax.ppermute(shares[step], "tensor", ring)
    return shares


def swap(held, flips):
    grown = []
    for blocks, flip in zip(held, flips):
        pairs = [(d, d ^ flip) for d in range(lax.axis_size("seq"))]
        sent = list(blocks)
        whole = [blocks[k] for k in sent]
        got = lax.ppermute(
            jnp.concatenate(whole, axis=0) if len(whole) > 1 else whole[0], "seq", pairs
        )
        grown.append(dict(blocks))
        for k, block in zip(sent, jnp.split(got, len(sent))):
            grown[-1][k ^ flip] = block
    return grown


def output_order(w_out, seq_count, tensor_count, columns):
    heads, cuts, halves, each = weight_cuts(w_out, seq_count, columns)
    row = jnp.arange(tensor_count * heads, dtype=jnp.int32)
    if each % HEAD:
        return [jnp.int32(0)], row
    seq_me = lax.axis_index("seq").astype(jnp.int32)
    me = lax.axis_index("tensor").astype(jnp.int32)
    which = [
        (seq_me % cuts + step) % cuts * halves + half for step in range(cuts) for half in range(halves)
    ]
    tensor, of = row // heads, row % heads
    return which, (of ^ (seq_me // cuts)) * tensor_count + (me - tensor) % tensor_count


def shards(hidden, depth, norm_gain, w_query, w_key, w_value, w_out):
    rows, columns = hidden.shape
    seq_count = lax.axis_size("seq")
    tensor_count = lax.axis_size("tensor")
    heads = w_query.shape[1] // HEAD
    group = seq_count // heads
    chunks = min(4, rows // (16 * group))
    chunk_rows = rows // chunks
    part = (lax.axis_index("seq") % group).astype(jnp.int32).reshape(1)
    me = lax.axis_index("tensor").astype(jnp.int32)
    gain = norm_gain.reshape(tensor_count, columns)
    active = (depth >= 2).astype(jnp.int32).reshape(rows, 1)
    made = []
    shares = weight_shares(w_out, seq_count, tensor_count, columns)

    def work(found):
        first = chunks - len(found) if made else 0
        here = active[first * chunk_rows : (first + len(found)) * chunk_rows]
        return project(
            me.reshape(1), sum(found, []), here, gain, w_query, w_key, w_value, seq_count, group
        )

    def to_heads(sent):
        return lax.all_to_all(sent, "seq", split_axis=0, concat_axis=0)

    def to_parts(got):
        rings = [
            [(d, d - d % group + (d - step) % group) for d in range(seq_count)]
            for step in range(1, group)
        ]
        return [got] + [lax.ppermute(got, "seq", ring) for ring in rings]

    def first_pair(first, step, last, found):
        if first == 2 and step == 2:
            last, pair, mine = lax.optimization_barrier((last, found[:2], shares))
            made.append((work(pair), mine))
        return last

    gathered = line_gather(
        [hidden[c * chunk_rows : (c + 1) * chunk_rows] for c in range(chunks)],
        tensor_count,
        first_pair,
    )
    rest = gathered[-2:]
    got = []
    if made:
        (early, shares), rest = lax.optimization_barrier((made[0], rest))
        got = [to_heads(early)]
    sending = send_shares(shares, tensor_count, rest[-1])
    sent = work(rest)
    sent, sending, got = lax.optimization_barrier((sent, sending, got))
    pieces = sum([to_parts(each) for each in got + [to_heads(sent)]], [])

    heads, cuts, halves, _ = weight_cuts(w_out, seq_count, columns)
    held, flips = [], []
    if sending is not None:
        held = [
            {0: jnp.concatenate([share[half] for share in sending], axis=0)}
            for half in range(halves)
        ]
        while cuts << len(flips) < seq_count:
            flips.append(cuts << len(flips))
        held = swap(held, [flips[0], flips[-1]])
    out = attend(part, pieces, chunks, group, rows)
    out, held = lax.optimization_barrier((out, held))
    home = lax.all_to_all(out, "seq", split_axis=0, concat_axis=0)
    home, held = lax.optimization_barrier((home, held))

    def spread(first, step, last, found):
        nonlocal held
        if held and 0 < step < len(flips):
            last, held = lax.optimization_barrier(
                (last, swap(held, [flips[step], flips[-1 - step]]))
            )
        return last

    found = line_gather([home[: seq_count // 2], home[seq_count // 2 :]], tensor_count, spread)
    weights = [jnp.concatenate([blocks[k] for k in sorted(blocks)], axis=0) for blocks in held]
    for turn in range(1, cuts):
        ring = [(d, d - d % cuts + (d - turn) % cuts) for d in range(seq_count)]
        weights += [lax.ppermute(weights[half], "seq", ring) for half in range(len(held))]
    if not held:
        weights = [lax.all_to_all(w_out, "tensor", split_axis=1, concat_axis=0, tiled=True)]
    cut_of, at = output_order(w_out, seq_count, tensor_count, columns)
    scalars = jnp.stack([me, *cut_of])
    return output(scalars, at, sum(found, []), weights, hidden, active, chunks, group, 2)


def solution(mesh):
    return jax.shard_map(
        shards,
        mesh=mesh,
        in_specs=(
            P("seq", "tensor"),
            P("seq"),
            P(),
            P(None, "tensor"),
            P(None, "tensor"),
            P(None, "tensor"),
            P("tensor", None),
        ),
        out_specs=P("seq", "tensor"),
        check_vma=False,
    )
```

```python
import math
from functools import partial

import jax
import jax.numpy as jnp
from jax import lax
from jax.experimental import pallas as pl
from jax.experimental.pallas import tpu as pltpu
from jax.sharding import PartitionSpec as P

HEAD = 128
MASKED = -1e30
ASIDE = 2.0**100
LIMIT = 63 * 2**20


def sources(me, count):
    found = [(me, None)]
    for step in range(count - 1):
        found.append((me - 1 - step, me - 1 - step >= 0))
        found.append((me + 1 + step, me + 1 + step < count))
    return found


def when(there, act):
    if there is None:
        act()
    else:
        pl.when(there)(act)


def line_gather(chunks, count, join=None):
    right = [(d, d + 1) for d in range(count - 1)]
    left = [(d + 1, d) for d in range(count - 1)]
    found = []
    for first in range(0, len(chunks), 2):
        pair = []
        for chunk in chunks[first : first + 2]:
            if first:
                chunk, _ = lax.optimization_barrier((chunk, found[first - 2]))
            pair.append([chunk])
        last = [(chunk[0], chunk[0]) for chunk in pair]
        for step in range(count - 1):
            if join is not None:
                last = join(first, step, last, found)
            for at in range(len(pair)):
                from_left = lax.ppermute(last[at][0], "tensor", right[step:])
                from_right = lax.ppermute(last[at][1], "tensor", left[: count - 1 - step])
                last[at] = (from_left, from_right)
                pair[at] += [from_left, from_right]
        found += pair
    return found


def project_kernel(group, count, me_ref, gain_ref, active_ref, *refs):
    matrices = refs[:3]
    pieces = refs[3:-5]
    out_ref, normed, held, piece_in, weight_in = refs[-5:]
    found = sources(me_ref[0], count)
    chunk_rows, width = pieces[0].shape
    chunks = len(pieces) // len(found)
    rows = chunks * chunk_rows

    def copy_of(number):
        chunk, (source, there) = number // len(found), found[number % len(found)]
        to = normed.at[source, chunk * chunk_rows : (chunk + 1) * chunk_rows, :]
        return there, lambda: pltpu.make_async_copy(
            pieces[number], to, piece_in.at[chunk, source]
        )

    for number in range(len(pieces)):
        there, copy = copy_of(number)
        when(there, lambda: copy().start())
    copies = [
        [
            pltpu.make_async_copy(
                matrix.at[step * width : (step + 1) * width, :],
                held.at[step, which],
                weight_in.at[step, which],
            )
            for which, matrix in enumerate(matrices)
        ]
        for step in range(count)
    ]
    for step in range(count):
        for copy in copies[step]:
            copy.start()
    for number in range(len(pieces)):
        there, copy = copy_of(number)
        when(there, lambda: copy().wait())

    square = jnp.zeros((rows, 1), jnp.float32)
    for source in range(count):
        values = normed[source].astype(jnp.float32)
        square = square + jnp.sum(values * values, axis=1, keepdims=True)
    row_scale = lax.rsqrt(square / (count * width) + 1e-05)
    for source in range(count):
        values = normed[source].astype(jnp.float32) * row_scale * gain_ref[source : source + 1, :]
        normed[source] = values.astype(jnp.bfloat16)
    part_rows = chunk_rows // group
    totals = [None] * 3
    for step in range(count):
        for which in range(3):
            copies[step][which].wait()
            product = jnp.dot(normed[step], held[step, which], preferred_element_type=jnp.float32)
            totals[which] = product if step == 0 else totals[which] + product
    for which, total in enumerate(totals):
        if which == 0:
            total = jnp.where(active_ref[...] > 0, total, ASIDE)
        total = total.astype(jnp.bfloat16)
        for head in range(total.shape[1] // HEAD):
            for part in range(group):
                for chunk in range(chunks):
                    first = chunk * chunk_rows + part * part_rows
                    out_ref[
                        head * group + part,
                        chunk * part_rows : (chunk + 1) * part_rows,
                        which * HEAD : (which + 1) * HEAD,
                    ] = total[first : first + part_rows, head * HEAD : (head + 1) * HEAD]


def project(me, pieces, active, gain, wq, wk, wv, seq_count, group):
    columns = pieces[0].shape[1]
    rows = active.shape[0]
    features, width = wq.shape
    count = features // columns
    vmem = pl.BlockSpec(memory_space=pltpu.VMEM)
    return pl.pallas_call(
        partial(project_kernel, group, count),
        in_specs=[pl.BlockSpec(memory_space=pltpu.SMEM), vmem, vmem]
        + [pl.BlockSpec(memory_space=pl.ANY)] * (3 + len(pieces)),
        out_specs=vmem,
        out_shape=jax.ShapeDtypeStruct((seq_count, rows // group, 3 * HEAD), jnp.bfloat16),
        scratch_shapes=[
            pltpu.VMEM((count, rows, columns), jnp.bfloat16),
            pltpu.VMEM((count, 3, columns, width), jnp.bfloat16),
            pltpu.SemaphoreType.DMA((rows // pieces[0].shape[0], count)),
            pltpu.SemaphoreType.DMA((count, 3)),
        ],
        compiler_params=pltpu.CompilerParams(vmem_limit_bytes=LIMIT),
        cost_estimate=pl.CostEstimate(
            flops=6 * rows * features * width,
            bytes_accessed=6 * features * width + 2 * rows * (features + 3 * width),
            transcendentals=0,
        ),
    )(me, gain, active, wq, wk, wv, *pieces)


def attend_kernel(chunks, group, rows, part_ref, *refs):
    pieces = refs[:-3]
    out_ref, keys, values = refs[-3:]
    seq_count = pieces[0].shape[0]
    chunk_rows = rows // chunks
    part_rows = chunk_rows // group
    part = part_ref[0]

    def place(home, _):
        chunk = 0
        for number in range(0, len(pieces), group):
            inside = pieces[number].shape[1] // part_rows
            for step in range(group):
                owner = lax.rem(part + step, group)
                piece = pieces[number + step]
                for at_chunk in range(inside):
                    at = home * rows + (chunk + at_chunk) * chunk_rows + owner * part_rows
                    to = pl.ds(pl.multiple_of(at, part_rows), part_rows)
                    of = slice(at_chunk * part_rows, (at_chunk + 1) * part_rows)
                    aside = piece[home, of, :HEAD].astype(jnp.float32) >= ASIDE
                    keys[to, :HEAD] = piece[home, of, HEAD : 2 * HEAD]
                    keys[to, HEAD:] = jnp.where(aside, MASKED, 0.0).astype(jnp.bfloat16)
                    values[to, :] = piece[home, of, 2 * HEAD :]
            chunk += inside
        return 0

    lax.fori_loop(0, seq_count, place, 0)
    scale = math.log2(math.e) / math.sqrt(HEAD)
    count = chunks * part_rows
    first_lane = lax.broadcasted_iota(jnp.int32, (count, HEAD), 1) == 0
    mask_lane = jnp.where(first_lane, 1.0, 0.0).astype(jnp.bfloat16)
    order = lax.broadcasted_iota(jnp.int32, (count, rows), 0)
    own = order // part_rows * chunk_rows + part * part_rows + order % part_rows
    later = lax.broadcasted_iota(jnp.int32, (count, rows), 1) > own

    def queries_of(home):
        queries = jnp.concatenate(
            [pieces[number][home, :, :HEAD] for number in range(0, len(pieces), group)], axis=0
        )
        return jnp.concatenate([queries, mask_lane], axis=1)

    def scores_of(queries, at):
        return scale * lax.dot_general(
            queries,
            keys[at, :],
            (((1,), (1,)), ((), ())),
            preferred_element_type=jnp.float32,
        )

    if seq_count <= 8:
        for home in range(seq_count):
            queries = queries_of(home)
            blocks = []
            for other in range(home + 1):
                scores = scores_of(queries, slice(other * rows, (other + 1) * rows))
                if other == home:
                    scores = jnp.where(later, MASKED, scores)
                blocks.append(scores)
            scores = jnp.concatenate(blocks, axis=1)
            best = jnp.max(scores, axis=1, keepdims=True)
            weights = jnp.exp2(scores - best)
            total = jnp.sum(weights, axis=1, keepdims=True)
            summed = jnp.dot(
                weights.astype(jnp.bfloat16),
                values[: (home + 1) * rows, :],
                preferred_element_type=jnp.float32,
            )
            out_ref[home] = (summed / total).astype(jnp.bfloat16)
        return

    def one_home(home, _):
        queries = queries_of(home)

        def fold(other, carry, diagonal):
            best, total, summed = carry
            at = pl.ds(pl.multiple_of(other * rows, rows), rows)
            scores = scores_of(queries, at)
            if diagonal:
                scores = jnp.where(later, MASKED, scores)
            newbest = jnp.maximum(best, jnp.max(scores, axis=1, keepdims=True))
            factor = jnp.exp2(best - newbest)
            weights = jnp.exp2(scores - newbest)
            total = total * factor + jnp.sum(weights, axis=1, keepdims=True)
            summed = summed * factor + jnp.dot(
                weights.astype(jnp.bfloat16), values[at, :], preferred_element_type=jnp.float32
            )
            return newbest, total, summed

        start = (
            jnp.full((count, 1), MASKED, jnp.float32),
            jnp.zeros((count, 1), jnp.float32),
            jnp.zeros((count, HEAD), jnp.float32),
        )
        carry = fold(home, start, True)
        carry = lax.fori_loop(0, home, lambda other, c: fold(other, c, False), carry)
        _, total, summed = carry
        out_ref[home] = (summed / total).astype(jnp.bfloat16)
        return 0

    lax.fori_loop(0, seq_count, one_home, 0)


def attend(part, pieces, chunks, group, rows):
    seq_count = pieces[0].shape[0]
    count = rows // group
    vmem = pl.BlockSpec(memory_space=pltpu.VMEM)
    pairs = seq_count * (seq_count + 1) // 2
    return pl.pallas_call(
        partial(attend_kernel, chunks, group, rows),
        in_specs=[pl.BlockSpec(memory_space=pltpu.SMEM)] + [vmem] * len(pieces),
        out_specs=vmem,
        out_shape=jax.ShapeDtypeStruct((seq_count, count, HEAD), jnp.bfloat16),
        scratch_shapes=[
            pltpu.VMEM((seq_count * rows, 2 * HEAD), jnp.bfloat16),
            pltpu.VMEM((seq_count * rows, HEAD), jnp.bfloat16),
        ],
        compiler_params=pltpu.CompilerParams(vmem_limit_bytes=LIMIT),
        cost_estimate=pl.CostEstimate(
            flops=6 * pairs * count * rows * HEAD,
            bytes_accessed=8 * seq_count * rows * HEAD,
            transcendentals=pairs * count * rows,
        ),
    )(part, *pieces)


def output_kernel(group, count, cuts, halves, me_ref, at_ref, active_ref, hidden_ref, *refs):
    weights = refs[:cuts]
    pieces = refs[cuts:-7]
    out_ref, rows_in, held, own, piece_in, weight_in, own_in = refs[-7:]
    heads = pieces[0].shape[0] // group
    found = sources(me_ref[0], count)
    own_copy = pltpu.make_async_copy(hidden_ref, own, own_in)
    weight_copies = [
        pltpu.make_async_copy(weight, held.at[cut], weight_in.at[cut])
        for cut, weight in enumerate(weights)
    ]

    def copies_of(number):
        half, (source, there) = number // len(found), found[number % len(found)]

        def each(act):
            for head in range(heads):
                at = pl.multiple_of(at_ref[(source * halves + half) * heads + head] * HEAD, HEAD)
                for part in range(group):
                    act(
                        pltpu.make_async_copy(
                            pieces[number].at[head * group + part],
                            rows_in.at[:, part, :, pl.ds(at, HEAD)],
                            piece_in.at[half, source, head, part],
                        )
                    )

        return there, each

    for number in range(len(pieces)):
        there, each = copies_of(number)
        when(there, lambda: each(lambda copy: copy.start()))
    weight_copies[0].start()
    own_copy.start()
    for copy in weight_copies[1:]:
        copy.start()
    for number in range(len(pieces)):
        there, each = copies_of(number)
        when(there, lambda: each(lambda copy: copy.wait()))

    rows, width = own.shape[0], held.shape[2]
    x = rows_in[...].reshape(rows, -1)
    for cut in range(cuts):
        weight_copies[cut].wait()
        columns = pl.ds(pl.multiple_of(me_ref[1 + cut] * width, width), width)
        shares = jnp.dot(x, held[cut], preferred_element_type=jnp.float32)
        if cut == 0:
            own_copy.wait()
        hidden = own[:, columns]
        renewed = (hidden.astype(jnp.float32) + shares).astype(jnp.bfloat16)
        out_ref[:, columns] = jnp.where(active_ref[...] > 0, renewed, hidden)


def output(scalars, at, pieces, weights, hidden, active, chunks, group, halves):
    rows, columns = hidden.shape
    depth, width = weights[0].shape
    cuts = len(weights)
    count = (len(pieces) // halves + 1) // 2
    part_rows = rows // chunks // group
    pieces = [piece.reshape(-1, chunks, part_rows, HEAD) for piece in pieces]
    smem = pl.BlockSpec(memory_space=pltpu.SMEM)
    vmem = pl.BlockSpec(memory_space=pltpu.VMEM)
    return pl.pallas_call(
        partial(output_kernel, group, count, cuts, halves),
        in_specs=[smem, smem, vmem]
        + [pl.BlockSpec(memory_space=pl.ANY)] * (1 + cuts + len(pieces)),
        out_specs=vmem,
        out_shape=jax.ShapeDtypeStruct((rows, columns), jnp.bfloat16),
        scratch_shapes=[
            pltpu.VMEM((chunks, group, part_rows, depth), jnp.bfloat16),
            pltpu.VMEM((cuts, depth, width), jnp.bfloat16),
            pltpu.VMEM((rows, columns), jnp.bfloat16),
            pltpu.SemaphoreType.DMA((halves, count, pieces[0].shape[0] // group, group)),
            pltpu.SemaphoreType.DMA((cuts,)),
            pltpu.SemaphoreType.DMA,
        ],
        compiler_params=pltpu.CompilerParams(vmem_limit_bytes=LIMIT),
        cost_estimate=pl.CostEstimate(
            flops=2 * rows * depth * columns,
            bytes_accessed=2 * (rows * depth + depth * columns + 2 * rows * columns),
            transcendentals=0,
        ),
    )(scalars, at, active, hidden, *weights, *pieces)


def share_kernel(place_ref, w_ref, *shares):
    for step, share in enumerate(shares):

        @pl.when(pl.program_id(0) == step)
        def _():
            each = share.shape[2]
            for half in range(share.shape[0]):
                share[half] = w_ref[:, half * each : (half + 1) * each]


def shares_of(w_out, place, count, halves, each):
    width = halves * each
    cuts = w_out.shape[1] // count // width
    return pl.pallas_call(
        share_kernel,
        grid_spec=pltpu.PrefetchScalarGridSpec(
            num_scalar_prefetch=1,
            grid=(count,),
            in_specs=[
                pl.BlockSpec(
                    (HEAD, width),
                    lambda j, place: (place[0], lax.rem(place[2] + j, count) * cuts + place[1]),
                )
            ],
            out_specs=[pl.BlockSpec((halves, HEAD, each), lambda j, place: (0, 0, 0))] * count,
        ),
        out_shape=[jax.ShapeDtypeStruct((halves, HEAD, each), w_out.dtype)] * count,
        compiler_params=pltpu.CompilerParams(vmem_limit_bytes=LIMIT),
    )(place, w_out)


def weight_cuts(w_out, seq_count, columns):
    heads = w_out.shape[0] // HEAD
    cuts = seq_count // heads
    width = columns // cuts
    halves = 2 if width % (2 * HEAD) == 0 else 1
    return heads, cuts, halves, width // halves


def weight_shares(w_out, seq_count, tensor_count, columns):
    heads, cuts, halves, each = weight_cuts(w_out, seq_count, columns)
    if each % HEAD:
        return None
    seq_me = lax.axis_index("seq").astype(jnp.int32)
    me = lax.axis_index("tensor").astype(jnp.int32)
    place = jnp.stack([seq_me // cuts, seq_me % cuts, me])
    return list(shares_of(w_out, place, tensor_count, halves, each))


def send_shares(shares, tensor_count):
    if shares is None:
        return None
    shares = list(shares)
    for step in range(1, tensor_count):
        ring = [(d, (d + step) % tensor_count) for d in range(tensor_count)]
        shares[step] = lax.ppermute(shares[step], "tensor", ring)
    return shares


def swap(held, flips):
    grown = []
    for blocks, flip in zip(held, flips):
        pairs = [(d, d ^ flip) for d in range(lax.axis_size("seq"))]
        sent = list(blocks)
        whole = [blocks[k] for k in sent]
        got = lax.ppermute(
            jnp.concatenate(whole, axis=0) if len(whole) > 1 else whole[0], "seq", pairs
        )
        grown.append(dict(blocks))
        for k, block in zip(sent, jnp.split(got, len(sent))):
            grown[-1][k ^ flip] = block
    return grown


def output_order(w_out, seq_count, tensor_count, columns):
    heads, cuts, halves, each = weight_cuts(w_out, seq_count, columns)
    row = jnp.arange(tensor_count * heads, dtype=jnp.int32)
    if each % HEAD:
        return [jnp.int32(0)], row
    seq_me = lax.axis_index("seq").astype(jnp.int32)
    me = lax.axis_index("tensor").astype(jnp.int32)
    which = [
        (seq_me % cuts + step) % cuts * halves + half for step in range(cuts) for half in range(halves)
    ]
    tensor, of = row // heads, row % heads
    return which, (of ^ (seq_me // cuts)) * tensor_count + (me - tensor) % tensor_count


def shards(hidden, depth, norm_gain, w_query, w_key, w_value, w_out):
    rows, columns = hidden.shape
    seq_count = lax.axis_size("seq")
    tensor_count = lax.axis_size("tensor")
    heads = w_query.shape[1] // HEAD
    group = seq_count // heads
    chunks = min(4, rows // (16 * group))
    chunk_rows = rows // chunks
    part = (lax.axis_index("seq") % group).astype(jnp.int32).reshape(1)
    me = lax.axis_index("tensor").astype(jnp.int32)
    gain = norm_gain.reshape(tensor_count, columns)
    active = (depth >= 2).astype(jnp.int32).reshape(rows, 1)
    made = []
    shares = weight_shares(w_out, seq_count, tensor_count, columns)

    def work(found):
        first = chunks - len(found) if made else 0
        here = active[first * chunk_rows : (first + len(found)) * chunk_rows]
        return project(
            me.reshape(1), sum(found, []), here, gain, w_query, w_key, w_value, seq_count, group
        )

    def to_heads(sent):
        return lax.all_to_all(sent, "seq", split_axis=0, concat_axis=0)

    def to_parts(got):
        rings = [
            [(d, d - d % group + (d - step) % group) for d in range(seq_count)]
            for step in range(1, group)
        ]
        return [got] + [lax.ppermute(got, "seq", ring) for ring in rings]

    def first_pair(first, step, last, found):
        if first == 2 and step == 2:
            last, pair, mine = lax.optimization_barrier((last, found[:2], shares))
            made.append((work(pair), mine))
        return last

    gathered = line_gather(
        [hidden[c * chunk_rows : (c + 1) * chunk_rows] for c in range(chunks)],
        tensor_count,
        first_pair,
    )
    rest = gathered[-2:]
    got = []
    if made:
        (early, shares), rest = lax.optimization_barrier((made[0], rest))
        got = [to_heads(early)]
    sent, got, shares = lax.optimization_barrier((work(rest), got, shares))
    sending = send_shares(shares, tensor_count)
    late, sending = lax.optimization_barrier((to_heads(sent), sending))
    pieces = sum([to_parts(each) for each in got + [late]], [])

    heads, cuts, halves, _ = weight_cuts(w_out, seq_count, columns)
    held, flips = [], []
    if sending is not None:
        held = [
            {0: jnp.concatenate([share[half] for share in sending], axis=0)}
            for half in range(halves)
        ]
        while cuts << len(flips) < seq_count:
            flips.append(cuts << len(flips))
        held = swap(held, [flips[0], flips[-1]])
    out = attend(part, pieces, chunks, group, rows)
    out, held = lax.optimization_barrier((out, held))
    home = lax.all_to_all(out, "seq", split_axis=0, concat_axis=0)
    home, held = lax.optimization_barrier((home, held))

    def spread(first, step, last, found):
        nonlocal held
        if held and step == 2:
            for stage in range(1, len(flips)):
                held = swap(held, [flips[stage], flips[-1 - stage]])
            last, held = lax.optimization_barrier((last, held))
        return last

    found = line_gather([home[: seq_count // 2], home[seq_count // 2 :]], tensor_count, spread)
    weights = [jnp.concatenate([blocks[k] for k in sorted(blocks)], axis=0) for blocks in held]
    for turn in range(1, cuts):
        ring = [(d, d - d % cuts + (d - turn) % cuts) for d in range(seq_count)]
        weights += [lax.ppermute(weights[half], "seq", ring) for half in range(len(held))]
    if not held:
        weights = [lax.all_to_all(w_out, "tensor", split_axis=1, concat_axis=0, tiled=True)]
    cut_of, at = output_order(w_out, seq_count, tensor_count, columns)
    scalars = jnp.stack([me, *cut_of])
    return output(scalars, at, sum(found, []), weights, hidden, active, chunks, group, 2)


def solution(mesh):
    return jax.shard_map(
        shards,
        mesh=mesh,
        in_specs=(
            P("seq", "tensor"),
            P("seq"),
            P(),
            P(None, "tensor"),
            P(None, "tensor"),
            P(None, "tensor"),
            P("tensor", None),
        ),
        out_specs=P("seq", "tensor"),
        check_vma=False,
    )
```

```python
import math
from functools import partial

import jax
import jax.numpy as jnp
from jax import lax
from jax.experimental import pallas as pl
from jax.experimental.pallas import tpu as pltpu
from jax.sharding import PartitionSpec as P

HEAD = 128
MASKED = -1e30
ASIDE = 2.0**100
LIMIT = 63 * 2**20


def sources(me, count):
    found = [(me, None)]
    for step in range(count - 1):
        found.append((me - 1 - step, me - 1 - step >= 0))
        found.append((me + 1 + step, me + 1 + step < count))
    return found


def when(there, act):
    if there is None:
        act()
    else:
        pl.when(there)(act)


def line_gather(chunks, count, join):
    right = [(d, d + 1) for d in range(count - 1)]
    left = [(d + 1, d) for d in range(count - 1)]
    found = [[chunk] for chunk in chunks]
    last = [(chunk, chunk) for chunk in chunks]
    for step in range(count - 1):
        last = join(step, last)
        for at in range(len(chunks)):
            from_left = lax.ppermute(last[at][0], "tensor", right[step:])
            from_right = lax.ppermute(last[at][1], "tensor", left[: count - 1 - step])
            last[at] = (from_left, from_right)
            found[at] += [from_left, from_right]
    return found


def project_kernel(group, count, me_ref, gain_ref, active_ref, *refs):
    matrices = refs[:3]
    pieces = refs[3:-5]
    out_ref, normed, held, piece_in, weight_in = refs[-5:]
    found = sources(me_ref[0], count)
    chunk_rows, width = pieces[0].shape
    chunks = len(pieces) // len(found)
    rows = chunks * chunk_rows

    def copy_of(number):
        chunk, (source, there) = number // len(found), found[number % len(found)]
        to = normed.at[source, chunk * chunk_rows : (chunk + 1) * chunk_rows, :]
        return there, lambda: pltpu.make_async_copy(
            pieces[number], to, piece_in.at[chunk, source]
        )

    for number in range(len(pieces)):
        there, copy = copy_of(number)
        when(there, lambda: copy().start())
    copies = [
        [
            pltpu.make_async_copy(
                matrix.at[step * width : (step + 1) * width, :],
                held.at[step, which],
                weight_in.at[step, which],
            )
            for which, matrix in enumerate(matrices)
        ]
        for step in range(count)
    ]
    for step in range(count):
        for copy in copies[step]:
            copy.start()
    for number in range(len(pieces)):
        there, copy = copy_of(number)
        when(there, lambda: copy().wait())

    square = jnp.zeros((rows, 1), jnp.float32)
    for source in range(count):
        values = normed[source].astype(jnp.float32)
        square = square + jnp.sum(values * values, axis=1, keepdims=True)
    row_scale = lax.rsqrt(square / (count * width) + 1e-05)
    for source in range(count):
        values = normed[source].astype(jnp.float32) * row_scale * gain_ref[source : source + 1, :]
        normed[source] = values.astype(jnp.bfloat16)
    part_rows = chunk_rows // group
    totals = [None] * 3
    for step in range(count):
        for which in range(3):
            copies[step][which].wait()
            product = jnp.dot(normed[step], held[step, which], preferred_element_type=jnp.float32)
            totals[which] = product if step == 0 else totals[which] + product
    for which, total in enumerate(totals):
        if which == 0:
            total = jnp.where(active_ref[...] > 0, total, ASIDE)
        total = total.astype(jnp.bfloat16)
        for head in range(total.shape[1] // HEAD):
            for part in range(group):
                for chunk in range(chunks):
                    first = chunk * chunk_rows + part * part_rows
                    out_ref[
                        head * group + part,
                        chunk * part_rows : (chunk + 1) * part_rows,
                        which * HEAD : (which + 1) * HEAD,
                    ] = total[first : first + part_rows, head * HEAD : (head + 1) * HEAD]


def project(me, pieces, active, gain, wq, wk, wv, seq_count, group):
    columns = pieces[0].shape[1]
    rows = active.shape[0]
    features, width = wq.shape
    count = features // columns
    vmem = pl.BlockSpec(memory_space=pltpu.VMEM)
    return pl.pallas_call(
        partial(project_kernel, group, count),
        in_specs=[pl.BlockSpec(memory_space=pltpu.SMEM), vmem, vmem]
        + [pl.BlockSpec(memory_space=pl.ANY)] * (3 + len(pieces)),
        out_specs=vmem,
        out_shape=jax.ShapeDtypeStruct((seq_count, rows // group, 3 * HEAD), jnp.bfloat16),
        scratch_shapes=[
            pltpu.VMEM((count, rows, columns), jnp.bfloat16),
            pltpu.VMEM((count, 3, columns, width), jnp.bfloat16),
            pltpu.SemaphoreType.DMA((rows // pieces[0].shape[0], count)),
            pltpu.SemaphoreType.DMA((count, 3)),
        ],
        compiler_params=pltpu.CompilerParams(vmem_limit_bytes=LIMIT),
        cost_estimate=pl.CostEstimate(
            flops=6 * rows * features * width,
            bytes_accessed=6 * features * width + 2 * rows * (features + 3 * width),
            transcendentals=0,
        ),
    )(me, gain, active, wq, wk, wv, *pieces)


def attend_kernel(chunks, group, rows, part_ref, *refs):
    pieces = refs[:-3]
    out_ref, keys, values = refs[-3:]
    seq_count = pieces[0].shape[0]
    chunk_rows = rows // chunks
    part_rows = chunk_rows // group
    part = part_ref[0]

    def place(home, _):
        chunk = 0
        for number in range(0, len(pieces), group):
            inside = pieces[number].shape[1] // part_rows
            for step in range(group):
                owner = lax.rem(part + step, group)
                piece = pieces[number + step]
                for at_chunk in range(inside):
                    at = home * rows + (chunk + at_chunk) * chunk_rows + owner * part_rows
                    to = pl.ds(pl.multiple_of(at, part_rows), part_rows)
                    of = slice(at_chunk * part_rows, (at_chunk + 1) * part_rows)
                    aside = piece[home, of, :HEAD].astype(jnp.float32) >= ASIDE
                    keys[to, :HEAD] = piece[home, of, HEAD : 2 * HEAD]
                    keys[to, HEAD:] = jnp.where(aside, MASKED, 0.0).astype(jnp.bfloat16)
                    values[to, :] = piece[home, of, 2 * HEAD :]
            chunk += inside
        return 0

    lax.fori_loop(0, seq_count, place, 0)
    scale = math.log2(math.e) / math.sqrt(HEAD)
    count = chunks * part_rows
    first_lane = lax.broadcasted_iota(jnp.int32, (count, HEAD), 1) == 0
    mask_lane = jnp.where(first_lane, 1.0, 0.0).astype(jnp.bfloat16)
    order = lax.broadcasted_iota(jnp.int32, (count, rows), 0)
    own = order // part_rows * chunk_rows + part * part_rows + order % part_rows
    later = lax.broadcasted_iota(jnp.int32, (count, rows), 1) > own

    def queries_of(home):
        queries = jnp.concatenate(
            [pieces[number][home, :, :HEAD] for number in range(0, len(pieces), group)], axis=0
        )
        return jnp.concatenate([queries, mask_lane], axis=1)

    def scores_of(queries, at):
        return scale * lax.dot_general(
            queries,
            keys[at, :],
            (((1,), (1,)), ((), ())),
            preferred_element_type=jnp.float32,
        )

    if seq_count <= 8:
        for home in range(seq_count):
            queries = queries_of(home)
            blocks = []
            for other in range(home + 1):
                scores = scores_of(queries, slice(other * rows, (other + 1) * rows))
                if other == home:
                    scores = jnp.where(later, MASKED, scores)
                blocks.append(scores)
            scores = jnp.concatenate(blocks, axis=1)
            best = jnp.max(scores, axis=1, keepdims=True)
            weights = jnp.exp2(scores - best)
            total = jnp.sum(weights, axis=1, keepdims=True)
            summed = jnp.dot(
                weights.astype(jnp.bfloat16),
                values[: (home + 1) * rows, :],
                preferred_element_type=jnp.float32,
            )
            out_ref[home] = (summed / total).astype(jnp.bfloat16)
        return

    def one_home(home, _):
        queries = queries_of(home)

        def fold(other, carry, diagonal):
            best, total, summed = carry
            at = pl.ds(pl.multiple_of(other * rows, rows), rows)
            scores = scores_of(queries, at)
            if diagonal:
                scores = jnp.where(later, MASKED, scores)
            newbest = jnp.maximum(best, jnp.max(scores, axis=1, keepdims=True))
            factor = jnp.exp2(best - newbest)
            weights = jnp.exp2(scores - newbest)
            total = total * factor + jnp.sum(weights, axis=1, keepdims=True)
            summed = summed * factor + jnp.dot(
                weights.astype(jnp.bfloat16), values[at, :], preferred_element_type=jnp.float32
            )
            return newbest, total, summed

        start = (
            jnp.full((count, 1), MASKED, jnp.float32),
            jnp.zeros((count, 1), jnp.float32),
            jnp.zeros((count, HEAD), jnp.float32),
        )
        carry = fold(home, start, True)
        carry = lax.fori_loop(0, home, lambda other, c: fold(other, c, False), carry)
        _, total, summed = carry
        out_ref[home] = (summed / total).astype(jnp.bfloat16)
        return 0

    lax.fori_loop(0, seq_count, one_home, 0)


def attend(part, pieces, chunks, group, rows):
    seq_count = pieces[0].shape[0]
    count = rows // group
    vmem = pl.BlockSpec(memory_space=pltpu.VMEM)
    pairs = seq_count * (seq_count + 1) // 2
    return pl.pallas_call(
        partial(attend_kernel, chunks, group, rows),
        in_specs=[pl.BlockSpec(memory_space=pltpu.SMEM)] + [vmem] * len(pieces),
        out_specs=vmem,
        out_shape=jax.ShapeDtypeStruct((seq_count, count, HEAD), jnp.bfloat16),
        scratch_shapes=[
            pltpu.VMEM((seq_count * rows, 2 * HEAD), jnp.bfloat16),
            pltpu.VMEM((seq_count * rows, HEAD), jnp.bfloat16),
        ],
        compiler_params=pltpu.CompilerParams(vmem_limit_bytes=LIMIT),
        cost_estimate=pl.CostEstimate(
            flops=6 * pairs * count * rows * HEAD,
            bytes_accessed=8 * seq_count * rows * HEAD,
            transcendentals=pairs * count * rows,
        ),
    )(part, *pieces)


def output_kernel(group, count, cuts, halves, me_ref, at_ref, active_ref, hidden_ref, *refs):
    weights = refs[:cuts]
    pieces = refs[cuts:-7]
    out_ref, rows_in, held, own, piece_in, weight_in, own_in = refs[-7:]
    heads = pieces[0].shape[0] // group
    found = sources(me_ref[0], count)
    own_copy = pltpu.make_async_copy(hidden_ref, own, own_in)
    weight_copies = [
        pltpu.make_async_copy(weight, held.at[cut], weight_in.at[cut])
        for cut, weight in enumerate(weights)
    ]

    def copies_of(number):
        half, (source, there) = number // len(found), found[number % len(found)]

        def each(act):
            for head in range(heads):
                at = pl.multiple_of(at_ref[(source * halves + half) * heads + head] * HEAD, HEAD)
                for part in range(group):
                    act(
                        pltpu.make_async_copy(
                            pieces[number].at[head * group + part],
                            rows_in.at[:, part, :, pl.ds(at, HEAD)],
                            piece_in.at[half, source, head, part],
                        )
                    )

        return there, each

    for number in range(len(pieces)):
        there, each = copies_of(number)
        when(there, lambda: each(lambda copy: copy.start()))
    weight_copies[0].start()
    own_copy.start()
    for copy in weight_copies[1:]:
        copy.start()
    for number in range(len(pieces)):
        there, each = copies_of(number)
        when(there, lambda: each(lambda copy: copy.wait()))

    rows, width = own.shape[0], held.shape[2]
    x = rows_in[...].reshape(rows, -1)
    for cut in range(cuts):
        weight_copies[cut].wait()
        columns = pl.ds(pl.multiple_of(me_ref[1 + cut] * width, width), width)
        shares = jnp.dot(x, held[cut], preferred_element_type=jnp.float32)
        if cut == 0:
            own_copy.wait()
        hidden = own[:, columns]
        renewed = (hidden.astype(jnp.float32) + shares).astype(jnp.bfloat16)
        out_ref[:, columns] = jnp.where(active_ref[...] > 0, renewed, hidden)


def output(scalars, at, pieces, weights, hidden, active, chunks, group, halves):
    rows, columns = hidden.shape
    depth, width = weights[0].shape
    cuts = len(weights)
    count = (len(pieces) // halves + 1) // 2
    part_rows = rows // chunks // group
    pieces = [piece.reshape(-1, chunks, part_rows, HEAD) for piece in pieces]
    smem = pl.BlockSpec(memory_space=pltpu.SMEM)
    vmem = pl.BlockSpec(memory_space=pltpu.VMEM)
    return pl.pallas_call(
        partial(output_kernel, group, count, cuts, halves),
        in_specs=[smem, smem, vmem]
        + [pl.BlockSpec(memory_space=pl.ANY)] * (1 + cuts + len(pieces)),
        out_specs=vmem,
        out_shape=jax.ShapeDtypeStruct((rows, columns), jnp.bfloat16),
        scratch_shapes=[
            pltpu.VMEM((chunks, group, part_rows, depth), jnp.bfloat16),
            pltpu.VMEM((cuts, depth, width), jnp.bfloat16),
            pltpu.VMEM((rows, columns), jnp.bfloat16),
            pltpu.SemaphoreType.DMA((halves, count, pieces[0].shape[0] // group, group)),
            pltpu.SemaphoreType.DMA((cuts,)),
            pltpu.SemaphoreType.DMA,
        ],
        compiler_params=pltpu.CompilerParams(vmem_limit_bytes=LIMIT),
        cost_estimate=pl.CostEstimate(
            flops=2 * rows * depth * columns,
            bytes_accessed=2 * (rows * depth + depth * columns + 2 * rows * columns),
            transcendentals=0,
        ),
    )(scalars, at, active, hidden, *weights, *pieces)


def share_kernel(place_ref, w_ref, *shares):
    for step, share in enumerate(shares):

        @pl.when(pl.program_id(0) == step)
        def _():
            each = share.shape[2]
            for half in range(share.shape[0]):
                share[half] = w_ref[:, half * each : (half + 1) * each]


def shares_of(w_out, place, count, halves, each):
    width = halves * each
    cuts = w_out.shape[1] // count // width
    return pl.pallas_call(
        share_kernel,
        grid_spec=pltpu.PrefetchScalarGridSpec(
            num_scalar_prefetch=1,
            grid=(count,),
            in_specs=[
                pl.BlockSpec(
                    (HEAD, width),
                    lambda j, place: (place[0], lax.rem(place[2] + j, count) * cuts + place[1]),
                )
            ],
            out_specs=[pl.BlockSpec((halves, HEAD, each), lambda j, place: (0, 0, 0))] * count,
        ),
        out_shape=[jax.ShapeDtypeStruct((halves, HEAD, each), w_out.dtype)] * count,
        compiler_params=pltpu.CompilerParams(vmem_limit_bytes=LIMIT),
    )(place, w_out)


def weight_cuts(w_out, seq_count, columns):
    heads = w_out.shape[0] // HEAD
    cuts = seq_count // heads
    width = columns // cuts
    halves = 2 if width % (2 * HEAD) == 0 else 1
    return heads, cuts, halves, width // halves


def weight_shares(w_out, seq_count, tensor_count, columns):
    heads, cuts, halves, each = weight_cuts(w_out, seq_count, columns)
    if each % HEAD:
        return None
    seq_me = lax.axis_index("seq").astype(jnp.int32)
    me = lax.axis_index("tensor").astype(jnp.int32)
    place = jnp.stack([seq_me // cuts, seq_me % cuts, me])
    return list(shares_of(w_out, place, tensor_count, halves, each))


def send_shares(shares, tensor_count):
    if shares is None:
        return None
    shares = list(shares)
    for step in range(1, tensor_count):
        ring = [(d, (d + step) % tensor_count) for d in range(tensor_count)]
        shares[step] = lax.ppermute(shares[step], "tensor", ring)
    return shares


def swap(held, flips):
    grown = []
    for blocks, flip in zip(held, flips):
        pairs = [(d, d ^ flip) for d in range(lax.axis_size("seq"))]
        sent = list(blocks)
        whole = [blocks[k] for k in sent]
        got = lax.ppermute(
            jnp.concatenate(whole, axis=0) if len(whole) > 1 else whole[0], "seq", pairs
        )
        grown.append(dict(blocks))
        for k, block in zip(sent, jnp.split(got, len(sent))):
            grown[-1][k ^ flip] = block
    return grown


def output_order(w_out, seq_count, tensor_count, columns):
    heads, cuts, halves, each = weight_cuts(w_out, seq_count, columns)
    row = jnp.arange(tensor_count * heads, dtype=jnp.int32)
    if each % HEAD:
        return [jnp.int32(0)], row
    seq_me = lax.axis_index("seq").astype(jnp.int32)
    me = lax.axis_index("tensor").astype(jnp.int32)
    which = [
        (seq_me % cuts + step) % cuts * halves + half for step in range(cuts) for half in range(halves)
    ]
    tensor, of = row // heads, row % heads
    return which, (of ^ (seq_me // cuts)) * tensor_count + (me - tensor) % tensor_count


def shards(hidden, depth, norm_gain, w_query, w_key, w_value, w_out):
    rows, columns = hidden.shape
    seq_count = lax.axis_size("seq")
    tensor_count = lax.axis_size("tensor")
    heads = w_query.shape[1] // HEAD
    group = seq_count // heads
    chunks = 2
    chunk_rows = rows // chunks
    part = (lax.axis_index("seq") % group).astype(jnp.int32).reshape(1)
    me = lax.axis_index("tensor").astype(jnp.int32)
    gain = norm_gain.reshape(tensor_count, columns)
    active = (depth >= 2).astype(jnp.int32).reshape(rows, 1)
    shares = weight_shares(w_out, seq_count, tensor_count, columns)

    def work(found, chunk):
        here = active[chunk * chunk_rows : (chunk + 1) * chunk_rows]
        return project(
            me.reshape(1), found, here, gain, w_query, w_key, w_value, seq_count, group
        )

    def to_heads(sent):
        return lax.all_to_all(sent, "seq", split_axis=0, concat_axis=0)

    def to_parts(got):
        rings = [
            [(d, d - d % group + (d - step) % group) for d in range(seq_count)]
            for step in range(1, group)
        ]
        return [got] + [lax.ppermute(got, "seq", ring) for ring in rings]

    def cut_weight(step, last):
        nonlocal shares
        if step == 1:
            last[1], shares = lax.optimization_barrier((last[1], shares))
        return last

    first, second = line_gather(
        [hidden[:chunk_rows], hidden[chunk_rows:]], tensor_count, cut_weight
    )
    early, second = lax.optimization_barrier((work(first, 0), second))
    sent, early, shares = lax.optimization_barrier((work(second, 1), to_heads(early), shares))
    sending = send_shares(shares, tensor_count)
    late, sending = lax.optimization_barrier((to_heads(sent), sending))
    pieces = to_parts(early) + to_parts(late)

    heads, cuts, halves, _ = weight_cuts(w_out, seq_count, columns)
    held, flips = [], []
    if sending is not None:
        held = [
            {0: jnp.concatenate([share[half] for share in sending], axis=0)}
            for half in range(halves)
        ]
        while cuts << len(flips) < seq_count:
            flips.append(cuts << len(flips))
        held = swap(held, [flips[0], flips[-1]])
    out = attend(part, pieces, chunks, group, rows)
    out, held = lax.optimization_barrier((out, held))
    home = lax.all_to_all(out, "seq", split_axis=0, concat_axis=0)
    home, held = lax.optimization_barrier((home, held))

    def spread(step, last):
        nonlocal held
        if held and step == 2:
            for stage in range(1, len(flips)):
                held = swap(held, [flips[stage], flips[-1 - stage]])
            last, held = lax.optimization_barrier((last, held))
        return last

    found = line_gather([home[: seq_count // 2], home[seq_count // 2 :]], tensor_count, spread)
    weights = [jnp.concatenate([blocks[k] for k in sorted(blocks)], axis=0) for blocks in held]
    for turn in range(1, cuts):
        ring = [(d, d - d % cuts + (d - turn) % cuts) for d in range(seq_count)]
        weights += [lax.ppermute(weights[half], "seq", ring) for half in range(len(held))]
    if not held:
        weights = [lax.all_to_all(w_out, "tensor", split_axis=1, concat_axis=0, tiled=True)]
    cut_of, at = output_order(w_out, seq_count, tensor_count, columns)
    scalars = jnp.stack([me, *cut_of])
    return output(scalars, at, sum(found, []), weights, hidden, active, chunks, group, 2)


def solution(mesh):
    return jax.shard_map(
        shards,
        mesh=mesh,
        in_specs=(
            P("seq", "tensor"),
            P("seq"),
            P(),
            P(None, "tensor"),
            P(None, "tensor"),
            P(None, "tensor"),
            P("tensor", None),
        ),
        out_specs=P("seq", "tensor"),
        check_vma=False,
    )
```

```python
import math
from functools import partial

import jax
import jax.numpy as jnp
from jax import lax
from jax.experimental import pallas as pl
from jax.experimental.pallas import tpu as pltpu
from jax.sharding import PartitionSpec as P

HEAD = 128
MASKED = -1e30
ASIDE = 2.0**100
LIMIT = 63 * 2**20


def sources(me, count):
    found = [(me, None)]
    for step in range(count - 1):
        found.append((me - 1 - step, me - 1 - step >= 0))
        found.append((me + 1 + step, me + 1 + step < count))
    return found


def when(there, act):
    if there is None:
        act()
    else:
        pl.when(there)(act)


def line_gather(chunks, count, join):
    right = [(d, d + 1) for d in range(count - 1)]
    left = [(d + 1, d) for d in range(count - 1)]
    found = [[chunk] for chunk in chunks]
    last = [(chunk, chunk) for chunk in chunks]
    for step in range(count - 1):
        last = join(step, last)
        for at in range(len(chunks)):
            from_left = lax.ppermute(last[at][0], "tensor", right[step:])
            from_right = lax.ppermute(last[at][1], "tensor", left[: count - 1 - step])
            last[at] = (from_left, from_right)
            found[at] += [from_left, from_right]
    return found


def project_kernel(group, count, me_ref, gain_ref, active_ref, *refs):
    matrices = refs[:3]
    pieces = refs[3:-5]
    out_ref, normed, held, piece_in, weight_in = refs[-5:]
    found = sources(me_ref[0], count)
    chunk_rows, width = pieces[0].shape
    chunks = len(pieces) // len(found)
    rows = chunks * chunk_rows

    def copy_of(number):
        chunk, (source, there) = number // len(found), found[number % len(found)]
        to = normed.at[source, chunk * chunk_rows : (chunk + 1) * chunk_rows, :]
        return there, lambda: pltpu.make_async_copy(
            pieces[number], to, piece_in.at[chunk, source]
        )

    for number in range(len(pieces)):
        there, copy = copy_of(number)
        when(there, lambda: copy().start())
    copies = [
        [
            pltpu.make_async_copy(
                matrix.at[step * width : (step + 1) * width, :],
                held.at[step, which],
                weight_in.at[step, which],
            )
            for which, matrix in enumerate(matrices)
        ]
        for step in range(count)
    ]
    for step in range(count):
        for copy in copies[step]:
            copy.start()
    for number in range(len(pieces)):
        there, copy = copy_of(number)
        when(there, lambda: copy().wait())

    square = jnp.zeros((rows, 1), jnp.float32)
    for source in range(count):
        values = normed[source].astype(jnp.float32)
        square = square + jnp.sum(values * values, axis=1, keepdims=True)
    row_scale = lax.rsqrt(square / (count * width) + 1e-05)
    for source in range(count):
        values = normed[source].astype(jnp.float32) * row_scale * gain_ref[source : source + 1, :]
        normed[source] = values.astype(jnp.bfloat16)
    part_rows = chunk_rows // group
    totals = [None] * 3
    for step in range(count):
        for which in range(3):
            copies[step][which].wait()
            product = jnp.dot(normed[step], held[step, which], preferred_element_type=jnp.float32)
            totals[which] = product if step == 0 else totals[which] + product
    for which, total in enumerate(totals):
        if which == 0:
            total = jnp.where(active_ref[...] > 0, total, ASIDE)
        total = total.astype(jnp.bfloat16)
        for head in range(total.shape[1] // HEAD):
            for part in range(group):
                for chunk in range(chunks):
                    first = chunk * chunk_rows + part * part_rows
                    out_ref[
                        head * group + part,
                        chunk * part_rows : (chunk + 1) * part_rows,
                        which * HEAD : (which + 1) * HEAD,
                    ] = total[first : first + part_rows, head * HEAD : (head + 1) * HEAD]


def project(me, pieces, active, gain, wq, wk, wv, seq_count, group):
    columns = pieces[0].shape[1]
    rows = active.shape[0]
    features, width = wq.shape
    count = features // columns
    vmem = pl.BlockSpec(memory_space=pltpu.VMEM)
    return pl.pallas_call(
        partial(project_kernel, group, count),
        in_specs=[pl.BlockSpec(memory_space=pltpu.SMEM), vmem, vmem]
        + [pl.BlockSpec(memory_space=pl.ANY)] * (3 + len(pieces)),
        out_specs=vmem,
        out_shape=jax.ShapeDtypeStruct((seq_count, rows // group, 3 * HEAD), jnp.bfloat16),
        scratch_shapes=[
            pltpu.VMEM((count, rows, columns), jnp.bfloat16),
            pltpu.VMEM((count, 3, columns, width), jnp.bfloat16),
            pltpu.SemaphoreType.DMA((rows // pieces[0].shape[0], count)),
            pltpu.SemaphoreType.DMA((count, 3)),
        ],
        compiler_params=pltpu.CompilerParams(vmem_limit_bytes=LIMIT),
        cost_estimate=pl.CostEstimate(
            flops=6 * rows * features * width,
            bytes_accessed=6 * features * width + 2 * rows * (features + 3 * width),
            transcendentals=0,
        ),
    )(me, gain, active, wq, wk, wv, *pieces)


def attend_kernel(chunks, group, rows, part_ref, *refs):
    pieces = refs[:-3]
    out_ref, keys, values = refs[-3:]
    seq_count = pieces[0].shape[0]
    chunk_rows = rows // chunks
    part_rows = chunk_rows // group
    part = part_ref[0]

    def place(home, _):
        chunk = 0
        for number in range(0, len(pieces), group):
            inside = pieces[number].shape[1] // part_rows
            for step in range(group):
                owner = lax.rem(part + step, group)
                piece = pieces[number + step]
                for at_chunk in range(inside):
                    at = home * rows + (chunk + at_chunk) * chunk_rows + owner * part_rows
                    to = pl.ds(pl.multiple_of(at, part_rows), part_rows)
                    of = slice(at_chunk * part_rows, (at_chunk + 1) * part_rows)
                    aside = piece[home, of, :HEAD].astype(jnp.float32) >= ASIDE
                    keys[to, :HEAD] = piece[home, of, HEAD : 2 * HEAD]
                    keys[to, HEAD:] = jnp.where(aside, MASKED, 0.0).astype(jnp.bfloat16)
                    values[to, :] = piece[home, of, 2 * HEAD :]
            chunk += inside
        return 0

    lax.fori_loop(0, seq_count, place, 0)
    scale = math.log2(math.e) / math.sqrt(HEAD)
    count = chunks * part_rows
    first_lane = lax.broadcasted_iota(jnp.int32, (count, HEAD), 1) == 0
    mask_lane = jnp.where(first_lane, 1.0, 0.0).astype(jnp.bfloat16)
    order = lax.broadcasted_iota(jnp.int32, (count, rows), 0)
    own = order // part_rows * chunk_rows + part * part_rows + order % part_rows
    later = lax.broadcasted_iota(jnp.int32, (count, rows), 1) > own

    def queries_of(home):
        queries = jnp.concatenate(
            [pieces[number][home, :, :HEAD] for number in range(0, len(pieces), group)], axis=0
        )
        return jnp.concatenate([queries, mask_lane], axis=1)

    def scores_of(queries, at):
        return scale * lax.dot_general(
            queries,
            keys[at, :],
            (((1,), (1,)), ((), ())),
            preferred_element_type=jnp.float32,
        )

    if seq_count <= 8:
        for home in range(seq_count):
            queries = queries_of(home)
            blocks = []
            for other in range(home + 1):
                scores = scores_of(queries, slice(other * rows, (other + 1) * rows))
                if other == home:
                    scores = jnp.where(later, MASKED, scores)
                blocks.append(scores)
            scores = jnp.concatenate(blocks, axis=1)
            best = jnp.max(scores, axis=1, keepdims=True)
            weights = jnp.exp2(scores - best)
            total = jnp.sum(weights, axis=1, keepdims=True)
            summed = jnp.dot(
                weights.astype(jnp.bfloat16),
                values[: (home + 1) * rows, :],
                preferred_element_type=jnp.float32,
            )
            out_ref[home] = (summed / total).astype(jnp.bfloat16)
        return

    def one_home(home, _):
        queries = queries_of(home)

        def fold(other, carry, diagonal):
            best, total, summed = carry
            at = pl.ds(pl.multiple_of(other * rows, rows), rows)
            scores = scores_of(queries, at)
            if diagonal:
                scores = jnp.where(later, MASKED, scores)
            newbest = jnp.maximum(best, jnp.max(scores, axis=1, keepdims=True))
            factor = jnp.exp2(best - newbest)
            weights = jnp.exp2(scores - newbest)
            total = total * factor + jnp.sum(weights, axis=1, keepdims=True)
            summed = summed * factor + jnp.dot(
                weights.astype(jnp.bfloat16), values[at, :], preferred_element_type=jnp.float32
            )
            return newbest, total, summed

        start = (
            jnp.full((count, 1), MASKED, jnp.float32),
            jnp.zeros((count, 1), jnp.float32),
            jnp.zeros((count, HEAD), jnp.float32),
        )
        carry = fold(home, start, True)
        carry = lax.fori_loop(0, home, lambda other, c: fold(other, c, False), carry)
        _, total, summed = carry
        out_ref[home] = (summed / total).astype(jnp.bfloat16)
        return 0

    lax.fori_loop(0, seq_count, one_home, 0)


def attend(part, pieces, chunks, group, rows):
    seq_count = pieces[0].shape[0]
    count = rows // group
    vmem = pl.BlockSpec(memory_space=pltpu.VMEM)
    pairs = seq_count * (seq_count + 1) // 2
    return pl.pallas_call(
        partial(attend_kernel, chunks, group, rows),
        in_specs=[pl.BlockSpec(memory_space=pltpu.SMEM)] + [vmem] * len(pieces),
        out_specs=vmem,
        out_shape=jax.ShapeDtypeStruct((seq_count, count, HEAD), jnp.bfloat16),
        scratch_shapes=[
            pltpu.VMEM((seq_count * rows, 2 * HEAD), jnp.bfloat16),
            pltpu.VMEM((seq_count * rows, HEAD), jnp.bfloat16),
        ],
        compiler_params=pltpu.CompilerParams(vmem_limit_bytes=LIMIT),
        cost_estimate=pl.CostEstimate(
            flops=6 * pairs * count * rows * HEAD,
            bytes_accessed=8 * seq_count * rows * HEAD,
            transcendentals=pairs * count * rows,
        ),
    )(part, *pieces)


def output_kernel(group, count, cuts, halves, me_ref, at_ref, active_ref, hidden_ref, *refs):
    weights = refs[:cuts]
    pieces = refs[cuts:-7]
    out_ref, rows_in, held, own, piece_in, weight_in, own_in = refs[-7:]
    heads = pieces[0].shape[0] // group
    found = sources(me_ref[0], count)
    own_copy = pltpu.make_async_copy(hidden_ref, own, own_in)
    weight_copies = [
        pltpu.make_async_copy(weight, held.at[cut], weight_in.at[cut])
        for cut, weight in enumerate(weights)
    ]

    def copies_of(number):
        half, (source, there) = number // len(found), found[number % len(found)]

        def each(act):
            for head in range(heads):
                at = pl.multiple_of(at_ref[(source * halves + half) * heads + head] * HEAD, HEAD)
                for part in range(group):
                    act(
                        pltpu.make_async_copy(
                            pieces[number].at[head * group + part],
                            rows_in.at[:, part, :, pl.ds(at, HEAD)],
                            piece_in.at[half, source, head, part],
                        )
                    )

        return there, each

    for number in range(len(pieces)):
        there, each = copies_of(number)
        when(there, lambda: each(lambda copy: copy.start()))
    weight_copies[0].start()
    own_copy.start()
    for copy in weight_copies[1:]:
        copy.start()
    for number in range(len(pieces)):
        there, each = copies_of(number)
        when(there, lambda: each(lambda copy: copy.wait()))

    rows, width = own.shape[0], held.shape[2]
    x = rows_in[...].reshape(rows, -1)
    for cut in range(cuts):
        weight_copies[cut].wait()
        columns = pl.ds(pl.multiple_of(me_ref[1 + cut] * width, width), width)
        shares = jnp.dot(x, held[cut], preferred_element_type=jnp.float32)
        if cut == 0:
            own_copy.wait()
        hidden = own[:, columns]
        renewed = (hidden.astype(jnp.float32) + shares).astype(jnp.bfloat16)
        out_ref[:, columns] = jnp.where(active_ref[...] > 0, renewed, hidden)


def output(scalars, at, pieces, weights, hidden, active, chunks, group, halves):
    rows, columns = hidden.shape
    depth, width = weights[0].shape
    cuts = len(weights)
    count = (len(pieces) // halves + 1) // 2
    part_rows = rows // chunks // group
    pieces = [piece.reshape(-1, chunks, part_rows, HEAD) for piece in pieces]
    smem = pl.BlockSpec(memory_space=pltpu.SMEM)
    vmem = pl.BlockSpec(memory_space=pltpu.VMEM)
    return pl.pallas_call(
        partial(output_kernel, group, count, cuts, halves),
        in_specs=[smem, smem, vmem]
        + [pl.BlockSpec(memory_space=pl.ANY)] * (1 + cuts + len(pieces)),
        out_specs=vmem,
        out_shape=jax.ShapeDtypeStruct((rows, columns), jnp.bfloat16),
        scratch_shapes=[
            pltpu.VMEM((chunks, group, part_rows, depth), jnp.bfloat16),
            pltpu.VMEM((cuts, depth, width), jnp.bfloat16),
            pltpu.VMEM((rows, columns), jnp.bfloat16),
            pltpu.SemaphoreType.DMA((halves, count, pieces[0].shape[0] // group, group)),
            pltpu.SemaphoreType.DMA((cuts,)),
            pltpu.SemaphoreType.DMA,
        ],
        compiler_params=pltpu.CompilerParams(vmem_limit_bytes=LIMIT),
        cost_estimate=pl.CostEstimate(
            flops=2 * rows * depth * columns,
            bytes_accessed=2 * (rows * depth + depth * columns + 2 * rows * columns),
            transcendentals=0,
        ),
    )(scalars, at, active, hidden, *weights, *pieces)


def share_kernel(place_ref, w_ref, *shares):
    for step, share in enumerate(shares):

        @pl.when(pl.program_id(0) == step)
        def _():
            each = share.shape[2]
            for half in range(share.shape[0]):
                share[half] = w_ref[:, half * each : (half + 1) * each]


def shares_of(w_out, place, count, halves, each):
    width = halves * each
    cuts = w_out.shape[1] // count // width
    return pl.pallas_call(
        share_kernel,
        grid_spec=pltpu.PrefetchScalarGridSpec(
            num_scalar_prefetch=1,
            grid=(count,),
            in_specs=[
                pl.BlockSpec(
                    (HEAD, width),
                    lambda j, place: (place[0], lax.rem(place[2] + j, count) * cuts + place[1]),
                )
            ],
            out_specs=[pl.BlockSpec((halves, HEAD, each), lambda j, place: (0, 0, 0))] * count,
        ),
        out_shape=[jax.ShapeDtypeStruct((halves, HEAD, each), w_out.dtype)] * count,
        compiler_params=pltpu.CompilerParams(vmem_limit_bytes=LIMIT),
    )(place, w_out)


def weight_cuts(w_out, seq_count, columns):
    heads = w_out.shape[0] // HEAD
    cuts = seq_count // heads
    width = columns // cuts
    halves = 2 if width % (2 * HEAD) == 0 else 1
    return heads, cuts, halves, width // halves


def weight_shares(w_out, seq_count, tensor_count, columns):
    heads, cuts, halves, each = weight_cuts(w_out, seq_count, columns)
    if each % HEAD:
        return None
    seq_me = lax.axis_index("seq").astype(jnp.int32)
    me = lax.axis_index("tensor").astype(jnp.int32)
    place = jnp.stack([seq_me // cuts, seq_me % cuts, me])
    return list(shares_of(w_out, place, tensor_count, halves, each))


def send_shares(shares, tensor_count):
    if shares is None:
        return None
    shares = list(shares)
    for step in range(1, tensor_count):
        ring = [(d, (d + step) % tensor_count) for d in range(tensor_count)]
        shares[step] = lax.ppermute(shares[step], "tensor", ring)
    return shares


def swap(held, flips):
    grown = []
    for blocks, flip in zip(held, flips):
        pairs = [(d, d ^ flip) for d in range(lax.axis_size("seq"))]
        sent = list(blocks)
        whole = [blocks[k] for k in sent]
        got = lax.ppermute(
            jnp.concatenate(whole, axis=0) if len(whole) > 1 else whole[0], "seq", pairs
        )
        grown.append(dict(blocks))
        for k, block in zip(sent, jnp.split(got, len(sent))):
            grown[-1][k ^ flip] = block
    return grown


def output_order(w_out, seq_count, tensor_count, columns):
    heads, cuts, halves, each = weight_cuts(w_out, seq_count, columns)
    row = jnp.arange(tensor_count * heads, dtype=jnp.int32)
    if each % HEAD:
        return [jnp.int32(0)], row
    seq_me = lax.axis_index("seq").astype(jnp.int32)
    me = lax.axis_index("tensor").astype(jnp.int32)
    which = [
        (seq_me % cuts + step) % cuts * halves + half for step in range(cuts) for half in range(halves)
    ]
    tensor, of = row // heads, row % heads
    return which, (of ^ (seq_me // cuts)) * tensor_count + (me - tensor) % tensor_count


def shards(hidden, depth, norm_gain, w_query, w_key, w_value, w_out):
    rows, columns = hidden.shape
    seq_count = lax.axis_size("seq")
    tensor_count = lax.axis_size("tensor")
    heads = w_query.shape[1] // HEAD
    group = seq_count // heads
    chunks = 2
    chunk_rows = rows // chunks
    part = (lax.axis_index("seq") % group).astype(jnp.int32).reshape(1)
    me = lax.axis_index("tensor").astype(jnp.int32)
    gain = norm_gain.reshape(tensor_count, columns)
    active = (depth >= 2).astype(jnp.int32).reshape(rows, 1)
    shares = weight_shares(w_out, seq_count, tensor_count, columns)

    def work(found, chunk):
        here = active[chunk * chunk_rows : (chunk + 1) * chunk_rows]
        return project(
            me.reshape(1), found, here, gain, w_query, w_key, w_value, seq_count, group
        )

    def to_heads(sent):
        return lax.all_to_all(sent, "seq", split_axis=0, concat_axis=0)

    def to_parts(got):
        rings = [
            [(d, d - d % group + (d - step) % group) for d in range(seq_count)]
            for step in range(1, group)
        ]
        return [got] + [lax.ppermute(got, "seq", ring) for ring in rings]

    def cut_weight(step, last):
        nonlocal shares
        if step == 1:
            last[1], shares = lax.optimization_barrier((last[1], shares))
        return last

    first, second = line_gather(
        [hidden[:chunk_rows], hidden[chunk_rows:]], tensor_count, cut_weight
    )
    early, second = lax.optimization_barrier((work(first, 0), second))
    sent, early, shares = lax.optimization_barrier((work(second, 1), to_heads(early), shares))
    sending = send_shares(shares, tensor_count)
    late, sending = lax.optimization_barrier((to_heads(sent), sending))
    pieces = to_parts(early) + to_parts(late)

    heads, cuts, halves, _ = weight_cuts(w_out, seq_count, columns)
    held, flips = [], []
    if sending is not None:
        held = [
            {0: jnp.concatenate([share[half] for share in sending], axis=0)}
            for half in range(halves)
        ]
        while cuts << len(flips) < seq_count:
            flips.append(cuts << len(flips))
        held = swap(held, [flips[0], flips[-1]])
    out = attend(part, pieces, chunks, group, rows)
    out, held = lax.optimization_barrier((out, held))
    home = lax.all_to_all(out, "seq", split_axis=0, concat_axis=0)
    home, held = lax.optimization_barrier((home, held))
    weights = []

    def spread(step, last):
        nonlocal held, weights
        if held and step == 1:
            for stage in range(1, len(flips)):
                held = swap(held, [flips[stage], flips[-1 - stage]])
            last, held = lax.optimization_barrier((last, held))
        if held and step == 2:
            weights = [
                jnp.concatenate([blocks[k] for k in sorted(blocks)], axis=0) for blocks in held
            ]
            for turn in range(1, cuts):
                ring = [(d, d - d % cuts + (d - turn) % cuts) for d in range(seq_count)]
                weights += [lax.ppermute(weights[half], "seq", ring) for half in range(halves)]
            last, weights = lax.optimization_barrier((last, weights))
        return last

    (found,) = line_gather([home], tensor_count, spread)
    if not held:
        weights = [lax.all_to_all(w_out, "tensor", split_axis=1, concat_axis=0, tiled=True)]
    cut_of, at = output_order(w_out, seq_count, tensor_count, columns)
    scalars = jnp.stack([me, *cut_of])
    return output(scalars, at, found, weights, hidden, active, chunks, group, 1)


def solution(mesh):
    return jax.shard_map(
        shards,
        mesh=mesh,
        in_specs=(
            P("seq", "tensor"),
            P("seq"),
            P(),
            P(None, "tensor"),
            P(None, "tensor"),
            P(None, "tensor"),
            P("tensor", None),
        ),
        out_specs=P("seq", "tensor"),
        check_vma=False,
    )
```

```python
import math
from functools import partial

import jax
import jax.numpy as jnp
from jax import lax
from jax.experimental import pallas as pl
from jax.experimental.pallas import tpu as pltpu
from jax.sharding import PartitionSpec as P

HEAD = 128
MASKED = -1e30
ASIDE = 2.0**100
LIMIT = 63 * 2**20


def sources(me, count):
    found = [(me, None)]
    for step in range(count - 1):
        found.append((me - 1 - step, me - 1 - step >= 0))
        found.append((me + 1 + step, me + 1 + step < count))
    return found


def when(there, act):
    if there is None:
        act()
    else:
        pl.when(there)(act)


def line_gather(chunks, count, join):
    right = [(d, d + 1) for d in range(count - 1)]
    left = [(d + 1, d) for d in range(count - 1)]
    found = [[chunk] for chunk in chunks]
    last = [(chunk, chunk) for chunk in chunks]
    for step in range(count - 1):
        last = join(step, last)
        for at in range(len(chunks)):
            from_left = lax.ppermute(last[at][0], "tensor", right[step:])
            from_right = lax.ppermute(last[at][1], "tensor", left[: count - 1 - step])
            last[at] = (from_left, from_right)
            found[at] += [from_left, from_right]
    return found


def project_kernel(group, count, me_ref, gain_ref, active_ref, *refs):
    matrices = refs[:3]
    pieces = refs[3:-5]
    out_ref, normed, held, piece_in, weight_in = refs[-5:]
    found = sources(me_ref[0], count)
    chunk_rows, width = pieces[0].shape
    chunks = len(pieces) // len(found)
    rows = chunks * chunk_rows

    def copy_of(number):
        chunk, (source, there) = number // len(found), found[number % len(found)]
        to = normed.at[source, chunk * chunk_rows : (chunk + 1) * chunk_rows, :]
        return there, lambda: pltpu.make_async_copy(
            pieces[number], to, piece_in.at[chunk, source]
        )

    for number in range(len(pieces)):
        there, copy = copy_of(number)
        when(there, lambda: copy().start())
    copies = [
        [
            pltpu.make_async_copy(
                matrix.at[step * width : (step + 1) * width, :],
                held.at[step, which],
                weight_in.at[step, which],
            )
            for which, matrix in enumerate(matrices)
        ]
        for step in range(count)
    ]
    for step in range(count):
        for copy in copies[step]:
            copy.start()
    for number in range(len(pieces)):
        there, copy = copy_of(number)
        when(there, lambda: copy().wait())

    square = jnp.zeros((rows, 1), jnp.float32)
    for source in range(count):
        values = normed[source].astype(jnp.float32)
        square = square + jnp.sum(values * values, axis=1, keepdims=True)
    row_scale = lax.rsqrt(square / (count * width) + 1e-05)
    for source in range(count):
        values = normed[source].astype(jnp.float32) * row_scale * gain_ref[source : source + 1, :]
        normed[source] = values.astype(jnp.bfloat16)
    part_rows = chunk_rows // group
    totals = [None] * 3
    for step in range(count):
        for which in range(3):
            copies[step][which].wait()
            product = jnp.dot(normed[step], held[step, which], preferred_element_type=jnp.float32)
            totals[which] = product if step == 0 else totals[which] + product
    for which, total in enumerate(totals):
        if which == 0:
            total = jnp.where(active_ref[...] > 0, total, ASIDE)
        total = total.astype(jnp.bfloat16)
        for head in range(total.shape[1] // HEAD):
            for part in range(group):
                for chunk in range(chunks):
                    first = chunk * chunk_rows + part * part_rows
                    out_ref[
                        head * group + part,
                        chunk * part_rows : (chunk + 1) * part_rows,
                        which * HEAD : (which + 1) * HEAD,
                    ] = total[first : first + part_rows, head * HEAD : (head + 1) * HEAD]


def project(me, pieces, active, gain, wq, wk, wv, seq_count, group):
    columns = pieces[0].shape[1]
    rows = active.shape[0]
    features, width = wq.shape
    count = features // columns
    vmem = pl.BlockSpec(memory_space=pltpu.VMEM)
    return pl.pallas_call(
        partial(project_kernel, group, count),
        in_specs=[pl.BlockSpec(memory_space=pltpu.SMEM), vmem, vmem]
        + [pl.BlockSpec(memory_space=pl.ANY)] * (3 + len(pieces)),
        out_specs=vmem,
        out_shape=jax.ShapeDtypeStruct((seq_count, rows // group, 3 * HEAD), jnp.bfloat16),
        scratch_shapes=[
            pltpu.VMEM((count, rows, columns), jnp.bfloat16),
            pltpu.VMEM((count, 3, columns, width), jnp.bfloat16),
            pltpu.SemaphoreType.DMA((rows // pieces[0].shape[0], count)),
            pltpu.SemaphoreType.DMA((count, 3)),
        ],
        compiler_params=pltpu.CompilerParams(vmem_limit_bytes=LIMIT),
        cost_estimate=pl.CostEstimate(
            flops=6 * rows * features * width,
            bytes_accessed=6 * features * width + 2 * rows * (features + 3 * width),
            transcendentals=0,
        ),
    )(me, gain, active, wq, wk, wv, *pieces)


def attend_kernel(chunks, group, rows, part_ref, *refs):
    pieces = refs[:-3]
    out_ref, keys, values = refs[-3:]
    seq_count = pieces[0].shape[0]
    chunk_rows = rows // chunks
    part_rows = chunk_rows // group
    part = part_ref[0]

    def place(home, _):
        chunk = 0
        for number in range(0, len(pieces), group):
            inside = pieces[number].shape[1] // part_rows
            for step in range(group):
                owner = lax.rem(part + step, group)
                piece = pieces[number + step]
                for at_chunk in range(inside):
                    at = home * rows + (chunk + at_chunk) * chunk_rows + owner * part_rows
                    to = pl.ds(pl.multiple_of(at, part_rows), part_rows)
                    of = slice(at_chunk * part_rows, (at_chunk + 1) * part_rows)
                    aside = piece[home, of, :HEAD].astype(jnp.float32) >= ASIDE
                    keys[to, :HEAD] = piece[home, of, HEAD : 2 * HEAD]
                    keys[to, HEAD:] = jnp.where(aside, MASKED, 0.0).astype(jnp.bfloat16)
                    values[to, :] = piece[home, of, 2 * HEAD :]
            chunk += inside
        return 0

    lax.fori_loop(0, seq_count, place, 0)
    scale = math.log2(math.e) / math.sqrt(HEAD)
    count = chunks * part_rows
    first_lane = lax.broadcasted_iota(jnp.int32, (count, HEAD), 1) == 0
    mask_lane = jnp.where(first_lane, 1.0, 0.0).astype(jnp.bfloat16)
    order = lax.broadcasted_iota(jnp.int32, (count, rows), 0)
    own = order // part_rows * chunk_rows + part * part_rows + order % part_rows
    later = lax.broadcasted_iota(jnp.int32, (count, rows), 1) > own

    def queries_of(home):
        queries = jnp.concatenate(
            [pieces[number][home, :, :HEAD] for number in range(0, len(pieces), group)], axis=0
        )
        return jnp.concatenate([queries, mask_lane], axis=1)

    def scores_of(queries, at):
        return scale * lax.dot_general(
            queries,
            keys[at, :],
            (((1,), (1,)), ((), ())),
            preferred_element_type=jnp.float32,
        )

    if seq_count <= 8:
        for home in range(seq_count):
            queries = queries_of(home)
            blocks = []
            for other in range(home + 1):
                scores = scores_of(queries, slice(other * rows, (other + 1) * rows))
                if other == home:
                    scores = jnp.where(later, MASKED, scores)
                blocks.append(scores)
            scores = jnp.concatenate(blocks, axis=1)
            best = jnp.max(scores, axis=1, keepdims=True)
            weights = jnp.exp2(scores - best)
            total = jnp.sum(weights, axis=1, keepdims=True)
            summed = jnp.dot(
                weights.astype(jnp.bfloat16),
                values[: (home + 1) * rows, :],
                preferred_element_type=jnp.float32,
            )
            out_ref[home] = (summed / total).astype(jnp.bfloat16)
        return

    def one_home(home, _):
        queries = queries_of(home)

        def fold(other, carry, diagonal):
            best, total, summed = carry
            at = pl.ds(pl.multiple_of(other * rows, rows), rows)
            scores = scores_of(queries, at)
            if diagonal:
                scores = jnp.where(later, MASKED, scores)
            newbest = jnp.maximum(best, jnp.max(scores, axis=1, keepdims=True))
            factor = jnp.exp2(best - newbest)
            weights = jnp.exp2(scores - newbest)
            total = total * factor + jnp.sum(weights, axis=1, keepdims=True)
            summed = summed * factor + jnp.dot(
                weights.astype(jnp.bfloat16), values[at, :], preferred_element_type=jnp.float32
            )
            return newbest, total, summed

        start = (
            jnp.full((count, 1), MASKED, jnp.float32),
            jnp.zeros((count, 1), jnp.float32),
            jnp.zeros((count, HEAD), jnp.float32),
        )
        carry = fold(home, start, True)
        carry = lax.fori_loop(0, home, lambda other, c: fold(other, c, False), carry)
        _, total, summed = carry
        out_ref[home] = (summed / total).astype(jnp.bfloat16)
        return 0

    lax.fori_loop(0, seq_count, one_home, 0)


def attend(part, pieces, chunks, group, rows):
    seq_count = pieces[0].shape[0]
    count = rows // group
    vmem = pl.BlockSpec(memory_space=pltpu.VMEM)
    pairs = seq_count * (seq_count + 1) // 2
    return pl.pallas_call(
        partial(attend_kernel, chunks, group, rows),
        in_specs=[pl.BlockSpec(memory_space=pltpu.SMEM)] + [vmem] * len(pieces),
        out_specs=vmem,
        out_shape=jax.ShapeDtypeStruct((seq_count, count, HEAD), jnp.bfloat16),
        scratch_shapes=[
            pltpu.VMEM((seq_count * rows, 2 * HEAD), jnp.bfloat16),
            pltpu.VMEM((seq_count * rows, HEAD), jnp.bfloat16),
        ],
        compiler_params=pltpu.CompilerParams(vmem_limit_bytes=LIMIT),
        cost_estimate=pl.CostEstimate(
            flops=6 * pairs * count * rows * HEAD,
            bytes_accessed=8 * seq_count * rows * HEAD,
            transcendentals=pairs * count * rows,
        ),
    )(part, *pieces)


def output_kernel(group, count, cuts, halves, me_ref, at_ref, active_ref, hidden_ref, *refs):
    weights = refs[:cuts]
    pieces = refs[cuts:-7]
    out_ref, rows_in, held, own, piece_in, weight_in, own_in = refs[-7:]
    heads = pieces[0].shape[0] // group
    found = sources(me_ref[0], count)
    own_copy = pltpu.make_async_copy(hidden_ref, own, own_in)
    weight_copies = [
        pltpu.make_async_copy(weight, held.at[cut], weight_in.at[cut])
        for cut, weight in enumerate(weights)
    ]

    def copies_of(number):
        half, (source, there) = number // len(found), found[number % len(found)]

        def each(act):
            for head in range(heads):
                at = pl.multiple_of(at_ref[(source * halves + half) * heads + head] * HEAD, HEAD)
                for part in range(group):
                    act(
                        pltpu.make_async_copy(
                            pieces[number].at[head * group + part],
                            rows_in.at[:, part, :, pl.ds(at, HEAD)],
                            piece_in.at[half, source, head, part],
                        )
                    )

        return there, each

    for number in range(len(pieces)):
        there, each = copies_of(number)
        when(there, lambda: each(lambda copy: copy.start()))
    weight_copies[0].start()
    own_copy.start()
    for copy in weight_copies[1:]:
        copy.start()
    for number in range(len(pieces)):
        there, each = copies_of(number)
        when(there, lambda: each(lambda copy: copy.wait()))

    rows, width = own.shape[0], held.shape[2]
    x = rows_in[...].reshape(rows, -1)
    for cut in range(cuts):
        weight_copies[cut].wait()
        columns = pl.ds(pl.multiple_of(me_ref[1 + cut] * width, width), width)
        shares = jnp.dot(x, held[cut], preferred_element_type=jnp.float32)
        if cut == 0:
            own_copy.wait()
        hidden = own[:, columns]
        renewed = (hidden.astype(jnp.float32) + shares).astype(jnp.bfloat16)
        out_ref[:, columns] = jnp.where(active_ref[...] > 0, renewed, hidden)


def output(scalars, at, pieces, weights, hidden, active, chunks, group, halves):
    rows, columns = hidden.shape
    depth, width = weights[0].shape
    cuts = len(weights)
    count = (len(pieces) // halves + 1) // 2
    part_rows = rows // chunks // group
    pieces = [piece.reshape(-1, chunks, part_rows, HEAD) for piece in pieces]
    smem = pl.BlockSpec(memory_space=pltpu.SMEM)
    vmem = pl.BlockSpec(memory_space=pltpu.VMEM)
    return pl.pallas_call(
        partial(output_kernel, group, count, cuts, halves),
        in_specs=[smem, smem, vmem]
        + [pl.BlockSpec(memory_space=pl.ANY)] * (1 + cuts + len(pieces)),
        out_specs=vmem,
        out_shape=jax.ShapeDtypeStruct((rows, columns), jnp.bfloat16),
        scratch_shapes=[
            pltpu.VMEM((chunks, group, part_rows, depth), jnp.bfloat16),
            pltpu.VMEM((cuts, depth, width), jnp.bfloat16),
            pltpu.VMEM((rows, columns), jnp.bfloat16),
            pltpu.SemaphoreType.DMA((halves, count, pieces[0].shape[0] // group, group)),
            pltpu.SemaphoreType.DMA((cuts,)),
            pltpu.SemaphoreType.DMA,
        ],
        compiler_params=pltpu.CompilerParams(vmem_limit_bytes=LIMIT),
        cost_estimate=pl.CostEstimate(
            flops=2 * rows * depth * columns,
            bytes_accessed=2 * (rows * depth + depth * columns + 2 * rows * columns),
            transcendentals=0,
        ),
    )(scalars, at, active, hidden, *weights, *pieces)


def share_kernel(place_ref, w_ref, *shares):
    for step, share in enumerate(shares):

        @pl.when(pl.program_id(0) == step)
        def _():
            each = share.shape[2]
            for half in range(share.shape[0]):
                share[half] = w_ref[:, half * each : (half + 1) * each]


def shares_of(w_out, place, count, halves, each):
    width = halves * each
    cuts = w_out.shape[1] // count // width
    return pl.pallas_call(
        share_kernel,
        grid_spec=pltpu.PrefetchScalarGridSpec(
            num_scalar_prefetch=1,
            grid=(count,),
            in_specs=[
                pl.BlockSpec(
                    (HEAD, width),
                    lambda j, place: (place[0], lax.rem(place[2] + j, count) * cuts + place[1]),
                )
            ],
            out_specs=[pl.BlockSpec((halves, HEAD, each), lambda j, place: (0, 0, 0))] * count,
        ),
        out_shape=[jax.ShapeDtypeStruct((halves, HEAD, each), w_out.dtype)] * count,
        compiler_params=pltpu.CompilerParams(vmem_limit_bytes=LIMIT),
    )(place, w_out)


def weight_cuts(w_out, seq_count, columns):
    heads = w_out.shape[0] // HEAD
    cuts = seq_count // heads
    width = columns // cuts
    halves = 2 if width % (2 * HEAD) == 0 else 1
    return heads, cuts, halves, width // halves


def weight_shares(w_out, seq_count, tensor_count, columns):
    heads, cuts, halves, each = weight_cuts(w_out, seq_count, columns)
    if each % HEAD:
        return None
    seq_me = lax.axis_index("seq").astype(jnp.int32)
    me = lax.axis_index("tensor").astype(jnp.int32)
    place = jnp.stack([seq_me // cuts, seq_me % cuts, me])
    return list(shares_of(w_out, place, tensor_count, halves, each))


def send_shares(shares, tensor_count):
    if shares is None:
        return None
    shares = list(shares)
    for step in range(1, tensor_count):
        ring = [(d, (d + step) % tensor_count) for d in range(tensor_count)]
        shares[step] = lax.ppermute(shares[step], "tensor", ring)
    return shares


def swap(held, flips):
    grown = []
    for blocks, flip in zip(held, flips):
        pairs = [(d, d ^ flip) for d in range(lax.axis_size("seq"))]
        sent = list(blocks)
        whole = [blocks[k] for k in sent]
        got = lax.ppermute(
            jnp.concatenate(whole, axis=0) if len(whole) > 1 else whole[0], "seq", pairs
        )
        grown.append(dict(blocks))
        for k, block in zip(sent, jnp.split(got, len(sent))):
            grown[-1][k ^ flip] = block
    return grown


def output_order(w_out, seq_count, tensor_count, columns):
    heads, cuts, halves, each = weight_cuts(w_out, seq_count, columns)
    row = jnp.arange(tensor_count * heads, dtype=jnp.int32)
    if each % HEAD:
        return [jnp.int32(0)], row
    seq_me = lax.axis_index("seq").astype(jnp.int32)
    me = lax.axis_index("tensor").astype(jnp.int32)
    which = [
        (seq_me % cuts + step) % cuts * halves + half for step in range(cuts) for half in range(halves)
    ]
    tensor, of = row // heads, row % heads
    return which, (of ^ (seq_me // cuts)) * tensor_count + (me - tensor) % tensor_count


def shards(hidden, depth, norm_gain, w_query, w_key, w_value, w_out):
    rows, columns = hidden.shape
    seq_count = lax.axis_size("seq")
    tensor_count = lax.axis_size("tensor")
    heads = w_query.shape[1] // HEAD
    group = seq_count // heads
    chunks = 2
    chunk_rows = rows // chunks
    part = (lax.axis_index("seq") % group).astype(jnp.int32).reshape(1)
    me = lax.axis_index("tensor").astype(jnp.int32)
    gain = norm_gain.reshape(tensor_count, columns)
    active = (depth >= 2).astype(jnp.int32).reshape(rows, 1)
    shares = weight_shares(w_out, seq_count, tensor_count, columns)

    def work(found, chunk):
        here = active[chunk * chunk_rows : (chunk + 1) * chunk_rows]
        return project(
            me.reshape(1), found, here, gain, w_query, w_key, w_value, seq_count, group
        )

    def to_heads(sent):
        return lax.all_to_all(sent, "seq", split_axis=0, concat_axis=0)

    def to_parts(got):
        rings = [
            [(d, d - d % group + (d - step) % group) for d in range(seq_count)]
            for step in range(1, group)
        ]
        return [got] + [lax.ppermute(got, "seq", ring) for ring in rings]

    def cut_weight(step, last):
        nonlocal shares
        if step == 1:
            last[1], shares = lax.optimization_barrier((last[1], shares))
        return last

    first, second = line_gather(
        [hidden[:chunk_rows], hidden[chunk_rows:]], tensor_count, cut_weight
    )
    early, second = lax.optimization_barrier((work(first, 0), second))
    sent, early, shares = lax.optimization_barrier((work(second, 1), to_heads(early), shares))
    sending = send_shares(shares, tensor_count)
    late, sending = lax.optimization_barrier((to_heads(sent), sending))
    pieces = to_parts(early) + to_parts(late)

    heads, cuts, halves, _ = weight_cuts(w_out, seq_count, columns)
    held, flips = [], []
    if sending is not None:
        held = [
            {0: jnp.concatenate([share[half] for share in sending], axis=0)}
            for half in range(halves)
        ]
        while cuts << len(flips) < seq_count:
            flips.append(cuts << len(flips))
        held = swap(held, [flips[0], flips[-1]])
    out = attend(part, pieces, chunks, group, rows)
    out, held = lax.optimization_barrier((out, held))
    home = lax.all_to_all(out, "seq", split_axis=0, concat_axis=0)
    for stage in range(1, len(flips)):
        held = swap(held, [flips[stage], flips[-1 - stage]])
    home, held = lax.optimization_barrier((home, held))
    found = line_gather(
        [home[: seq_count // 2], home[seq_count // 2 :]], tensor_count, lambda step, last: last
    )
    weights = [jnp.concatenate([blocks[k] for k in sorted(blocks)], axis=0) for blocks in held]
    for turn in range(1, cuts):
        ring = [(d, d - d % cuts + (d - turn) % cuts) for d in range(seq_count)]
        weights += [lax.ppermute(weights[half], "seq", ring) for half in range(len(held))]
    if not held:
        weights = [lax.all_to_all(w_out, "tensor", split_axis=1, concat_axis=0, tiled=True)]
    cut_of, at = output_order(w_out, seq_count, tensor_count, columns)
    scalars = jnp.stack([me, *cut_of])
    return output(scalars, at, sum(found, []), weights, hidden, active, chunks, group, 2)


def solution(mesh):
    return jax.shard_map(
        shards,
        mesh=mesh,
        in_specs=(
            P("seq", "tensor"),
            P("seq"),
            P(),
            P(None, "tensor"),
            P(None, "tensor"),
            P(None, "tensor"),
            P("tensor", None),
        ),
        out_specs=P("seq", "tensor"),
        check_vma=False,
    )
```

```python
import math
from functools import partial

import jax
import jax.numpy as jnp
from jax import lax
from jax.experimental import pallas as pl
from jax.experimental.pallas import tpu as pltpu
from jax.sharding import PartitionSpec as P

HEAD = 128
MASKED = -1e30
ASIDE = 2.0**100
LIMIT = 63 * 2**20


def sources(me, count):
    found = [(me, None)]
    for step in range(count - 1):
        found.append((me - 1 - step, me - 1 - step >= 0))
        found.append((me + 1 + step, me + 1 + step < count))
    return found


def when(there, act):
    if there is None:
        act()
    else:
        pl.when(there)(act)


def line_gather(chunks, count, join):
    right = [(d, d + 1) for d in range(count - 1)]
    left = [(d + 1, d) for d in range(count - 1)]
    found = [[chunk] for chunk in chunks]
    last = [(chunk, chunk) for chunk in chunks]
    for step in range(count - 1):
        last = join(step, last)
        for at in range(len(chunks)):
            from_left = lax.ppermute(last[at][0], "tensor", right[step:])
            from_right = lax.ppermute(last[at][1], "tensor", left[: count - 1 - step])
            last[at] = (from_left, from_right)
            found[at] += [from_left, from_right]
    return found


def project_kernel(group, count, me_ref, gain_ref, active_ref, *refs):
    matrices = refs[:3]
    pieces = refs[3:-5]
    out_ref, normed, held, piece_in, weight_in = refs[-5:]
    found = sources(me_ref[0], count)
    chunk_rows, width = pieces[0].shape
    chunks = len(pieces) // len(found)
    rows = chunks * chunk_rows

    def copy_of(number):
        chunk, (source, there) = number // len(found), found[number % len(found)]
        to = normed.at[source, chunk * chunk_rows : (chunk + 1) * chunk_rows, :]
        return there, lambda: pltpu.make_async_copy(
            pieces[number], to, piece_in.at[chunk, source]
        )

    for number in range(len(pieces)):
        there, copy = copy_of(number)
        when(there, lambda: copy().start())
    copies = [
        [
            pltpu.make_async_copy(
                matrix.at[step * width : (step + 1) * width, :],
                held.at[step, which],
                weight_in.at[step, which],
            )
            for which, matrix in enumerate(matrices)
        ]
        for step in range(count)
    ]
    for step in range(count):
        for copy in copies[step]:
            copy.start()
    for number in range(len(pieces)):
        there, copy = copy_of(number)
        when(there, lambda: copy().wait())

    square = jnp.zeros((rows, 1), jnp.float32)
    for source in range(count):
        values = normed[source].astype(jnp.float32)
        square = square + jnp.sum(values * values, axis=1, keepdims=True)
    row_scale = lax.rsqrt(square / (count * width) + 1e-05)
    for source in range(count):
        values = normed[source].astype(jnp.float32) * row_scale * gain_ref[source : source + 1, :]
        normed[source] = values.astype(jnp.bfloat16)
    part_rows = chunk_rows // group
    totals = [None] * 3
    for step in range(count):
        for which in range(3):
            copies[step][which].wait()
            product = jnp.dot(normed[step], held[step, which], preferred_element_type=jnp.float32)
            totals[which] = product if step == 0 else totals[which] + product
    for which, total in enumerate(totals):
        if which == 0:
            total = jnp.where(active_ref[...] > 0, total, ASIDE)
        total = total.astype(jnp.bfloat16)
        for head in range(total.shape[1] // HEAD):
            for part in range(group):
                for chunk in range(chunks):
                    first = chunk * chunk_rows + part * part_rows
                    out_ref[
                        head * group + part,
                        chunk * part_rows : (chunk + 1) * part_rows,
                        which * HEAD : (which + 1) * HEAD,
                    ] = total[first : first + part_rows, head * HEAD : (head + 1) * HEAD]


def project(me, pieces, active, gain, wq, wk, wv, seq_count, group):
    columns = pieces[0].shape[1]
    rows = active.shape[0]
    features, width = wq.shape
    count = features // columns
    vmem = pl.BlockSpec(memory_space=pltpu.VMEM)
    return pl.pallas_call(
        partial(project_kernel, group, count),
        in_specs=[pl.BlockSpec(memory_space=pltpu.SMEM), vmem, vmem]
        + [pl.BlockSpec(memory_space=pl.ANY)] * (3 + len(pieces)),
        out_specs=vmem,
        out_shape=jax.ShapeDtypeStruct((seq_count, rows // group, 3 * HEAD), jnp.bfloat16),
        scratch_shapes=[
            pltpu.VMEM((count, rows, columns), jnp.bfloat16),
            pltpu.VMEM((count, 3, columns, width), jnp.bfloat16),
            pltpu.SemaphoreType.DMA((rows // pieces[0].shape[0], count)),
            pltpu.SemaphoreType.DMA((count, 3)),
        ],
        compiler_params=pltpu.CompilerParams(vmem_limit_bytes=LIMIT),
        cost_estimate=pl.CostEstimate(
            flops=6 * rows * features * width,
            bytes_accessed=6 * features * width + 2 * rows * (features + 3 * width),
            transcendentals=0,
        ),
    )(me, gain, active, wq, wk, wv, *pieces)


def attend_kernel(chunks, group, rows, part_ref, *refs):
    pieces = refs[:-3]
    out_ref, keys, values = refs[-3:]
    seq_count = pieces[0].shape[0]
    chunk_rows = rows // chunks
    part_rows = chunk_rows // group
    part = part_ref[0]

    def place(home, _):
        chunk = 0
        for number in range(0, len(pieces), group):
            inside = pieces[number].shape[1] // part_rows
            for step in range(group):
                owner = lax.rem(part + step, group)
                piece = pieces[number + step]
                for at_chunk in range(inside):
                    at = home * rows + (chunk + at_chunk) * chunk_rows + owner * part_rows
                    to = pl.ds(pl.multiple_of(at, part_rows), part_rows)
                    of = slice(at_chunk * part_rows, (at_chunk + 1) * part_rows)
                    aside = piece[home, of, :HEAD].astype(jnp.float32) >= ASIDE
                    keys[to, :HEAD] = piece[home, of, HEAD : 2 * HEAD]
                    keys[to, HEAD:] = jnp.where(aside, MASKED, 0.0).astype(jnp.bfloat16)
                    values[to, :] = piece[home, of, 2 * HEAD :]
            chunk += inside
        return 0

    lax.fori_loop(0, seq_count, place, 0)
    scale = math.log2(math.e) / math.sqrt(HEAD)
    count = chunks * part_rows
    first_lane = lax.broadcasted_iota(jnp.int32, (count, HEAD), 1) == 0
    mask_lane = jnp.where(first_lane, 1.0, 0.0).astype(jnp.bfloat16)
    order = lax.broadcasted_iota(jnp.int32, (count, rows), 0)
    own = order // part_rows * chunk_rows + part * part_rows + order % part_rows
    later = lax.broadcasted_iota(jnp.int32, (count, rows), 1) > own

    def queries_of(home):
        queries = jnp.concatenate(
            [pieces[number][home, :, :HEAD] for number in range(0, len(pieces), group)], axis=0
        )
        return jnp.concatenate([queries, mask_lane], axis=1)

    def scores_of(queries, at):
        return scale * lax.dot_general(
            queries,
            keys[at, :],
            (((1,), (1,)), ((), ())),
            preferred_element_type=jnp.float32,
        )

    if seq_count <= 8:
        for home in range(seq_count):
            queries = queries_of(home)
            blocks = []
            for other in range(home + 1):
                scores = scores_of(queries, slice(other * rows, (other + 1) * rows))
                if other == home:
                    scores = jnp.where(later, MASKED, scores)
                blocks.append(scores)
            scores = jnp.concatenate(blocks, axis=1)
            best = jnp.max(scores, axis=1, keepdims=True)
            weights = jnp.exp2(scores - best)
            total = jnp.sum(weights, axis=1, keepdims=True)
            summed = jnp.dot(
                weights.astype(jnp.bfloat16),
                values[: (home + 1) * rows, :],
                preferred_element_type=jnp.float32,
            )
            out_ref[home] = (summed / total).astype(jnp.bfloat16)
        return

    def one_home(home, _):
        queries = queries_of(home)

        def fold(other, carry, diagonal):
            best, total, summed = carry
            at = pl.ds(pl.multiple_of(other * rows, rows), rows)
            scores = scores_of(queries, at)
            if diagonal:
                scores = jnp.where(later, MASKED, scores)
            newbest = jnp.maximum(best, jnp.max(scores, axis=1, keepdims=True))
            factor = jnp.exp2(best - newbest)
            weights = jnp.exp2(scores - newbest)
            total = total * factor + jnp.sum(weights, axis=1, keepdims=True)
            summed = summed * factor + jnp.dot(
                weights.astype(jnp.bfloat16), values[at, :], preferred_element_type=jnp.float32
            )
            return newbest, total, summed

        start = (
            jnp.full((count, 1), MASKED, jnp.float32),
            jnp.zeros((count, 1), jnp.float32),
            jnp.zeros((count, HEAD), jnp.float32),
        )
        carry = fold(home, start, True)
        carry = lax.fori_loop(0, home, lambda other, c: fold(other, c, False), carry)
        _, total, summed = carry
        out_ref[home] = (summed / total).astype(jnp.bfloat16)
        return 0

    lax.fori_loop(0, seq_count, one_home, 0)


def attend(part, pieces, chunks, group, rows):
    seq_count = pieces[0].shape[0]
    count = rows // group
    vmem = pl.BlockSpec(memory_space=pltpu.VMEM)
    pairs = seq_count * (seq_count + 1) // 2
    return pl.pallas_call(
        partial(attend_kernel, chunks, group, rows),
        in_specs=[pl.BlockSpec(memory_space=pltpu.SMEM)] + [vmem] * len(pieces),
        out_specs=vmem,
        out_shape=jax.ShapeDtypeStruct((seq_count, count, HEAD), jnp.bfloat16),
        scratch_shapes=[
            pltpu.VMEM((seq_count * rows, 2 * HEAD), jnp.bfloat16),
            pltpu.VMEM((seq_count * rows, HEAD), jnp.bfloat16),
        ],
        compiler_params=pltpu.CompilerParams(vmem_limit_bytes=LIMIT),
        cost_estimate=pl.CostEstimate(
            flops=6 * pairs * count * rows * HEAD,
            bytes_accessed=8 * seq_count * rows * HEAD,
            transcendentals=pairs * count * rows,
        ),
    )(part, *pieces)


def output_kernel(group, count, cuts, blocks, halves, me_ref, at_ref, active_ref, hidden_ref, *refs):
    weights = refs[: cuts * blocks]
    pieces = refs[cuts * blocks : -7]
    out_ref, rows_in, held, own, piece_in, weight_in, own_in = refs[-7:]
    heads = pieces[0].shape[0] // group
    found = sources(me_ref[0], count)
    own_copy = pltpu.make_async_copy(hidden_ref, own, own_in)
    depth = weights[0].shape[0]
    weight_copies = [
        pltpu.make_async_copy(
            weight,
            held.at[number // blocks, number % blocks * depth : (number % blocks + 1) * depth, :],
            weight_in.at[number],
        )
        for number, weight in enumerate(weights)
    ]

    def copies_of(number):
        half, (source, there) = number // len(found), found[number % len(found)]

        def each(act):
            for head in range(heads):
                at = pl.multiple_of(at_ref[(source * halves + half) * heads + head] * HEAD, HEAD)
                for part in range(group):
                    act(
                        pltpu.make_async_copy(
                            pieces[number].at[head * group + part],
                            rows_in.at[:, part, :, pl.ds(at, HEAD)],
                            piece_in.at[half, source, head, part],
                        )
                    )

        return there, each

    for number in range(len(pieces)):
        there, each = copies_of(number)
        when(there, lambda: each(lambda copy: copy.start()))
    for copy in weight_copies[:blocks] + [own_copy] + weight_copies[blocks:]:
        copy.start()
    for number in range(len(pieces)):
        there, each = copies_of(number)
        when(there, lambda: each(lambda copy: copy.wait()))

    rows, width = own.shape[0], held.shape[2]
    x = rows_in[...].reshape(rows, -1)
    for cut in range(cuts):
        for copy in weight_copies[cut * blocks : (cut + 1) * blocks]:
            copy.wait()
        columns = pl.ds(pl.multiple_of(me_ref[1 + cut] * width, width), width)
        shares = jnp.dot(x, held[cut], preferred_element_type=jnp.float32)
        if cut == 0:
            own_copy.wait()
        hidden = own[:, columns]
        renewed = (hidden.astype(jnp.float32) + shares).astype(jnp.bfloat16)
        out_ref[:, columns] = jnp.where(active_ref[...] > 0, renewed, hidden)


def output(scalars, at, pieces, weights, hidden, active, chunks, group, halves):
    rows, columns = hidden.shape
    width = weights[0].shape[1]
    cuts = columns // width
    blocks = len(weights) // cuts
    depth = weights[0].shape[0] * blocks
    count = (len(pieces) // halves + 1) // 2
    part_rows = rows // chunks // group
    pieces = [piece.reshape(-1, chunks, part_rows, HEAD) for piece in pieces]
    smem = pl.BlockSpec(memory_space=pltpu.SMEM)
    vmem = pl.BlockSpec(memory_space=pltpu.VMEM)
    return pl.pallas_call(
        partial(output_kernel, group, count, cuts, blocks, halves),
        in_specs=[smem, smem, vmem]
        + [pl.BlockSpec(memory_space=pl.ANY)] * (1 + len(weights) + len(pieces)),
        out_specs=vmem,
        out_shape=jax.ShapeDtypeStruct((rows, columns), jnp.bfloat16),
        scratch_shapes=[
            pltpu.VMEM((chunks, group, part_rows, depth), jnp.bfloat16),
            pltpu.VMEM((cuts, depth, width), jnp.bfloat16),
            pltpu.VMEM((rows, columns), jnp.bfloat16),
            pltpu.SemaphoreType.DMA((halves, count, pieces[0].shape[0] // group, group)),
            pltpu.SemaphoreType.DMA((cuts * blocks,)),
            pltpu.SemaphoreType.DMA,
        ],
        compiler_params=pltpu.CompilerParams(vmem_limit_bytes=LIMIT),
        cost_estimate=pl.CostEstimate(
            flops=2 * rows * depth * columns,
            bytes_accessed=2 * (rows * depth + depth * columns + 2 * rows * columns),
            transcendentals=0,
        ),
    )(scalars, at, active, hidden, *weights, *pieces)


def share_kernel(place_ref, w_ref, *shares):
    for step, share in enumerate(shares):

        @pl.when(pl.program_id(0) == step)
        def _():
            share[...] = w_ref[...]


def weight_shares(w_out, seq_count, tensor_count, columns):
    depth = w_out.shape[0]
    cuts = seq_count // (depth // HEAD)
    width = columns // cuts
    if width % HEAD:
        return None
    cut = lax.axis_index("seq").astype(jnp.int32) % cuts
    place = jnp.stack([lax.axis_index("tensor").astype(jnp.int32), cut])
    return list(
        pl.pallas_call(
            share_kernel,
            grid_spec=pltpu.PrefetchScalarGridSpec(
                num_scalar_prefetch=1,
                grid=(tensor_count,),
                in_specs=[
                    pl.BlockSpec(
                        (depth, width),
                        lambda j, place: (0, lax.rem(place[0] + j, tensor_count) * cuts + place[1]),
                    )
                ],
                out_specs=[pl.BlockSpec((depth, width), lambda j, place: (0, 0))] * tensor_count,
            ),
            out_shape=[jax.ShapeDtypeStruct((depth, width), w_out.dtype)] * tensor_count,
            compiler_params=pltpu.CompilerParams(vmem_limit_bytes=LIMIT),
        )(place, w_out)
    )


def send_share(shares, step):
    if shares is None:
        return None
    count = len(shares)
    return lax.ppermute(shares[step], "tensor", [(d, (d + step) % count) for d in range(count)])


def output_order(w_out, seq_count, tensor_count, whole):
    heads = w_out.shape[0] // HEAD
    cuts = seq_count // heads
    row = jnp.arange(tensor_count * heads, dtype=jnp.int32)
    if whole:
        return [jnp.int32(0)], row
    seq_me = lax.axis_index("seq").astype(jnp.int32)
    me = lax.axis_index("tensor").astype(jnp.int32)
    which = [(seq_me % cuts + step) % cuts for step in range(cuts)]
    return which, (me - row // heads) % tensor_count * heads + row % heads


def shards(hidden, depth, norm_gain, w_query, w_key, w_value, w_out):
    rows, columns = hidden.shape
    seq_count = lax.axis_size("seq")
    tensor_count = lax.axis_size("tensor")
    heads = w_query.shape[1] // HEAD
    group = seq_count // heads
    chunks = 2
    chunk_rows = rows // chunks
    part = (lax.axis_index("seq") % group).astype(jnp.int32).reshape(1)
    me = lax.axis_index("tensor").astype(jnp.int32)
    gain = norm_gain.reshape(tensor_count, columns)
    active = (depth >= 2).astype(jnp.int32).reshape(rows, 1)
    shares = weight_shares(w_out, seq_count, tensor_count, columns)

    def work(found, chunk):
        here = active[chunk * chunk_rows : (chunk + 1) * chunk_rows]
        return project(
            me.reshape(1), found, here, gain, w_query, w_key, w_value, seq_count, group
        )

    def to_heads(sent):
        return lax.all_to_all(sent, "seq", split_axis=0, concat_axis=0)

    def to_parts(got):
        rings = [
            [(d, d - d % group + (d - step) % group) for d in range(seq_count)]
            for step in range(1, group)
        ]
        return [got] + [lax.ppermute(got, "seq", ring) for ring in rings]

    def cut_weight(step, last):
        nonlocal shares
        if step == 1:
            last[1], shares = lax.optimization_barrier((last[1], shares))
        return last

    first, second = line_gather(
        [hidden[:chunk_rows], hidden[chunk_rows:]], tensor_count, cut_weight
    )
    early, second = lax.optimization_barrier((work(first, 0), second))
    sent, early, shares = lax.optimization_barrier((work(second, 1), to_heads(early), shares))
    late, far = lax.optimization_barrier((to_heads(sent), send_share(shares, 2)))
    pieces = to_parts(early) + to_parts(late)
    out, near = lax.optimization_barrier(
        (attend(part, pieces, chunks, group, rows), send_share(shares, 1))
    )
    home = lax.all_to_all(out, "seq", split_axis=0, concat_axis=0)
    if shares is None:
        weights = [lax.all_to_all(w_out, "tensor", split_axis=1, concat_axis=0, tiled=True)]
    else:
        _, rest = lax.optimization_barrier((near, shares))
        others = [send_share(rest, step) for step in range(3, tensor_count)]
        home, others = lax.optimization_barrier((home, others))
        weights = [shares[0], near, far, *others]
        for step in range(1, group):
            ring = [(d, d - d % group + (d - step) % group) for d in range(seq_count)]
            weights += [lax.ppermute(weight, "seq", ring) for weight in weights[:tensor_count]]
    found = line_gather(
        [home[: seq_count // 2], home[seq_count // 2 :]], tensor_count, lambda step, last: last
    )
    cut_of, at = output_order(w_out, seq_count, tensor_count, shares is None)
    scalars = jnp.stack([me, *cut_of])
    return output(scalars, at, sum(found, []), weights, hidden, active, chunks, group, 2)


def solution(mesh):
    return jax.shard_map(
        shards,
        mesh=mesh,
        in_specs=(
            P("seq", "tensor"),
            P("seq"),
            P(),
            P(None, "tensor"),
            P(None, "tensor"),
            P(None, "tensor"),
            P("tensor", None),
        ),
        out_specs=P("seq", "tensor"),
        check_vma=False,
    )
```

```python
import math
from functools import partial

import jax
import jax.numpy as jnp
from jax import lax
from jax.experimental import pallas as pl
from jax.experimental.pallas import tpu as pltpu
from jax.sharding import PartitionSpec as P

HEAD = 128
MASKED = -1e30
ASIDE = 2.0**100
LIMIT = 63 * 2**20


def sources(me, count):
    found = [(me, None)]
    for step in range(count - 1):
        found.append((me - 1 - step, me - 1 - step >= 0))
        found.append((me + 1 + step, me + 1 + step < count))
    return found


def when(there, act):
    if there is None:
        act()
    else:
        pl.when(there)(act)


def line_gather(chunks, count, join):
    right = [(d, d + 1) for d in range(count - 1)]
    left = [(d + 1, d) for d in range(count - 1)]
    found = [[chunk] for chunk in chunks]
    last = [(chunk, chunk) for chunk in chunks]
    for step in range(count - 1):
        last = join(step, last)
        for at in range(len(chunks)):
            from_left = lax.ppermute(last[at][0], "tensor", right[step:])
            from_right = lax.ppermute(last[at][1], "tensor", left[: count - 1 - step])
            last[at] = (from_left, from_right)
            found[at] += [from_left, from_right]
    return found


def project_kernel(group, count, me_ref, gain_ref, active_ref, *refs):
    matrices = refs[:3]
    pieces = refs[3:-5]
    out_ref, normed, held, piece_in, weight_in = refs[-5:]
    found = sources(me_ref[0], count)
    chunk_rows, width = pieces[0].shape
    chunks = len(pieces) // len(found)
    rows = chunks * chunk_rows

    def copy_of(number):
        chunk, (source, there) = number // len(found), found[number % len(found)]
        to = normed.at[source, chunk * chunk_rows : (chunk + 1) * chunk_rows, :]
        return there, lambda: pltpu.make_async_copy(
            pieces[number], to, piece_in.at[chunk, source]
        )

    for number in range(len(pieces)):
        there, copy = copy_of(number)
        when(there, lambda: copy().start())
    copies = [
        [
            pltpu.make_async_copy(
                matrix.at[step * width : (step + 1) * width, :],
                held.at[step, which],
                weight_in.at[step, which],
            )
            for which, matrix in enumerate(matrices)
        ]
        for step in range(count)
    ]
    for step in range(count):
        for copy in copies[step]:
            copy.start()
    for number in range(len(pieces)):
        there, copy = copy_of(number)
        when(there, lambda: copy().wait())

    square = jnp.zeros((rows, 1), jnp.float32)
    for source in range(count):
        values = normed[source].astype(jnp.float32)
        square = square + jnp.sum(values * values, axis=1, keepdims=True)
    row_scale = lax.rsqrt(square / (count * width) + 1e-05)
    for source in range(count):
        values = normed[source].astype(jnp.float32) * row_scale * gain_ref[source : source + 1, :]
        normed[source] = values.astype(jnp.bfloat16)
    part_rows = chunk_rows // group
    totals = [None] * 3
    for step in range(count):
        for which in range(3):
            copies[step][which].wait()
            product = jnp.dot(normed[step], held[step, which], preferred_element_type=jnp.float32)
            totals[which] = product if step == 0 else totals[which] + product
    for which, total in enumerate(totals):
        if which == 0:
            total = jnp.where(active_ref[...] > 0, total, ASIDE)
        total = total.astype(jnp.bfloat16)
        for head in range(total.shape[1] // HEAD):
            for part in range(group):
                for chunk in range(chunks):
                    first = chunk * chunk_rows + part * part_rows
                    out_ref[
                        head * group + part,
                        chunk * part_rows : (chunk + 1) * part_rows,
                        which * HEAD : (which + 1) * HEAD,
                    ] = total[first : first + part_rows, head * HEAD : (head + 1) * HEAD]


def project(me, pieces, active, gain, wq, wk, wv, seq_count, group):
    columns = pieces[0].shape[1]
    rows = active.shape[0]
    features, width = wq.shape
    count = features // columns
    vmem = pl.BlockSpec(memory_space=pltpu.VMEM)
    return pl.pallas_call(
        partial(project_kernel, group, count),
        in_specs=[pl.BlockSpec(memory_space=pltpu.SMEM), vmem, vmem]
        + [pl.BlockSpec(memory_space=pl.ANY)] * (3 + len(pieces)),
        out_specs=vmem,
        out_shape=jax.ShapeDtypeStruct((seq_count, rows // group, 3 * HEAD), jnp.bfloat16),
        scratch_shapes=[
            pltpu.VMEM((count, rows, columns), jnp.bfloat16),
            pltpu.VMEM((count, 3, columns, width), jnp.bfloat16),
            pltpu.SemaphoreType.DMA((rows // pieces[0].shape[0], count)),
            pltpu.SemaphoreType.DMA((count, 3)),
        ],
        compiler_params=pltpu.CompilerParams(vmem_limit_bytes=LIMIT),
        cost_estimate=pl.CostEstimate(
            flops=6 * rows * features * width,
            bytes_accessed=6 * features * width + 2 * rows * (features + 3 * width),
            transcendentals=0,
        ),
    )(me, gain, active, wq, wk, wv, *pieces)


def attend_kernel(chunks, group, rows, part_ref, *refs):
    pieces = refs[:-3]
    out_ref, keys, values = refs[-3:]
    seq_count = pieces[0].shape[0]
    chunk_rows = rows // chunks
    part_rows = chunk_rows // group
    part = part_ref[0]

    def place(home, _):
        chunk = 0
        for number in range(0, len(pieces), group):
            inside = pieces[number].shape[1] // part_rows
            for step in range(group):
                owner = lax.rem(part + step, group)
                piece = pieces[number + step]
                for at_chunk in range(inside):
                    at = home * rows + (chunk + at_chunk) * chunk_rows + owner * part_rows
                    to = pl.ds(pl.multiple_of(at, part_rows), part_rows)
                    of = slice(at_chunk * part_rows, (at_chunk + 1) * part_rows)
                    aside = piece[home, of, :HEAD].astype(jnp.float32) >= ASIDE
                    keys[to, :HEAD] = piece[home, of, HEAD : 2 * HEAD]
                    keys[to, HEAD:] = jnp.where(aside, MASKED, 0.0).astype(jnp.bfloat16)
                    values[to, :] = piece[home, of, 2 * HEAD :]
            chunk += inside
        return 0

    lax.fori_loop(0, seq_count, place, 0)
    scale = math.log2(math.e) / math.sqrt(HEAD)
    count = chunks * part_rows
    first_lane = lax.broadcasted_iota(jnp.int32, (count, HEAD), 1) == 0
    mask_lane = jnp.where(first_lane, 1.0, 0.0).astype(jnp.bfloat16)
    order = lax.broadcasted_iota(jnp.int32, (count, rows), 0)
    own = order // part_rows * chunk_rows + part * part_rows + order % part_rows
    later = lax.broadcasted_iota(jnp.int32, (count, rows), 1) > own

    def queries_of(home):
        queries = jnp.concatenate(
            [pieces[number][home, :, :HEAD] for number in range(0, len(pieces), group)], axis=0
        )
        return jnp.concatenate([queries, mask_lane], axis=1)

    def scores_of(queries, at):
        return scale * lax.dot_general(
            queries,
            keys[at, :],
            (((1,), (1,)), ((), ())),
            preferred_element_type=jnp.float32,
        )

    if seq_count <= 8:
        for home in range(seq_count):
            queries = queries_of(home)
            blocks = []
            for other in range(home + 1):
                scores = scores_of(queries, slice(other * rows, (other + 1) * rows))
                if other == home:
                    scores = jnp.where(later, MASKED, scores)
                blocks.append(scores)
            scores = jnp.concatenate(blocks, axis=1)
            best = jnp.max(scores, axis=1, keepdims=True)
            weights = jnp.exp2(scores - best)
            total = jnp.sum(weights, axis=1, keepdims=True)
            summed = jnp.dot(
                weights.astype(jnp.bfloat16),
                values[: (home + 1) * rows, :],
                preferred_element_type=jnp.float32,
            )
            out_ref[home] = (summed / total).astype(jnp.bfloat16)
        return

    def one_home(home, _):
        queries = queries_of(home)

        def fold(other, carry, diagonal):
            best, total, summed = carry
            at = pl.ds(pl.multiple_of(other * rows, rows), rows)
            scores = scores_of(queries, at)
            if diagonal:
                scores = jnp.where(later, MASKED, scores)
            newbest = jnp.maximum(best, jnp.max(scores, axis=1, keepdims=True))
            factor = jnp.exp2(best - newbest)
            weights = jnp.exp2(scores - newbest)
            total = total * factor + jnp.sum(weights, axis=1, keepdims=True)
            summed = summed * factor + jnp.dot(
                weights.astype(jnp.bfloat16), values[at, :], preferred_element_type=jnp.float32
            )
            return newbest, total, summed

        start = (
            jnp.full((count, 1), MASKED, jnp.float32),
            jnp.zeros((count, 1), jnp.float32),
            jnp.zeros((count, HEAD), jnp.float32),
        )
        carry = fold(home, start, True)
        carry = lax.fori_loop(0, home, lambda other, c: fold(other, c, False), carry)
        _, total, summed = carry
        out_ref[home] = (summed / total).astype(jnp.bfloat16)
        return 0

    lax.fori_loop(0, seq_count, one_home, 0)


def attend(part, pieces, chunks, group, rows):
    seq_count = pieces[0].shape[0]
    count = rows // group
    vmem = pl.BlockSpec(memory_space=pltpu.VMEM)
    pairs = seq_count * (seq_count + 1) // 2
    return pl.pallas_call(
        partial(attend_kernel, chunks, group, rows),
        in_specs=[pl.BlockSpec(memory_space=pltpu.SMEM)] + [vmem] * len(pieces),
        out_specs=vmem,
        out_shape=jax.ShapeDtypeStruct((seq_count, count, HEAD), jnp.bfloat16),
        scratch_shapes=[
            pltpu.VMEM((seq_count * rows, 2 * HEAD), jnp.bfloat16),
            pltpu.VMEM((seq_count * rows, HEAD), jnp.bfloat16),
        ],
        compiler_params=pltpu.CompilerParams(vmem_limit_bytes=LIMIT),
        cost_estimate=pl.CostEstimate(
            flops=6 * pairs * count * rows * HEAD,
            bytes_accessed=8 * seq_count * rows * HEAD,
            transcendentals=pairs * count * rows,
        ),
    )(part, *pieces)


def output_kernel(group, count, cuts, blocks, halves, me_ref, at_ref, active_ref, hidden_ref, *refs):
    weights = refs[: cuts * blocks]
    pieces = refs[cuts * blocks : -7]
    out_ref, rows_in, held, own, piece_in, weight_in, own_in = refs[-7:]
    heads = pieces[0].shape[0] // group
    found = sources(me_ref[0], count)
    own_copy = pltpu.make_async_copy(hidden_ref, own, own_in)
    depth = weights[0].shape[0]
    weight_copies = [
        pltpu.make_async_copy(
            weight,
            held.at[number // blocks, number % blocks * depth : (number % blocks + 1) * depth, :],
            weight_in.at[number],
        )
        for number, weight in enumerate(weights)
    ]

    def copies_of(number):
        half, (source, there) = number // len(found), found[number % len(found)]

        def each(act):
            for head in range(heads):
                at = pl.multiple_of(at_ref[(source * halves + half) * heads + head] * HEAD, HEAD)
                for part in range(group):
                    act(
                        pltpu.make_async_copy(
                            pieces[number].at[head * group + part],
                            rows_in.at[:, part, :, pl.ds(at, HEAD)],
                            piece_in.at[half, source, head, part],
                        )
                    )

        return there, each

    for number in range(len(pieces)):
        there, each = copies_of(number)
        when(there, lambda: each(lambda copy: copy.start()))
    for copy in weight_copies[:blocks] + [own_copy] + weight_copies[blocks:]:
        copy.start()
    for number in range(len(pieces)):
        there, each = copies_of(number)
        when(there, lambda: each(lambda copy: copy.wait()))

    rows, width = own.shape[0], held.shape[2]
    x = rows_in[...].reshape(rows, -1)
    for cut in range(cuts):
        for copy in weight_copies[cut * blocks : (cut + 1) * blocks]:
            copy.wait()
        columns = pl.ds(pl.multiple_of(me_ref[1 + cut] * width, width), width)
        shares = jnp.dot(x, held[cut], preferred_element_type=jnp.float32)
        if cut == 0:
            own_copy.wait()
        hidden = own[:, columns]
        renewed = (hidden.astype(jnp.float32) + shares).astype(jnp.bfloat16)
        out_ref[:, columns] = jnp.where(active_ref[...] > 0, renewed, hidden)


def output(scalars, at, pieces, weights, hidden, active, chunks, group, halves):
    rows, columns = hidden.shape
    width = weights[0].shape[1]
    cuts = columns // width
    blocks = len(weights) // cuts
    depth = weights[0].shape[0] * blocks
    count = (len(pieces) // halves + 1) // 2
    part_rows = rows // chunks // group
    pieces = [piece.reshape(-1, chunks, part_rows, HEAD) for piece in pieces]
    smem = pl.BlockSpec(memory_space=pltpu.SMEM)
    vmem = pl.BlockSpec(memory_space=pltpu.VMEM)
    return pl.pallas_call(
        partial(output_kernel, group, count, cuts, blocks, halves),
        in_specs=[smem, smem, vmem]
        + [pl.BlockSpec(memory_space=pl.ANY)] * (1 + len(weights) + len(pieces)),
        out_specs=vmem,
        out_shape=jax.ShapeDtypeStruct((rows, columns), jnp.bfloat16),
        scratch_shapes=[
            pltpu.VMEM((chunks, group, part_rows, depth), jnp.bfloat16),
            pltpu.VMEM((cuts, depth, width), jnp.bfloat16),
            pltpu.VMEM((rows, columns), jnp.bfloat16),
            pltpu.SemaphoreType.DMA((halves, count, pieces[0].shape[0] // group, group)),
            pltpu.SemaphoreType.DMA((cuts * blocks,)),
            pltpu.SemaphoreType.DMA,
        ],
        compiler_params=pltpu.CompilerParams(vmem_limit_bytes=LIMIT),
        cost_estimate=pl.CostEstimate(
            flops=2 * rows * depth * columns,
            bytes_accessed=2 * (rows * depth + depth * columns + 2 * rows * columns),
            transcendentals=0,
        ),
    )(scalars, at, active, hidden, *weights, *pieces)


def share_kernel(place_ref, w_ref, *shares):
    for step, share in enumerate(shares):

        @pl.when(pl.program_id(0) == step)
        def _():
            share[...] = w_ref[...]


def weight_shares(w_out, seq_count, tensor_count, columns):
    depth = w_out.shape[0]
    cuts = seq_count // (depth // HEAD)
    width = columns // cuts
    if width % HEAD:
        return None
    cut = lax.axis_index("seq").astype(jnp.int32) % cuts
    place = jnp.stack([lax.axis_index("tensor").astype(jnp.int32), cut])
    return list(
        pl.pallas_call(
            share_kernel,
            grid_spec=pltpu.PrefetchScalarGridSpec(
                num_scalar_prefetch=1,
                grid=(tensor_count,),
                in_specs=[
                    pl.BlockSpec(
                        (depth, width),
                        lambda j, place: (0, lax.rem(place[0] + j, tensor_count) * cuts + place[1]),
                    )
                ],
                out_specs=[pl.BlockSpec((depth, width), lambda j, place: (0, 0))] * tensor_count,
            ),
            out_shape=[jax.ShapeDtypeStruct((depth, width), w_out.dtype)] * tensor_count,
            compiler_params=pltpu.CompilerParams(vmem_limit_bytes=LIMIT),
        )(place, w_out)
    )


def send_share(shares, step, rows=slice(None)):
    if shares is None:
        return None
    count = len(shares)
    ring = [(d, (d + step) % count) for d in range(count)]
    return lax.ppermute(shares[step][rows], "tensor", ring)


def output_order(w_out, seq_count, tensor_count, whole):
    heads = w_out.shape[0] // HEAD
    cuts = seq_count // heads
    row = jnp.arange(tensor_count * heads, dtype=jnp.int32)
    if whole:
        return [jnp.int32(0)], row
    seq_me = lax.axis_index("seq").astype(jnp.int32)
    me = lax.axis_index("tensor").astype(jnp.int32)
    which = [(seq_me % cuts + step) % cuts for step in range(cuts)]
    return which, (me - row // heads) % tensor_count * heads + row % heads


def shards(hidden, depth, norm_gain, w_query, w_key, w_value, w_out):
    rows, columns = hidden.shape
    seq_count = lax.axis_size("seq")
    tensor_count = lax.axis_size("tensor")
    heads = w_query.shape[1] // HEAD
    group = seq_count // heads
    chunks = 2
    chunk_rows = rows // chunks
    part = (lax.axis_index("seq") % group).astype(jnp.int32).reshape(1)
    me = lax.axis_index("tensor").astype(jnp.int32)
    gain = norm_gain.reshape(tensor_count, columns)
    active = (depth >= 2).astype(jnp.int32).reshape(rows, 1)
    shares = weight_shares(w_out, seq_count, tensor_count, columns)

    def work(found, chunk):
        here = active[chunk * chunk_rows : (chunk + 1) * chunk_rows]
        return project(
            me.reshape(1), found, here, gain, w_query, w_key, w_value, seq_count, group
        )

    def to_heads(sent):
        return lax.all_to_all(sent, "seq", split_axis=0, concat_axis=0)

    def to_parts(got):
        rings = [
            [(d, d - d % group + (d - step) % group) for d in range(seq_count)]
            for step in range(1, group)
        ]
        return [got] + [lax.ppermute(got, "seq", ring) for ring in rings]

    def cut_weight(step, last):
        nonlocal shares
        if step == 1:
            last[1], shares = lax.optimization_barrier((last[1], shares))
        return last

    first, second = line_gather(
        [hidden[:chunk_rows], hidden[chunk_rows:]], tensor_count, cut_weight
    )
    early, second, shares = lax.optimization_barrier((work(first, 0), second, shares))
    middle = w_out.shape[0] // 2
    sent, early, far, shares = lax.optimization_barrier(
        (work(second, 1), to_heads(early), send_share(shares, 2, slice(0, middle)), shares)
    )
    late, rest = lax.optimization_barrier(
        (to_heads(sent), send_share(shares, 2, slice(middle, None)))
    )
    pieces = to_parts(early) + to_parts(late)
    out, near = lax.optimization_barrier(
        (attend(part, pieces, chunks, group, rows), send_share(shares, 1))
    )
    home = lax.all_to_all(out, "seq", split_axis=0, concat_axis=0)
    if shares is None:
        weights = [lax.all_to_all(w_out, "tensor", split_axis=1, concat_axis=0, tiled=True)]
    else:
        _, last = lax.optimization_barrier((near, shares))
        others = [send_share(last, step) for step in range(3, tensor_count)]
        home, others = lax.optimization_barrier((home, others))
        weights = [shares[0], near, jnp.concatenate([far, rest], axis=0), *others]
        for step in range(1, group):
            ring = [(d, d - d % group + (d - step) % group) for d in range(seq_count)]
            weights += [lax.ppermute(weight, "seq", ring) for weight in weights[:tensor_count]]
    found = line_gather(
        [home[: seq_count // 2], home[seq_count // 2 :]], tensor_count, lambda step, last: last
    )
    cut_of, at = output_order(w_out, seq_count, tensor_count, shares is None)
    scalars = jnp.stack([me, *cut_of])
    return output(scalars, at, sum(found, []), weights, hidden, active, chunks, group, 2)


def solution(mesh):
    return jax.shard_map(
        shards,
        mesh=mesh,
        in_specs=(
            P("seq", "tensor"),
            P("seq"),
            P(),
            P(None, "tensor"),
            P(None, "tensor"),
            P(None, "tensor"),
            P("tensor", None),
        ),
        out_specs=P("seq", "tensor"),
        check_vma=False,
    )
```

```python
import math
from functools import partial

import jax
import jax.numpy as jnp
from jax import lax
from jax.experimental import pallas as pl
from jax.experimental.pallas import tpu as pltpu
from jax.sharding import PartitionSpec as P

HEAD = 128
MASKED = -1e30
ASIDE = 2.0**100
LIMIT = 63 * 2**20


def sources(me, count):
    found = [(me, None)]
    for step in range(count - 1):
        found.append((me - 1 - step, me - 1 - step >= 0))
        found.append((me + 1 + step, me + 1 + step < count))
    return found


def when(there, act):
    if there is None:
        act()
    else:
        pl.when(there)(act)


def line_gather(chunks, count, join):
    right = [(d, d + 1) for d in range(count - 1)]
    left = [(d + 1, d) for d in range(count - 1)]
    found = [[chunk] for chunk in chunks]
    last = [(chunk, chunk) for chunk in chunks]
    for step in range(count - 1):
        last = join(step, last)
        for at in range(len(chunks)):
            from_left = lax.ppermute(last[at][0], "tensor", right[step:])
            from_right = lax.ppermute(last[at][1], "tensor", left[: count - 1 - step])
            last[at] = (from_left, from_right)
            found[at] += [from_left, from_right]
    return found


def project_kernel(group, count, me_ref, gain_ref, active_ref, *refs):
    matrices = refs[:3]
    pieces = refs[3:-5]
    out_ref, normed, held, piece_in, weight_in = refs[-5:]
    found = sources(me_ref[0], count)
    chunk_rows, width = pieces[0].shape
    chunks = len(pieces) // len(found)
    rows = chunks * chunk_rows

    def copy_of(number):
        chunk, (source, there) = number // len(found), found[number % len(found)]
        to = normed.at[source, chunk * chunk_rows : (chunk + 1) * chunk_rows, :]
        return there, lambda: pltpu.make_async_copy(
            pieces[number], to, piece_in.at[chunk, source]
        )

    for number in range(len(pieces)):
        there, copy = copy_of(number)
        when(there, lambda: copy().start())
    copies = [
        [
            pltpu.make_async_copy(
                matrix.at[step * width : (step + 1) * width, :],
                held.at[step, which],
                weight_in.at[step, which],
            )
            for which, matrix in enumerate(matrices)
        ]
        for step in range(count)
    ]
    for step in range(count):
        for copy in copies[step]:
            copy.start()
    for number in range(len(pieces)):
        there, copy = copy_of(number)
        when(there, lambda: copy().wait())

    square = jnp.zeros((rows, 1), jnp.float32)
    for source in range(count):
        values = normed[source].astype(jnp.float32)
        square = square + jnp.sum(values * values, axis=1, keepdims=True)
    row_scale = lax.rsqrt(square / (count * width) + 1e-05)
    for source in range(count):
        values = normed[source].astype(jnp.float32) * row_scale * gain_ref[source : source + 1, :]
        normed[source] = values.astype(jnp.bfloat16)
    part_rows = chunk_rows // group
    totals = [None] * 3
    for step in range(count):
        for which in range(3):
            copies[step][which].wait()
            product = jnp.dot(normed[step], held[step, which], preferred_element_type=jnp.float32)
            totals[which] = product if step == 0 else totals[which] + product
    for which, total in enumerate(totals):
        if which == 0:
            total = jnp.where(active_ref[...] > 0, total, ASIDE)
        total = total.astype(jnp.bfloat16)
        for head in range(total.shape[1] // HEAD):
            for part in range(group):
                for chunk in range(chunks):
                    first = chunk * chunk_rows + part * part_rows
                    out_ref[
                        head * group + part,
                        chunk * part_rows : (chunk + 1) * part_rows,
                        which * HEAD : (which + 1) * HEAD,
                    ] = total[first : first + part_rows, head * HEAD : (head + 1) * HEAD]


def project(me, pieces, active, gain, wq, wk, wv, seq_count, group):
    columns = pieces[0].shape[1]
    rows = active.shape[0]
    features, width = wq.shape
    count = features // columns
    vmem = pl.BlockSpec(memory_space=pltpu.VMEM)
    return pl.pallas_call(
        partial(project_kernel, group, count),
        in_specs=[pl.BlockSpec(memory_space=pltpu.SMEM), vmem, vmem]
        + [pl.BlockSpec(memory_space=pl.ANY)] * (3 + len(pieces)),
        out_specs=vmem,
        out_shape=jax.ShapeDtypeStruct((seq_count, rows // group, 3 * HEAD), jnp.bfloat16),
        scratch_shapes=[
            pltpu.VMEM((count, rows, columns), jnp.bfloat16),
            pltpu.VMEM((count, 3, columns, width), jnp.bfloat16),
            pltpu.SemaphoreType.DMA((rows // pieces[0].shape[0], count)),
            pltpu.SemaphoreType.DMA((count, 3)),
        ],
        compiler_params=pltpu.CompilerParams(vmem_limit_bytes=LIMIT),
        cost_estimate=pl.CostEstimate(
            flops=6 * rows * features * width,
            bytes_accessed=6 * features * width + 2 * rows * (features + 3 * width),
            transcendentals=0,
        ),
    )(me, gain, active, wq, wk, wv, *pieces)


def attend_kernel(chunks, group, rows, part_ref, *refs):
    pieces = refs[:-3]
    out_ref, keys, values = refs[-3:]
    seq_count = pieces[0].shape[0]
    chunk_rows = rows // chunks
    part_rows = chunk_rows // group
    part = part_ref[0]

    def place(home, _):
        chunk = 0
        for number in range(0, len(pieces), group):
            inside = pieces[number].shape[1] // part_rows
            for step in range(group):
                owner = lax.rem(part + step, group)
                piece = pieces[number + step]
                for at_chunk in range(inside):
                    at = home * rows + (chunk + at_chunk) * chunk_rows + owner * part_rows
                    to = pl.ds(pl.multiple_of(at, part_rows), part_rows)
                    of = slice(at_chunk * part_rows, (at_chunk + 1) * part_rows)
                    aside = piece[home, of, :HEAD].astype(jnp.float32) >= ASIDE
                    keys[to, :HEAD] = piece[home, of, HEAD : 2 * HEAD]
                    keys[to, HEAD:] = jnp.where(aside, MASKED, 0.0).astype(jnp.bfloat16)
                    values[to, :] = piece[home, of, 2 * HEAD :]
            chunk += inside
        return 0

    lax.fori_loop(0, seq_count, place, 0)
    scale = math.log2(math.e) / math.sqrt(HEAD)
    count = chunks * part_rows
    first_lane = lax.broadcasted_iota(jnp.int32, (count, HEAD), 1) == 0
    mask_lane = jnp.where(first_lane, 1.0, 0.0).astype(jnp.bfloat16)
    order = lax.broadcasted_iota(jnp.int32, (count, rows), 0)
    own = order // part_rows * chunk_rows + part * part_rows + order % part_rows
    later = lax.broadcasted_iota(jnp.int32, (count, rows), 1) > own

    def queries_of(home):
        queries = jnp.concatenate(
            [pieces[number][home, :, :HEAD] for number in range(0, len(pieces), group)], axis=0
        )
        return jnp.concatenate([queries, mask_lane], axis=1)

    def scores_of(queries, at):
        return scale * lax.dot_general(
            queries,
            keys[at, :],
            (((1,), (1,)), ((), ())),
            preferred_element_type=jnp.float32,
        )

    if seq_count <= 8:
        for home in range(seq_count):
            queries = queries_of(home)
            blocks = []
            for other in range(home + 1):
                scores = scores_of(queries, slice(other * rows, (other + 1) * rows))
                if other == home:
                    scores = jnp.where(later, MASKED, scores)
                blocks.append(scores)
            scores = jnp.concatenate(blocks, axis=1)
            best = jnp.max(scores, axis=1, keepdims=True)
            weights = jnp.exp2(scores - best)
            total = jnp.sum(weights, axis=1, keepdims=True)
            summed = jnp.dot(
                weights.astype(jnp.bfloat16),
                values[: (home + 1) * rows, :],
                preferred_element_type=jnp.float32,
            )
            out_ref[home] = (summed / total).astype(jnp.bfloat16)
        return

    def one_home(home, _):
        queries = queries_of(home)

        def fold(other, carry, diagonal):
            best, total, summed = carry
            at = pl.ds(pl.multiple_of(other * rows, rows), rows)
            scores = scores_of(queries, at)
            if diagonal:
                scores = jnp.where(later, MASKED, scores)
            newbest = jnp.maximum(best, jnp.max(scores, axis=1, keepdims=True))
            factor = jnp.exp2(best - newbest)
            weights = jnp.exp2(scores - newbest)
            total = total * factor + jnp.sum(weights, axis=1, keepdims=True)
            summed = summed * factor + jnp.dot(
                weights.astype(jnp.bfloat16), values[at, :], preferred_element_type=jnp.float32
            )
            return newbest, total, summed

        start = (
            jnp.full((count, 1), MASKED, jnp.float32),
            jnp.zeros((count, 1), jnp.float32),
            jnp.zeros((count, HEAD), jnp.float32),
        )
        carry = fold(home, start, True)
        carry = lax.fori_loop(0, home, lambda other, c: fold(other, c, False), carry)
        _, total, summed = carry
        out_ref[home] = (summed / total).astype(jnp.bfloat16)
        return 0

    lax.fori_loop(0, seq_count, one_home, 0)


def attend(part, pieces, chunks, group, rows):
    seq_count = pieces[0].shape[0]
    count = rows // group
    vmem = pl.BlockSpec(memory_space=pltpu.VMEM)
    pairs = seq_count * (seq_count + 1) // 2
    return pl.pallas_call(
        partial(attend_kernel, chunks, group, rows),
        in_specs=[pl.BlockSpec(memory_space=pltpu.SMEM)] + [vmem] * len(pieces),
        out_specs=vmem,
        out_shape=jax.ShapeDtypeStruct((seq_count, count, HEAD), jnp.bfloat16),
        scratch_shapes=[
            pltpu.VMEM((seq_count * rows, 2 * HEAD), jnp.bfloat16),
            pltpu.VMEM((seq_count * rows, HEAD), jnp.bfloat16),
        ],
        compiler_params=pltpu.CompilerParams(vmem_limit_bytes=LIMIT),
        cost_estimate=pl.CostEstimate(
            flops=6 * pairs * count * rows * HEAD,
            bytes_accessed=8 * seq_count * rows * HEAD,
            transcendentals=pairs * count * rows,
        ),
    )(part, *pieces)


def output_kernel(group, count, cuts, blocks, halves, me_ref, at_ref, active_ref, hidden_ref, *refs):
    weights = refs[: cuts * blocks]
    pieces = refs[cuts * blocks : -7]
    out_ref, rows_in, held, own, piece_in, weight_in, own_in = refs[-7:]
    heads = pieces[0].shape[0] // group
    found = sources(me_ref[0], count)
    own_copy = pltpu.make_async_copy(hidden_ref, own, own_in)
    depth = weights[0].shape[0]
    weight_copies = [
        pltpu.make_async_copy(
            weight,
            held.at[number // blocks, number % blocks * depth : (number % blocks + 1) * depth, :],
            weight_in.at[number],
        )
        for number, weight in enumerate(weights)
    ]

    def copies_of(number):
        half, (source, there) = number // len(found), found[number % len(found)]

        def each(act):
            for head in range(heads):
                at = pl.multiple_of(at_ref[(source * halves + half) * heads + head] * HEAD, HEAD)
                for part in range(group):
                    act(
                        pltpu.make_async_copy(
                            pieces[number].at[head * group + part],
                            rows_in.at[:, part, :, pl.ds(at, HEAD)],
                            piece_in.at[half, source, head, part],
                        )
                    )

        return there, each

    for number in range(len(pieces)):
        there, each = copies_of(number)
        when(there, lambda: each(lambda copy: copy.start()))
    for copy in weight_copies[:blocks] + [own_copy] + weight_copies[blocks:]:
        copy.start()
    for number in range(len(pieces)):
        there, each = copies_of(number)
        when(there, lambda: each(lambda copy: copy.wait()))

    rows, width = own.shape[0], held.shape[2]
    x = rows_in[...].reshape(rows, -1)
    for cut in range(cuts):
        for copy in weight_copies[cut * blocks : (cut + 1) * blocks]:
            copy.wait()
        columns = pl.ds(pl.multiple_of(me_ref[1 + cut] * width, width), width)
        shares = jnp.dot(x, held[cut], preferred_element_type=jnp.float32)
        if cut == 0:
            own_copy.wait()
        hidden = own[:, columns]
        renewed = (hidden.astype(jnp.float32) + shares).astype(jnp.bfloat16)
        out_ref[:, columns] = jnp.where(active_ref[...] > 0, renewed, hidden)


def output(scalars, at, pieces, weights, hidden, active, chunks, group, halves):
    rows, columns = hidden.shape
    width = weights[0].shape[1]
    cuts = columns // width
    blocks = len(weights) // cuts
    depth = weights[0].shape[0] * blocks
    count = (len(pieces) // halves + 1) // 2
    part_rows = rows // chunks // group
    pieces = [piece.reshape(-1, chunks, part_rows, HEAD) for piece in pieces]
    smem = pl.BlockSpec(memory_space=pltpu.SMEM)
    vmem = pl.BlockSpec(memory_space=pltpu.VMEM)
    return pl.pallas_call(
        partial(output_kernel, group, count, cuts, blocks, halves),
        in_specs=[smem, smem, vmem]
        + [pl.BlockSpec(memory_space=pl.ANY)] * (1 + len(weights) + len(pieces)),
        out_specs=vmem,
        out_shape=jax.ShapeDtypeStruct((rows, columns), jnp.bfloat16),
        scratch_shapes=[
            pltpu.VMEM((chunks, group, part_rows, depth), jnp.bfloat16),
            pltpu.VMEM((cuts, depth, width), jnp.bfloat16),
            pltpu.VMEM((rows, columns), jnp.bfloat16),
            pltpu.SemaphoreType.DMA((halves, count, pieces[0].shape[0] // group, group)),
            pltpu.SemaphoreType.DMA((cuts * blocks,)),
            pltpu.SemaphoreType.DMA,
        ],
        compiler_params=pltpu.CompilerParams(vmem_limit_bytes=LIMIT),
        cost_estimate=pl.CostEstimate(
            flops=2 * rows * depth * columns,
            bytes_accessed=2 * (rows * depth + depth * columns + 2 * rows * columns),
            transcendentals=0,
        ),
    )(scalars, at, active, hidden, *weights, *pieces)


def share_kernel(place_ref, w_ref, *shares):
    for number, share in enumerate(shares):
        step = number if number < 3 else number - 1
        first = w_ref.shape[0] // 2 if number == 3 else 0

        @pl.when(pl.program_id(0) == step)
        def _():
            share[...] = w_ref[first : first + share.shape[0], :]


def weight_shares(w_out, seq_count, tensor_count, columns):
    depth = w_out.shape[0]
    cuts = seq_count // (depth // HEAD)
    width = columns // cuts
    if width % HEAD:
        return None
    cut = lax.axis_index("seq").astype(jnp.int32) % cuts
    sizes = [depth, depth, depth // 2, depth // 2] + [depth] * (tensor_count - 3)
    place = jnp.stack([lax.axis_index("tensor").astype(jnp.int32), cut])
    return list(
        pl.pallas_call(
            share_kernel,
            grid_spec=pltpu.PrefetchScalarGridSpec(
                num_scalar_prefetch=1,
                grid=(tensor_count,),
                in_specs=[
                    pl.BlockSpec(
                        (depth, width),
                        lambda j, place: (0, lax.rem(place[0] + j, tensor_count) * cuts + place[1]),
                    )
                ],
                out_specs=[pl.BlockSpec((size, width), lambda j, place: (0, 0)) for size in sizes],
            ),
            out_shape=[jax.ShapeDtypeStruct((size, width), w_out.dtype) for size in sizes],
            compiler_params=pltpu.CompilerParams(vmem_limit_bytes=LIMIT),
        )(place, w_out)
    )


def send_share(shares, number):
    if shares is None:
        return None
    step = number if number < 3 else number - 1
    count = len(shares) - 1
    ring = [(d, (d + step) % count) for d in range(count)]
    return lax.ppermute(shares[number], "tensor", ring)


def output_order(w_out, seq_count, tensor_count, whole):
    heads = w_out.shape[0] // HEAD
    cuts = seq_count // heads
    row = jnp.arange(tensor_count * heads, dtype=jnp.int32)
    if whole:
        return [jnp.int32(0)], row
    seq_me = lax.axis_index("seq").astype(jnp.int32)
    me = lax.axis_index("tensor").astype(jnp.int32)
    which = [(seq_me % cuts + step) % cuts for step in range(cuts)]
    return which, (me - row // heads) % tensor_count * heads + row % heads


def shards(hidden, depth, norm_gain, w_query, w_key, w_value, w_out):
    rows, columns = hidden.shape
    seq_count = lax.axis_size("seq")
    tensor_count = lax.axis_size("tensor")
    heads = w_query.shape[1] // HEAD
    group = seq_count // heads
    chunks = 2
    chunk_rows = rows // chunks
    part = (lax.axis_index("seq") % group).astype(jnp.int32).reshape(1)
    me = lax.axis_index("tensor").astype(jnp.int32)
    gain = norm_gain.reshape(tensor_count, columns)
    active = (depth >= 2).astype(jnp.int32).reshape(rows, 1)
    shares = weight_shares(w_out, seq_count, tensor_count, columns)

    def work(found, chunk):
        here = active[chunk * chunk_rows : (chunk + 1) * chunk_rows]
        return project(
            me.reshape(1), found, here, gain, w_query, w_key, w_value, seq_count, group
        )

    def to_heads(sent):
        return lax.all_to_all(sent, "seq", split_axis=0, concat_axis=0)

    def to_parts(got):
        rings = [
            [(d, d - d % group + (d - step) % group) for d in range(seq_count)]
            for step in range(1, group)
        ]
        return [got] + [lax.ppermute(got, "seq", ring) for ring in rings]

    def cut_weight(step, last):
        nonlocal shares
        if step == 1:
            last[1], shares = lax.optimization_barrier((last[1], shares))
        return last

    first, second = line_gather(
        [hidden[:chunk_rows], hidden[chunk_rows:]], tensor_count, cut_weight
    )
    early, second, shares = lax.optimization_barrier((work(first, 0), second, shares))
    sent, early, far, shares = lax.optimization_barrier(
        (work(second, 1), to_heads(early), send_share(shares, 2), shares)
    )
    late, rest = lax.optimization_barrier((to_heads(sent), send_share(shares, 3)))
    pieces = to_parts(early) + to_parts(late)
    out, near = lax.optimization_barrier(
        (attend(part, pieces, chunks, group, rows), send_share(shares, 1))
    )
    home = lax.all_to_all(out, "seq", split_axis=0, concat_axis=0)
    if shares is None:
        weights = [lax.all_to_all(w_out, "tensor", split_axis=1, concat_axis=0, tiled=True)]
    else:
        _, last = lax.optimization_barrier((near, shares))
        others = [send_share(last, number) for number in range(4, tensor_count + 1)]
        home, others = lax.optimization_barrier((home, others))
        weights = [shares[0], near, jnp.concatenate([far, rest], axis=0), *others]
        for step in range(1, group):
            ring = [(d, d - d % group + (d - step) % group) for d in range(seq_count)]
            weights += [lax.ppermute(weight, "seq", ring) for weight in weights[:tensor_count]]
    found = line_gather(
        [home[: seq_count // 2], home[seq_count // 2 :]], tensor_count, lambda step, last: last
    )
    cut_of, at = output_order(w_out, seq_count, tensor_count, shares is None)
    scalars = jnp.stack([me, *cut_of])
    return output(scalars, at, sum(found, []), weights, hidden, active, chunks, group, 2)


def solution(mesh):
    return jax.shard_map(
        shards,
        mesh=mesh,
        in_specs=(
            P("seq", "tensor"),
            P("seq"),
            P(),
            P(None, "tensor"),
            P(None, "tensor"),
            P(None, "tensor"),
            P("tensor", None),
        ),
        out_specs=P("seq", "tensor"),
        check_vma=False,
    )
```

```python
import math
from functools import partial

import jax
import jax.numpy as jnp
from jax import lax
from jax.experimental import pallas as pl
from jax.experimental.pallas import tpu as pltpu
from jax.sharding import PartitionSpec as P

HEAD = 128
MASKED = -1e30
ASIDE = 2.0**100
LIMIT = 63 * 2**20


def sources(me, count):
    found = [(me, None)]
    for step in range(count - 1):
        found.append((me - 1 - step, me - 1 - step >= 0))
        found.append((me + 1 + step, me + 1 + step < count))
    return found


def when(there, act):
    if there is None:
        act()
    else:
        pl.when(there)(act)


def line_gather(chunks, count, join):
    right = [(d, d + 1) for d in range(count - 1)]
    left = [(d + 1, d) for d in range(count - 1)]
    found = [[chunk] for chunk in chunks]
    last = [(chunk, chunk) for chunk in chunks]
    for step in range(count - 1):
        last = join(step, last)
        for at in range(len(chunks)):
            from_left = lax.ppermute(last[at][0], "tensor", right[step:])
            from_right = lax.ppermute(last[at][1], "tensor", left[: count - 1 - step])
            last[at] = (from_left, from_right)
            found[at] += [from_left, from_right]
    return found


def project_kernel(group, count, begin, me_ref, gain_ref, active_ref, *refs):
    matrices = refs[:3]
    pieces = refs[3:-5]
    out_ref, normed, held, piece_in, weight_in = refs[-5:]
    found = sources(me_ref[0], count)
    chunk_rows, width = pieces[0].shape
    chunks = len(pieces) // len(found)
    rows = chunks * chunk_rows

    def copy_of(number):
        chunk, (source, there) = number // len(found), found[number % len(found)]
        to = normed.at[source, chunk * chunk_rows : (chunk + 1) * chunk_rows, :]
        return there, lambda: pltpu.make_async_copy(
            pieces[number], to, piece_in.at[chunk, source]
        )

    for number in range(len(pieces)):
        there, copy = copy_of(number)
        when(there, lambda: copy().start())
    copies = [
        [
            pltpu.make_async_copy(
                matrix.at[step * width : (step + 1) * width, :],
                held.at[step, which],
                weight_in.at[step, which],
            )
            for which, matrix in enumerate(matrices)
        ]
        for step in range(count)
    ]
    for step in range(count):
        for copy in copies[step]:
            copy.start()
    for number in range(len(pieces)):
        there, copy = copy_of(number)
        when(there, lambda: copy().wait())

    square = jnp.zeros((rows, 1), jnp.float32)
    for source in range(count):
        values = normed[source].astype(jnp.float32)
        square = square + jnp.sum(values * values, axis=1, keepdims=True)
    row_scale = lax.rsqrt(square / (count * width) + 1e-05)
    for source in range(count):
        values = normed[source].astype(jnp.float32) * row_scale * gain_ref[source : source + 1, :]
        normed[source] = values.astype(jnp.bfloat16)
    part_rows = chunk_rows // group
    totals = [None] * 3
    for step in range(count):
        for which in range(3):
            copies[step][which].wait()
            product = jnp.dot(normed[step], held[step, which], preferred_element_type=jnp.float32)
            totals[which] = product if step == 0 else totals[which] + product
    for which, total in enumerate(totals):
        if which == 0:
            total = jnp.where(active_ref[begin : begin + rows, :] > 0, total, ASIDE)
        total = total.astype(jnp.bfloat16)
        for head in range(total.shape[1] // HEAD):
            for part in range(group):
                for chunk in range(chunks):
                    first = chunk * chunk_rows + part * part_rows
                    out_ref[
                        head * group + part,
                        chunk * part_rows : (chunk + 1) * part_rows,
                        which * HEAD : (which + 1) * HEAD,
                    ] = total[first : first + part_rows, head * HEAD : (head + 1) * HEAD]


def project(me, pieces, active, chunk, gain, wq, wk, wv, seq_count, group):
    rows, columns = pieces[0].shape
    features, width = wq.shape
    count = features // columns
    vmem = pl.BlockSpec(memory_space=pltpu.VMEM)
    return pl.pallas_call(
        partial(project_kernel, group, count, chunk * rows),
        in_specs=[pl.BlockSpec(memory_space=pltpu.SMEM), vmem, vmem]
        + [pl.BlockSpec(memory_space=pl.ANY)] * (3 + len(pieces)),
        out_specs=vmem,
        out_shape=jax.ShapeDtypeStruct((seq_count, rows // group, 3 * HEAD), jnp.bfloat16),
        scratch_shapes=[
            pltpu.VMEM((count, rows, columns), jnp.bfloat16),
            pltpu.VMEM((count, 3, columns, width), jnp.bfloat16),
            pltpu.SemaphoreType.DMA((rows // pieces[0].shape[0], count)),
            pltpu.SemaphoreType.DMA((count, 3)),
        ],
        compiler_params=pltpu.CompilerParams(vmem_limit_bytes=LIMIT),
        cost_estimate=pl.CostEstimate(
            flops=6 * rows * features * width,
            bytes_accessed=6 * features * width + 2 * rows * (features + 3 * width),
            transcendentals=0,
        ),
    )(me, gain, active, wq, wk, wv, *pieces)


def attend_kernel(chunks, group, rows, part_ref, *refs):
    pieces = refs[:-3]
    out_ref, keys, values = refs[-3:]
    seq_count = pieces[0].shape[0]
    chunk_rows = rows // chunks
    part_rows = chunk_rows // group
    part = part_ref[0]

    def place(home, _):
        chunk = 0
        for number in range(0, len(pieces), group):
            inside = pieces[number].shape[1] // part_rows
            for step in range(group):
                owner = lax.rem(part + step, group)
                piece = pieces[number + step]
                for at_chunk in range(inside):
                    at = home * rows + (chunk + at_chunk) * chunk_rows + owner * part_rows
                    to = pl.ds(pl.multiple_of(at, part_rows), part_rows)
                    of = slice(at_chunk * part_rows, (at_chunk + 1) * part_rows)
                    aside = piece[home, of, :HEAD].astype(jnp.float32) >= ASIDE
                    keys[to, :HEAD] = piece[home, of, HEAD : 2 * HEAD]
                    keys[to, HEAD:] = jnp.where(aside, MASKED, 0.0).astype(jnp.bfloat16)
                    values[to, :] = piece[home, of, 2 * HEAD :]
            chunk += inside
        return 0

    lax.fori_loop(0, seq_count, place, 0)
    scale = math.log2(math.e) / math.sqrt(HEAD)
    count = chunks * part_rows
    first_lane = lax.broadcasted_iota(jnp.int32, (count, HEAD), 1) == 0
    mask_lane = jnp.where(first_lane, 1.0, 0.0).astype(jnp.bfloat16)
    order = lax.broadcasted_iota(jnp.int32, (count, rows), 0)
    own = order // part_rows * chunk_rows + part * part_rows + order % part_rows
    later = lax.broadcasted_iota(jnp.int32, (count, rows), 1) > own

    def queries_of(home):
        queries = jnp.concatenate(
            [pieces[number][home, :, :HEAD] for number in range(0, len(pieces), group)], axis=0
        )
        return jnp.concatenate([queries, mask_lane], axis=1)

    def scores_of(queries, at):
        return scale * lax.dot_general(
            queries,
            keys[at, :],
            (((1,), (1,)), ((), ())),
            preferred_element_type=jnp.float32,
        )

    if seq_count <= 8:
        for home in range(seq_count):
            queries = queries_of(home)
            blocks = []
            for other in range(home + 1):
                scores = scores_of(queries, slice(other * rows, (other + 1) * rows))
                if other == home:
                    scores = jnp.where(later, MASKED, scores)
                blocks.append(scores)
            scores = jnp.concatenate(blocks, axis=1)
            best = jnp.max(scores, axis=1, keepdims=True)
            weights = jnp.exp2(scores - best)
            total = jnp.sum(weights, axis=1, keepdims=True)
            summed = jnp.dot(
                weights.astype(jnp.bfloat16),
                values[: (home + 1) * rows, :],
                preferred_element_type=jnp.float32,
            )
            out_ref[home] = (summed / total).astype(jnp.bfloat16)
        return

    def one_home(home, _):
        queries = queries_of(home)

        def fold(other, carry, diagonal):
            best, total, summed = carry
            at = pl.ds(pl.multiple_of(other * rows, rows), rows)
            scores = scores_of(queries, at)
            if diagonal:
                scores = jnp.where(later, MASKED, scores)
            newbest = jnp.maximum(best, jnp.max(scores, axis=1, keepdims=True))
            factor = jnp.exp2(best - newbest)
            weights = jnp.exp2(scores - newbest)
            total = total * factor + jnp.sum(weights, axis=1, keepdims=True)
            summed = summed * factor + jnp.dot(
                weights.astype(jnp.bfloat16), values[at, :], preferred_element_type=jnp.float32
            )
            return newbest, total, summed

        start = (
            jnp.full((count, 1), MASKED, jnp.float32),
            jnp.zeros((count, 1), jnp.float32),
            jnp.zeros((count, HEAD), jnp.float32),
        )
        carry = fold(home, start, True)
        carry = lax.fori_loop(0, home, lambda other, c: fold(other, c, False), carry)
        _, total, summed = carry
        out_ref[home] = (summed / total).astype(jnp.bfloat16)
        return 0

    lax.fori_loop(0, seq_count, one_home, 0)


def attend(part, pieces, chunks, group, rows):
    seq_count = pieces[0].shape[0]
    count = rows // group
    vmem = pl.BlockSpec(memory_space=pltpu.VMEM)
    pairs = seq_count * (seq_count + 1) // 2
    return pl.pallas_call(
        partial(attend_kernel, chunks, group, rows),
        in_specs=[pl.BlockSpec(memory_space=pltpu.SMEM)] + [vmem] * len(pieces),
        out_specs=vmem,
        out_shape=jax.ShapeDtypeStruct((seq_count, count, HEAD), jnp.bfloat16),
        scratch_shapes=[
            pltpu.VMEM((seq_count * rows, 2 * HEAD), jnp.bfloat16),
            pltpu.VMEM((seq_count * rows, HEAD), jnp.bfloat16),
        ],
        compiler_params=pltpu.CompilerParams(vmem_limit_bytes=LIMIT),
        cost_estimate=pl.CostEstimate(
            flops=6 * pairs * count * rows * HEAD,
            bytes_accessed=8 * seq_count * rows * HEAD,
            transcendentals=pairs * count * rows,
        ),
    )(part, *pieces)


def output_kernel(group, count, cuts, blocks, halves, me_ref, at_ref, active_ref, hidden_ref, *refs):
    weights = refs[: cuts * blocks]
    pieces = refs[cuts * blocks : -7]
    out_ref, rows_in, held, own, piece_in, weight_in, own_in = refs[-7:]
    heads = pieces[0].shape[0] // group
    found = sources(me_ref[0], count)
    own_copy = pltpu.make_async_copy(hidden_ref, own, own_in)
    depth = weights[0].shape[0]
    weight_copies = [
        pltpu.make_async_copy(
            weight,
            held.at[number // blocks, number % blocks * depth : (number % blocks + 1) * depth, :],
            weight_in.at[number],
        )
        for number, weight in enumerate(weights)
    ]

    def copies_of(number):
        half, (source, there) = number // len(found), found[number % len(found)]

        def each(act):
            for head in range(heads):
                at = pl.multiple_of(at_ref[(source * halves + half) * heads + head] * HEAD, HEAD)
                for part in range(group):
                    act(
                        pltpu.make_async_copy(
                            pieces[number].at[head * group + part],
                            rows_in.at[:, part, :, pl.ds(at, HEAD)],
                            piece_in.at[half, source, head, part],
                        )
                    )

        return there, each

    for number in range(len(pieces)):
        there, each = copies_of(number)
        when(there, lambda: each(lambda copy: copy.start()))
    for copy in weight_copies[:blocks] + [own_copy] + weight_copies[blocks:]:
        copy.start()
    for number in range(len(pieces)):
        there, each = copies_of(number)
        when(there, lambda: each(lambda copy: copy.wait()))

    rows, width = own.shape[0], held.shape[2]
    x = rows_in[...].reshape(rows, -1)
    for cut in range(cuts):
        for copy in weight_copies[cut * blocks : (cut + 1) * blocks]:
            copy.wait()
        columns = pl.ds(pl.multiple_of(me_ref[1 + cut] * width, width), width)
        shares = jnp.dot(x, held[cut], preferred_element_type=jnp.float32)
        if cut == 0:
            own_copy.wait()
        hidden = own[:, columns]
        renewed = (hidden.astype(jnp.float32) + shares).astype(jnp.bfloat16)
        out_ref[:, columns] = jnp.where(active_ref[...] > 0, renewed, hidden)


def output(scalars, at, pieces, weights, hidden, active, chunks, group, halves):
    rows, columns = hidden.shape
    width = weights[0].shape[1]
    cuts = columns // width
    blocks = len(weights) // cuts
    depth = weights[0].shape[0] * blocks
    count = (len(pieces) // halves + 1) // 2
    part_rows = rows // chunks // group
    pieces = [piece.reshape(-1, chunks, part_rows, HEAD) for piece in pieces]
    smem = pl.BlockSpec(memory_space=pltpu.SMEM)
    vmem = pl.BlockSpec(memory_space=pltpu.VMEM)
    return pl.pallas_call(
        partial(output_kernel, group, count, cuts, blocks, halves),
        in_specs=[smem, smem, vmem]
        + [pl.BlockSpec(memory_space=pl.ANY)] * (1 + len(weights) + len(pieces)),
        out_specs=vmem,
        out_shape=jax.ShapeDtypeStruct((rows, columns), jnp.bfloat16),
        scratch_shapes=[
            pltpu.VMEM((chunks, group, part_rows, depth), jnp.bfloat16),
            pltpu.VMEM((cuts, depth, width), jnp.bfloat16),
            pltpu.VMEM((rows, columns), jnp.bfloat16),
            pltpu.SemaphoreType.DMA((halves, count, pieces[0].shape[0] // group, group)),
            pltpu.SemaphoreType.DMA((cuts * blocks,)),
            pltpu.SemaphoreType.DMA,
        ],
        compiler_params=pltpu.CompilerParams(vmem_limit_bytes=LIMIT),
        cost_estimate=pl.CostEstimate(
            flops=2 * rows * depth * columns,
            bytes_accessed=2 * (rows * depth + depth * columns + 2 * rows * columns),
            transcendentals=0,
        ),
    )(scalars, at, active, hidden, *weights, *pieces)


def share_kernel(place_ref, w_ref, *shares):
    for number, share in enumerate(shares):
        step = number if number < 3 else number - 1
        first = w_ref.shape[0] // 2 if number == 3 else 0

        @pl.when(pl.program_id(0) == step)
        def _():
            share[...] = w_ref[first : first + share.shape[0], :]


def weight_shares(w_out, seq_count, tensor_count, columns):
    depth = w_out.shape[0]
    cuts = seq_count // (depth // HEAD)
    width = columns // cuts
    if width % HEAD:
        return None
    cut = lax.axis_index("seq").astype(jnp.int32) % cuts
    sizes = [depth, depth, depth // 2, depth // 2] + [depth] * (tensor_count - 3)
    place = jnp.stack([lax.axis_index("tensor").astype(jnp.int32), cut])
    return list(
        pl.pallas_call(
            share_kernel,
            grid_spec=pltpu.PrefetchScalarGridSpec(
                num_scalar_prefetch=1,
                grid=(tensor_count,),
                in_specs=[
                    pl.BlockSpec(
                        (depth, width),
                        lambda j, place: (0, lax.rem(place[0] + j, tensor_count) * cuts + place[1]),
                    )
                ],
                out_specs=[pl.BlockSpec((size, width), lambda j, place: (0, 0)) for size in sizes],
            ),
            out_shape=[jax.ShapeDtypeStruct((size, width), w_out.dtype) for size in sizes],
            compiler_params=pltpu.CompilerParams(vmem_limit_bytes=LIMIT),
        )(place, w_out)
    )


def send_share(shares, number):
    if shares is None:
        return None
    step = number if number < 3 else number - 1
    count = len(shares) - 1
    ring = [(d, (d + step) % count) for d in range(count)]
    return lax.ppermute(shares[number], "tensor", ring)


def output_order(w_out, seq_count, tensor_count, whole):
    heads = w_out.shape[0] // HEAD
    cuts = seq_count // heads
    row = jnp.arange(tensor_count * heads, dtype=jnp.int32)
    if whole:
        return [jnp.int32(0)], row
    seq_me = lax.axis_index("seq").astype(jnp.int32)
    me = lax.axis_index("tensor").astype(jnp.int32)
    which = [(seq_me % cuts + step) % cuts for step in range(cuts)]
    return which, (me - row // heads) % tensor_count * heads + row % heads


def shards(hidden, depth, norm_gain, w_query, w_key, w_value, w_out):
    rows, columns = hidden.shape
    seq_count = lax.axis_size("seq")
    tensor_count = lax.axis_size("tensor")
    heads = w_query.shape[1] // HEAD
    group = seq_count // heads
    chunks = 2
    chunk_rows = rows // chunks
    part = (lax.axis_index("seq") % group).astype(jnp.int32).reshape(1)
    me = lax.axis_index("tensor").astype(jnp.int32)
    gain = norm_gain.reshape(tensor_count, columns)
    active = (depth >= 2).astype(jnp.int32).reshape(rows, 1)
    shares = weight_shares(w_out, seq_count, tensor_count, columns)

    def work(found, chunk):
        return project(
            me.reshape(1), found, active, chunk, gain, w_query, w_key, w_value, seq_count, group
        )

    def to_heads(sent):
        return lax.all_to_all(sent, "seq", split_axis=0, concat_axis=0)

    def to_parts(got):
        rings = [
            [(d, d - d % group + (d - step) % group) for d in range(seq_count)]
            for step in range(1, group)
        ]
        return [got] + [lax.ppermute(got, "seq", ring) for ring in rings]

    def cut_weight(step, last):
        nonlocal shares
        if step == 1:
            last[1], shares = lax.optimization_barrier((last[1], shares))
        return last

    first, second = line_gather(
        [hidden[:chunk_rows], hidden[chunk_rows:]], tensor_count, cut_weight
    )
    early, second, shares = lax.optimization_barrier((work(first, 0), second, shares))
    sent, early, far, shares = lax.optimization_barrier(
        (work(second, 1), to_heads(early), send_share(shares, 2), shares)
    )
    late, rest = lax.optimization_barrier((to_heads(sent), send_share(shares, 3)))
    pieces = to_parts(early) + to_parts(late)
    out, near = lax.optimization_barrier(
        (attend(part, pieces, chunks, group, rows), send_share(shares, 1))
    )
    home = lax.all_to_all(out, "seq", split_axis=0, concat_axis=0)
    if shares is None:
        weights = [lax.all_to_all(w_out, "tensor", split_axis=1, concat_axis=0, tiled=True)]
    else:
        _, last = lax.optimization_barrier((near, shares))
        others = [send_share(last, number) for number in range(4, tensor_count + 1)]
        home, others = lax.optimization_barrier((home, others))
        weights = [shares[0], near, jnp.concatenate([far, rest], axis=0), *others]
        for step in range(1, group):
            ring = [(d, d - d % group + (d - step) % group) for d in range(seq_count)]
            weights += [lax.ppermute(weight, "seq", ring) for weight in weights[:tensor_count]]
    found = line_gather(
        [home[: seq_count // 2], home[seq_count // 2 :]], tensor_count, lambda step, last: last
    )
    cut_of, at = output_order(w_out, seq_count, tensor_count, shares is None)
    scalars = jnp.stack([me, *cut_of])
    return output(scalars, at, sum(found, []), weights, hidden, active, chunks, group, 2)


def solution(mesh):
    return jax.shard_map(
        shards,
        mesh=mesh,
        in_specs=(
            P("seq", "tensor"),
            P("seq"),
            P(),
            P(None, "tensor"),
            P(None, "tensor"),
            P(None, "tensor"),
            P("tensor", None),
        ),
        out_specs=P("seq", "tensor"),
        check_vma=False,
    )
```
